32 devices in a mesh: ctx: 8 (over y, x, core), head: 4 (over z).
Axes of the slice: x: 2, y: 2, z: 4, core: 2. Of those that a mesh axis runs over, the one named last changes fastest.
Arguments:
- query_input: bfloat16 [4096, 4096], P('ctx', 'head'), may hold values from -96 to 96
- key_input: bfloat16 [4096, 4096], P('ctx', 'head'), may hold values from -6 to 6
- value_input: bfloat16 [4096, 4096], P('ctx', 'head'), may hold values from -6 to 6
- out_weight: bfloat16 [4096, 4096], P('head'), may hold values from -0.125 to 0.125
- out_cotangent: bfloat16 [4096, 4096], P('ctx', 'head'), may hold values from -6 to 6
Outputs:
- mixed: float32 [4096, 4096], P('ctx', 'head')
- grad_q: float32 [4096, 4096], P('ctx', 'head')
- grad_k: float32 [4096, 4096], P('ctx', 'head')
- grad_v: float32 [4096, 4096], P('ctx', 'head')
- weight_grad: float32 [4096, 4096], P('head', 'ctx')
- level_max: float32 [5, 32], P(None, 'head')
The draws below stay inside these ranges and needn't reach their ends.
All inputs are finite; a program needn't handle non-finite values.
Results may differ from the reference program's by a relative error of at most 0.04.
Values may be sent and summed in bfloat16 or wider, within the bound.
No kernel may reach another device: no remote copies, remote signals or barrier semaphores. Data moves between devices by JAX's collectives and lax.ppermute only.
A program may use at most 128 MiB of HBM per device.

```python
import math
import jax
import jax.numpy as jnp
from jax import lax

D = 4096
H = 32
DH = 128
BLK = 128
LEVELS = 5
TOK_DEV = 512
SEQ = 4096


def rising(length_total, lower_end, upper_end):
    position = jnp.arange(length_total, dtype=jnp.float32) / float(length_total - 1)
    return lower_end + (upper_end - lower_end) * position


def rough_part(key):
    return jnp.clip(jax.random.normal(key, (SEQ, D), jnp.float32), -4.0, 4.0)


def segment_part(key):
    blocks = jnp.clip(jax.random.normal(key, (SEQ // TOK_DEV, D), jnp.float32), -3.0, 3.0)
    return jnp.repeat(blocks, TOK_DEV, axis=0)


def query_key_pair(key):
    streams = jax.random.split(jax.random.fold_in(key, 7), 4)
    growth = rising(SEQ, 1.0, 3.0)
    queries = growth[:, None] * (0.8 * rough_part(streams[0]) + 0.8 * segment_part(streams[1]))
    key_rows = 0.8 * rough_part(streams[2]) + 0.8 * segment_part(streams[3])
    return (queries, key_rows)


def draw_query_input(key, part):
    return query_key_pair(key)[0].astype(jnp.bfloat16)


def draw_key_input(key, part):
    return query_key_pair(key)[1].astype(jnp.bfloat16)


def draw_value_input(key, part):
    streams = jax.random.split(jax.random.fold_in(key, 19), 2)
    values = 0.7 * rough_part(streams[0]) + segment_part(streams[1])
    return values.astype(jnp.bfloat16)


def raised(result, rng, source, target, parts, factor):
    def block_of(dim):
        return (jnp.arange(result.shape[dim]) // (result.shape[dim] // parts)).reshape((-1,) + (1,) * (result.ndim - 1 - dim))

    one_side = jax.random.permutation(rng, parts)[block_of(target)]
    far = (block_of(target) + parts // 2) % parts
    return jnp.where((block_of(source) == one_side) | (block_of(source) == far), factor * result, result)


def shard_levels(own_key, shape, pieces, least, largest):
    level = 1.0
    for dim, shards_of in pieces:
        draws = jax.random.uniform(jax.random.fold_in(jax.random.fold_in(own_key, 6), dim), (shards_of,), jnp.float32, least / len(pieces), largest / len(pieces))
        level = level * jnp.repeat(jnp.exp(draws), shape[dim] // shards_of).reshape((-1,) + (1,) * (len(shape) - 1 - dim))
    return level


def noise_with(stream_key, dims, spread, limit, shards, heavy, kind=jnp.bfloat16):
    array = spread * jax.random.normal(stream_key, dims, jnp.float32)
    if shards:
        array = array * shard_levels(stream_key, dims, shards, -0.22, 0.18)
    return jnp.clip(raised(array, jax.random.fold_in(stream_key, 3), *heavy), -limit, limit).astype(kind)


def setup_inputs(seed: int = 0) -> dict:
    streams_of = jax.random.split(jax.random.key(seed), 6)
    return {
        "query_input": draw_query_input(jax.random.fold_in(streams_of[5], 71), 0),
        "key_input": draw_key_input(jax.random.fold_in(streams_of[5], 71), 0),
        "value_input": draw_value_input(jax.random.fold_in(streams_of[5], 71), 0),
        "out_weight": noise_with(streams_of[3], (D, D), D ** -0.5, 0.125, ((0, 4),), (0, 1, 4, 2.0)),
        "out_cotangent": noise_with(streams_of[4], (SEQ, D), 1.0, 6.0, ((0, 8), (1, 4)), (0, 1, 8, 2.0)),
    }


LOG_TWO = math.log(2.0)


def rounded(tensor):
    return lax.optimization_barrier(tensor.astype(jnp.bfloat16)).astype(jnp.float32)


def coarse(tensor, factor):
    if factor == 1:
        return tensor
    row_count = tensor.shape[0] // factor
    blocked = tensor.reshape(row_count, factor, tensor.shape[1], tensor.shape[2]).astype(jnp.float32)
    return (jnp.sum(blocked, axis=1) * (1.0 / factor)).astype(jnp.bfloat16)


def own_blocks(tensor):
    return tensor.reshape(tensor.shape[0] // BLK, BLK, tensor.shape[1], tensor.shape[2])


def partner_blocks(tensor):
    block_count = tensor.shape[0] // BLK
    paired = tensor.reshape(block_count // 2, 2, BLK, tensor.shape[1], tensor.shape[2])
    return jnp.flip(paired, 1).reshape(block_count, BLK, tensor.shape[1], tensor.shape[2])


def unpair(grouped):
    block_count = grouped.shape[0]
    paired = grouped.reshape(block_count // 2, 2, BLK, grouped.shape[2], grouped.shape[3])
    return jnp.flip(paired, 1).reshape(block_count * BLK, grouped.shape[2], grouped.shape[3])


def level_groups(coarse_q, coarse_k, coarse_v, level_index):
    queries = own_blocks(coarse_q)
    key_rows = partner_blocks(coarse_k)
    value_rows = partner_blocks(coarse_v)
    if level_index == 0:
        key_rows = jnp.concatenate([own_blocks(coarse_k), key_rows], 1)
        value_rows = jnp.concatenate([own_blocks(coarse_v), value_rows], 1)
    return queries, key_rows, value_rows


def score_block(queries, key_rows, log_shift):
    scores = jnp.einsum("gqhd,gkhd->gqhk", queries.astype(jnp.float32), key_rows.astype(jnp.float32))
    return scores * (DH ** -0.5) + log_shift


def level_forward(queries, key_rows, value_rows, log_shift):
    scores = score_block(queries, key_rows, log_shift)
    row_peak = jnp.max(scores, axis=-1)
    exponent = jnp.exp(scores - row_peak[..., None])
    row_total = jnp.sum(exponent, axis=-1)
    weighted = jnp.einsum("gqhk,gkhd->gqhd", rounded(exponent), value_rows.astype(jnp.float32))
    return row_peak, row_total, weighted


def level_backward(queries, key_rows, value_rows, log_shift, row_peak, row_grad, row_scalar):
    score_scale = DH ** -0.5
    exponent = jnp.exp(score_block(queries, key_rows, log_shift) - row_peak[..., None])
    grad_float = row_grad.astype(jnp.float32)
    grad_weights = jnp.einsum("gqhd,gkhd->gqhk", grad_float, value_rows.astype(jnp.float32))
    grad_scores = rounded(exponent * (grad_weights - row_scalar[..., None]))
    query_part = jnp.einsum("gqhk,gkhd->gqhd", grad_scores, key_rows.astype(jnp.float32)) * score_scale
    key_part = jnp.einsum("gqhk,gqhd->gkhd", grad_scores, queries.astype(jnp.float32)) * score_scale
    value_part = jnp.einsum("gqhk,gqhd->gkhd", rounded(exponent), grad_float)
    return query_part, key_part, value_part


def forward_slab(query_slab, key_slab, value_slab):
    records = []
    for level_index in range(LEVELS):
        factor = 2 ** level_index
        groups = level_groups(coarse(query_slab, factor), coarse(key_slab, factor), coarse(value_slab, factor), level_index)
        row_peak, row_total, weighted = level_forward(groups[0], groups[1], groups[2], level_index * LOG_TWO)
        records.append((row_peak, row_total, weighted, groups))
    return records


def combine(records, token_count):
    expanded = []
    for level_index, record in enumerate(records):
        factor = 2 ** level_index
        expanded.append(jnp.repeat(record[0].reshape(token_count // factor, -1), factor, axis=0))
    highest = expanded[0]
    for expanded_peak in expanded[1:]:
        highest = jnp.maximum(highest, expanded_peak)
    scales = [jnp.exp(expanded_peak - highest) for expanded_peak in expanded]
    denominator = jnp.zeros_like(highest)
    numerator = jnp.zeros((token_count, records[0][2].shape[2], records[0][2].shape[3]), highest.dtype)
    for level_index, record in enumerate(records):
        factor = 2 ** level_index
        row_count = token_count // factor
        row_total = jnp.repeat(record[1].reshape(row_count, -1), factor, axis=0)
        weighted = jnp.repeat(record[2].reshape(row_count, record[2].shape[2], record[2].shape[3]), factor, axis=0)
        denominator = denominator + scales[level_index] * row_total
        numerator = numerator + scales[level_index][..., None] * weighted
    return numerator / denominator[..., None], scales, denominator


def backward_slab(query_slab, key_slab, value_slab, grad_slab):
    records = forward_slab(query_slab, key_slab, value_slab)
    token_count = query_slab.shape[0]
    heads_count = query_slab.shape[1]
    attn_f, scales, denominator = combine(records, token_count)
    grad_f = grad_slab.astype(jnp.float32)
    row_delta = jnp.sum(grad_f * attn_f, axis=-1)
    grad_q = jnp.zeros_like(attn_f)
    grad_k = jnp.zeros_like(attn_f)
    grad_v = jnp.zeros_like(attn_f)
    for level_index, record in enumerate(records):
        factor = 2 ** level_index
        row_count = token_count // factor
        level_share = scales[level_index] / denominator
        row_grad = jnp.sum((level_share[..., None] * grad_f).reshape(row_count, factor, heads_count, DH), axis=1).astype(jnp.bfloat16)
        row_scalar = jnp.sum((level_share * row_delta).reshape(row_count, factor, heads_count), axis=1)
        queries, key_rows, value_rows = record[3]
        block_count = queries.shape[0]
        query_part, key_part, value_part = level_backward(queries, key_rows, value_rows, level_index * LOG_TWO, record[0], row_grad.reshape(block_count, -1, heads_count, DH), row_scalar.reshape(block_count, -1, heads_count))
        query_coarse = query_part.reshape(row_count, heads_count, DH)
        if level_index == 0:
            key_coarse = key_part[:, :BLK].reshape(row_count, heads_count, DH) + unpair(key_part[:, BLK:])
            value_coarse = value_part[:, :BLK].reshape(row_count, heads_count, DH) + unpair(value_part[:, BLK:])
        else:
            key_coarse = unpair(key_part)
            value_coarse = unpair(value_part)
        inverse = 1.0 / factor
        grad_q = grad_q + jnp.repeat(query_coarse, factor, axis=0) * inverse
        grad_k = grad_k + jnp.repeat(key_coarse, factor, axis=0) * inverse
        grad_v = grad_v + jnp.repeat(value_coarse, factor, axis=0) * inverse
    return grad_q, grad_k, grad_v


def by_head(tensor):
    return jnp.transpose(tensor.reshape(SEQ, H, DH), (1, 0, 2))[:, :, None, :]


def from_head(tensor):
    return jnp.transpose(tensor[:, :, 0, :], (1, 0, 2)).reshape(SEQ, D)


def forward_head(slabs):
    records = forward_slab(slabs[0], slabs[1], slabs[2])
    attn_f = combine(records, SEQ)[0]
    peaks = jnp.stack([jnp.max(record[0]) - level_index * LOG_TWO for level_index, record in enumerate(records)])
    return attn_f, peaks


def backward_head(slabs):
    return backward_slab(slabs[0], slabs[1], slabs[2], slabs[3])


def reference(query_input, key_input, value_input, out_weight, out_cotangent):
    query_heads = by_head(query_input)
    key_heads = by_head(key_input)
    value_heads = by_head(value_input)
    attn_heads, peaks = lax.map(forward_head, (query_heads, key_heads, value_heads))
    attn = from_head(attn_heads).astype(jnp.bfloat16)
    mixed = jnp.dot(attn, out_weight, preferred_element_type=jnp.float32)
    grad_attn = jnp.dot(out_cotangent, out_weight.T, preferred_element_type=jnp.float32).astype(jnp.bfloat16)
    weight_grad = jnp.dot(attn.T, out_cotangent, preferred_element_type=jnp.float32)
    grads = lax.map(backward_head, (query_heads, key_heads, value_heads, by_head(grad_attn)))
    grad_q = from_head(grads[0])
    grad_k = from_head(grads[1])
    grad_v = from_head(grads[2])
    level_max = jnp.transpose(peaks)
    return mixed, grad_q, grad_k, grad_v, weight_grad, level_max
```

```python
import functools
import math

import jax
import jax.numpy as jnp
from jax import lax
from jax.experimental import pallas as pl
from jax.experimental.pallas import tpu as pltpu
from jax.sharding import PartitionSpec as P

DH = 128
BLK = 128
LEVELS = 5
SCALE = DH ** (-0.5)
LOG_TWO = math.log(2.0)
F32 = jnp.float32
BF16 = jnp.bfloat16
VMEM_LIMIT = 48 * 1024 * 1024


def dot_nn(a, b):
    return lax.dot_general(a, b, (((1,), (0,)), ((), ())), preferred_element_type=F32)


def dot_nt(a, b):
    return lax.dot_general(a, b, (((1,), (1,)), ((), ())), preferred_element_type=F32)


def dot_tn(a, b):
    return lax.dot_general(a, b, (((0,), (0,)), ((), ())), preferred_element_type=F32)


def pool_matrix(level, rows, tokens):
    row = lax.broadcasted_iota(jnp.int32, (rows, tokens), 0)
    token = lax.broadcasted_iota(jnp.int32, (rows, tokens), 1)
    return jnp.where(lax.shift_right_logical(token, level) == row, 0.5**level, 0.0).astype(BF16)


def pooled(level, tensor):
    tokens = tensor.shape[0]
    return dot_nn(pool_matrix(level, tokens >> level, tokens), tensor).astype(BF16)


def expand_two(scratch, base, value):
    rows = value.shape[0]
    scratch[pl.ds(base, rows, stride=2), :] = value
    scratch[pl.ds(base + 1, rows, stride=2), :] = value
    return scratch[pl.ds(base, 2 * rows), :]


def pool_kernel(k_ref, v_ref, two_ref, three_ref, four_ref):
    k = k_ref[...]
    v = v_ref[...]
    for level, out in ((2, two_ref), (3, three_ref), (4, four_ref)):
        rows = k.shape[0] >> level
        out[pl.ds(0, rows), :] = pooled(level, k)
        out[pl.ds(rows, rows), :] = pooled(level, v)


def pool_call(key, value):
    tokens, width = key.shape
    step = 256
    spec = pl.BlockSpec((tokens, step), lambda i: (0, i))
    rows = [2 * (tokens >> level) for level in (2, 3, 4)]
    return pl.pallas_call(
        pool_kernel,
        grid=(width // step,),
        in_specs=[spec, spec],
        out_specs=[pl.BlockSpec((r, step), lambda i: (0, i)) for r in rows],
        out_shape=[jax.ShapeDtypeStruct((r, width), BF16) for r in rows],
        compiler_params=pltpu.CompilerParams(vmem_limit_bytes=VMEM_LIMIT),
        cost_estimate=pl.CostEstimate(
            flops=4 * 224 * tokens * width, bytes_accessed=6 * tokens * width, transcendentals=0
        ),
        name="pool_keys",
    )(key, value)


def gather_rows(refs):
    keys = []
    values = []
    for ref in refs:
        half = ref.shape[0] // 2
        keys.append(ref[pl.ds(0, half), :])
        values.append(ref[pl.ds(half, half), :])
    if len(refs) == 1:
        return keys[0], values[0]
    return jnp.concatenate(keys, 0), jnp.concatenate(values, 0)


def level_block(q, k, v, shift):
    scores = dot_nt(q, k) * SCALE + shift
    peak = jnp.max(scores, axis=-1, keepdims=True)
    weights = jnp.exp(scores - peak)
    total = jnp.sum(weights, axis=-1, keepdims=True)
    mean = dot_nn(weights.astype(BF16), v) / total
    return peak, peak + jnp.log(total), mean


def forward_kernel(
    q_ref, k_ref, v_ref, t2, t3a, t3b, t4a, t4b, t4c, t4d, attn_ref, lse_ref, top_ref, lse_s, out_s
):
    head = pl.program_id(0)
    q = q_ref[...]
    k = k_ref[...]
    v = v_ref[...]
    tokens = q.shape[0]
    tops = []
    state = None
    base = 0
    for level in range(LEVELS - 1, -1, -1):
        shift = level * LOG_TWO
        if level >= 2:
            refs = {2: (t2,), 3: (t3a, t3b), 4: (t4a, t4b, t4c, t4d)}[level]
            keys, values = gather_rows(refs)
            peak, lse, mean = level_block(pooled(level, q), keys, values, shift)
        else:
            parts = []
            if level == 1:
                qc, kc, vc = pooled(1, q), pooled(1, k), pooled(1, v)
                for b in range(2):
                    mine = slice(b * BLK, (b + 1) * BLK)
                    other = slice((1 - b) * BLK, (2 - b) * BLK)
                    parts.append(level_block(qc[mine], kc[other], vc[other], shift))
            else:
                for b in range(tokens // (2 * BLK)):
                    both = slice(b * 2 * BLK, (b + 1) * 2 * BLK)
                    parts.append(level_block(q[both], k[both], v[both], 0.0))
            peak, lse, mean = [jnp.concatenate(p, 0) for p in zip(*parts)]
        tops.append((level, jnp.max(peak) - shift))
        lse = jnp.broadcast_to(lse, mean.shape)
        if state is None:
            state = (lse, mean)
            continue
        rows = mean.shape[0]
        other_lse = expand_two(lse_s, base, state[0])
        other_mean = expand_two(out_s, base, state[1])
        base += rows
        top = jnp.maximum(lse, other_lse)
        mine = jnp.exp(lse - top)
        other = jnp.exp(other_lse - top)
        total = mine + other
        state = (top + jnp.log(total), (mine * mean + other * other_mean) / total)
    attn_ref[...] = state[1].astype(BF16)
    lane = lax.broadcasted_iota(jnp.int32, state[0].shape, 1)
    lse_ref[...] = jnp.where(lane == head, state[0], lse_ref[...])
    row = lax.broadcasted_iota(jnp.int32, (8, 128), 0)
    tile = jnp.zeros((8, 128), F32)
    for level, value in tops:
        tile = jnp.where(row == level, value, tile)
    top_ref[0] = tile


def forward_call(query, key, value, received):
    tokens, width = query.shape
    heads = width // DH
    spec = pl.BlockSpec((tokens, DH), lambda h: (0, h))
    extra = [pl.BlockSpec((r.shape[0], DH), lambda h: (0, h)) for r in received]
    grown = tokens + tokens // 2 + tokens // 4 + tokens // 8
    return pl.pallas_call(
        forward_kernel,
        grid=(heads,),
        in_specs=[spec, spec, spec] + extra,
        out_specs=[
            spec,
            pl.BlockSpec((tokens, 128), lambda h: (0, 0)),
            pl.BlockSpec((1, 8, 128), lambda h: (h, 0, 0)),
        ],
        out_shape=[
            jax.ShapeDtypeStruct((tokens, width), BF16),
            jax.ShapeDtypeStruct((tokens, 128), F32),
            jax.ShapeDtypeStruct((heads, 8, 128), F32),
        ],
        scratch_shapes=[pltpu.VMEM((grown, 128), F32), pltpu.VMEM((grown, 128), F32)],
        compiler_params=pltpu.CompilerParams(vmem_limit_bytes=VMEM_LIMIT),
        cost_estimate=pl.CostEstimate(
            flops=8 * 376 * tokens * width, bytes_accessed=10 * tokens * width, transcendentals=0
        ),
        name="attention_forward",
    )(query, key, value, *received)


def backward_block(q, k, v, shift, lse, grad, scalar):
    weights = jnp.exp(dot_nt(q, k) * SCALE + (shift - lse))
    grad_scores = (weights * (dot_nt(grad, v) - scalar)).astype(BF16)
    grad_q = dot_nn(grad_scores, k) * SCALE
    grad_k = dot_tn(grad_scores, q) * SCALE
    grad_v = dot_tn(weights.astype(BF16), grad)
    return grad_q, grad_k, grad_v


def backward_kernel(
    q_ref, k_ref, v_ref, attn_ref, grad_ref, lse_ref, t2, t3a, t3b, t4a, t4b, t4c, t4d,
    gq_ref, gk_ref, gv_ref, r2, r3a, r3b, r4a, r4b, r4c, r4d,
    lse_s, grad_s, scal_s, gq_s, gk_s, gv_s,
):
    head = pl.program_id(0)
    q = q_ref[...]
    k = k_ref[...]
    v = v_ref[...]
    grad = grad_ref[...]
    tokens = q.shape[0]
    grad_f = grad.astype(F32)
    lane = lax.broadcasted_iota(jnp.int32, (tokens, 128), 1)
    lse = jnp.sum(jnp.where(lane == head, lse_ref[...], 0.0), axis=-1, keepdims=True)
    scalar = jnp.sum(grad_f * attn_ref[...].astype(F32), axis=-1, keepdims=True)
    lse_s[pl.ds(0, tokens), :] = jnp.broadcast_to(lse, (tokens, 128))
    scal_s[pl.ds(0, tokens), :] = jnp.broadcast_to(scalar, (tokens, 128))
    grad_s[pl.ds(0, tokens), :] = grad_f
    base = 0
    rows = tokens
    places = {}
    for level in range(1, LEVELS):
        half = rows // 2
        even = pl.ds(base, half, stride=2)
        odd = pl.ds(base + 1, half, stride=2)
        lse_even, lse_odd = lse_s[even, :], lse_s[odd, :]
        least = jnp.minimum(lse_even, lse_odd)
        factor_even = jnp.exp(least - lse_even)
        factor_odd = jnp.exp(least - lse_odd)
        nxt = pl.ds(base + rows, half)
        lse_s[nxt, :] = least
        grad_s[nxt, :] = factor_even * grad_s[even, :] + factor_odd * grad_s[odd, :]
        scal_s[nxt, :] = factor_even * scal_s[even, :] + factor_odd * scal_s[odd, :]
        places[level] = nxt
        base += rows
        rows = half
    grad_q = None
    up = 0
    for level in range(LEVELS - 1, -1, -1):
        shift = level * LOG_TWO
        if level >= 2:
            refs = {2: (t2,), 3: (t3a, t3b), 4: (t4a, t4b, t4c, t4d)}[level]
            outs = {2: (r2,), 3: (r3a, r3b), 4: (r4a, r4b, r4c, r4d)}[level]
            keys, values = gather_rows(refs)
            place = places[level]
            part_q, part_k, part_v = backward_block(
                pooled(level, q), keys, values, shift,
                lse_s[place, :], grad_s[place, :].astype(BF16), scal_s[place, :],
            )
            piece = BLK // len(outs)
            for i, out in enumerate(outs):
                out[pl.ds(0, piece), :] = part_k[i * piece : (i + 1) * piece].astype(BF16)
                out[pl.ds(piece, piece), :] = part_v[i * piece : (i + 1) * piece].astype(BF16)
        elif level == 1:
            place = places[level]
            qc, kc, vc = pooled(1, q), pooled(1, k), pooled(1, v)
            low, gr, sc = lse_s[place, :], grad_s[place, :].astype(BF16), scal_s[place, :]
            parts = []
            for b in range(2):
                mine = slice(b * BLK, (b + 1) * BLK)
                other = slice((1 - b) * BLK, (2 - b) * BLK)
                parts.append(
                    backward_block(qc[mine], kc[other], vc[other], shift, low[mine], gr[mine], sc[mine])
                )
            part_q = jnp.concatenate([parts[0][0], parts[1][0]], 0)
            part_k = jnp.concatenate([parts[1][1], parts[0][1]], 0)
            part_v = jnp.concatenate([parts[1][2], parts[0][2]], 0)
            coarse_k = expand_two(gk_s, 0, part_k * 0.5)
            coarse_v = expand_two(gv_s, 0, part_v * 0.5)
        if level == 0:
            for b in range(tokens // (2 * BLK)):
                both = slice(b * 2 * BLK, (b + 1) * 2 * BLK)
                part_q, part_k, part_v = backward_block(
                    q[both], k[both], v[both], 0.0, lse[both], grad[both], scalar[both]
                )
                here = pl.ds(b * 2 * BLK, 2 * BLK)
                gq_ref[here, :] = part_q + grad_q[both]
                gk_ref[here, :] = part_k + coarse_k[both]
                gv_ref[here, :] = part_v + coarse_v[both]
        else:
            grad_q = part_q if grad_q is None else part_q + grad_q
            rows = grad_q.shape[0]
            grad_q = expand_two(gq_s, up, grad_q * 0.5)
            up += 2 * rows


def backward_call(query, key, value, attn, grad, lse, received):
    tokens, width = query.shape
    heads = width // DH
    spec = pl.BlockSpec((tokens, DH), lambda h: (0, h))
    extra = [pl.BlockSpec((r.shape[0], DH), lambda h: (0, h)) for r in received]
    full = jax.ShapeDtypeStruct((tokens, width), F32)
    scratch = pltpu.VMEM((2 * tokens, 128), F32)
    return pl.pallas_call(
        backward_kernel,
        grid=(heads,),
        in_specs=[spec] * 5 + [pl.BlockSpec((tokens, 128), lambda h: (0, 0))] + extra,
        out_specs=[spec] * 3 + extra,
        out_shape=[full] * 3 + [jax.ShapeDtypeStruct(r.shape, BF16) for r in received],
        scratch_shapes=[scratch] * 6,
        compiler_params=pltpu.CompilerParams(vmem_limit_bytes=VMEM_LIMIT),
        cost_estimate=pl.CostEstimate(
            flops=20 * 376 * tokens * width, bytes_accessed=24 * tokens * width, transcendentals=0
        ),
        name="attention_backward",
    )(query, key, value, attn, grad, lse, *received)


def finish_kernel(gk_ref, gv_ref, t2, t3a, t3b, t4a, t4b, t4c, t4d, ok_ref, ov_ref, k_s, v_s):
    for part, local, out, scr in ((0, gk_ref, ok_ref, k_s), (1, gv_ref, ov_ref, v_s)):
        state = None
        base = 0
        for refs in ((t4a, t4b, t4c, t4d), (t3a, t3b), (t2,)):
            rows = refs[0].shape[0] // 2
            here = pl.ds(part * rows, rows)
            total = refs[0][here, :].astype(F32)
            for ref in refs[1:]:
                total = total + ref[here, :].astype(F32)
            state = total if state is None else total + state
            state = expand_two(scr, base, state * 0.5)
            base += 2 * rows
        state = expand_two(scr, base, state * 0.5)
        out[...] = local[...] + state


def finish_call(grad_k, grad_v, returned):
    tokens, width = grad_k.shape
    step = 128
    spec = pl.BlockSpec((tokens, step), lambda h: (0, h))
    extra = [pl.BlockSpec((r.shape[0], step), lambda h: (0, h)) for r in returned]
    full = jax.ShapeDtypeStruct((tokens, width), F32)
    scratch = pltpu.VMEM((2 * tokens, step), F32)
    return pl.pallas_call(
        finish_kernel,
        grid=(width // step,),
        in_specs=[spec, spec] + extra,
        out_specs=[spec, spec],
        out_shape=[full, full],
        scratch_shapes=[scratch, scratch],
        compiler_params=pltpu.CompilerParams(vmem_limit_bytes=VMEM_LIMIT),
        cost_estimate=pl.CostEstimate(
            flops=8 * tokens * width, bytes_accessed=18 * tokens * width, transcendentals=0
        ),
        name="add_returned",
    )(grad_k, grad_v, *returned)


def swap(value, axis, mask):
    return lax.ppermute(value, axis, [(i, i ^ mask) for i in range(lax.axis_size(axis))])


def shift(value, axis, pairs):
    return lax.ppermute(value, axis, pairs)


def per_device(query, key, value, out_weight, cotangent):
    tokens, width = query.shape
    model = out_weight.shape[1]
    count = lax.axis_size("head")
    ctx_count = lax.axis_size("ctx")
    column = model // ctx_count
    me = lax.axis_index("ctx")
    z = lax.axis_index("head")

    right, left = cotangent, cotangent
    from_left, from_right = [], []
    for step in range(1, count):
        right = shift(right, "head", [(i, i + 1) for i in range(step - 1, count - 1)])
        left = shift(left, "head", [(i, i - 1) for i in range(1, count - step + 1)])
        from_left.append(right)
        from_right.append(left)

    sent = pool_call(key, value)
    masks = (1, 2, 3, 4, 5, 6, 7)
    which = (0, 1, 1, 2, 2, 2, 2)
    received = [swap(sent[w], "ctx", m) for m, w in zip(masks, which)]
    attn, lse, tops = forward_call(query, key, value, received)

    level_max = jnp.transpose(tops[:, :LEVELS, 0])
    mask = 1
    while mask < ctx_count:
        level_max = jnp.maximum(level_max, swap(level_max, "ctx", mask))
        mask *= 2

    product = dot_nn(attn, out_weight).astype(BF16)

    def chunk(index):
        return lax.dynamic_slice(product, (0, lax.rem(index + count, count) * width), (tokens, width))

    to_left, to_right = None, None
    for step in range(1, count):
        piece = chunk(z + step)
        to_left = piece if to_left is None else (to_left.astype(F32) + piece).astype(BF16)
        to_left = shift(to_left, "head", [(i, i - 1) for i in range(count - step, count)])
        piece = chunk(z - step)
        to_right = piece if to_right is None else (to_right.astype(F32) + piece).astype(BF16)
        to_right = shift(to_right, "head", [(i, i + 1) for i in range(0, step)])
    mixed = chunk(z).astype(F32) + to_left.astype(F32) + to_right.astype(F32)

    whole = jnp.zeros((tokens, model), BF16)
    whole = lax.dynamic_update_slice(whole, cotangent, (0, z * width))
    for step in range(1, count):
        got = jnp.where(step <= z, from_left[step - 1], from_right[count - step - 1])
        whole = lax.dynamic_update_slice(whole, got, (0, lax.rem(z - step + count, count) * width))

    attn_other = swap(attn, "ctx", 1)
    terms = []
    chips = ctx_count // 2
    for i in range(chips):
        mine = lax.dynamic_slice(whole, (0, (me ^ (2 * i)) * column), (tokens, column))
        theirs = lax.dynamic_slice(whole, (0, (me ^ (2 * i) ^ 1) * column), (tokens, column))
        theirs = swap(theirs, "ctx", 1)
        term = dot_tn(attn, mine) + dot_tn(attn_other, theirs)
        terms.append(term if i == 0 else swap(term.astype(BF16), "ctx", 2 * i))
    weight_grad = terms[0]
    for term in terms[1:]:
        weight_grad = weight_grad + term.astype(F32)

    grad_attn = dot_nt(whole, out_weight).astype(BF16)
    outs = backward_call(query, key, value, attn, grad_attn, lse, received)
    grad_q, grad_k, grad_v = outs[:3]
    returned = [swap(part, "ctx", m) for m, part in zip(masks, outs[3:])]
    grad_k, grad_v = finish_call(grad_k, grad_v, returned)
    return mixed, grad_q, grad_k, grad_v, weight_grad, level_max


def solution(mesh):
    tokens = P("ctx", "head")
    return jax.shard_map(
        per_device,
        mesh=mesh,
        in_specs=(tokens, tokens, tokens, P("head", None), tokens),
        out_specs=(tokens, tokens, tokens, tokens, P("head", "ctx"), P(None, "head")),
        check_vma=False,
    )
```

```python
import functools
import math

import jax
import jax.numpy as jnp
from jax import lax
from jax.experimental import pallas as pl
from jax.experimental.pallas import tpu as pltpu
from jax.sharding import PartitionSpec as P

DH = 128
BLK = 128
LEVELS = 5
SCALE = DH ** (-0.5)
LOG_TWO = math.log(2.0)
F32 = jnp.float32
BF16 = jnp.bfloat16
VMEM_LIMIT = 60 * 1024 * 1024


def dot_nn(a, b):
    return lax.dot_general(a, b, (((1,), (0,)), ((), ())), preferred_element_type=F32)


def dot_nt(a, b):
    return lax.dot_general(a, b, (((1,), (1,)), ((), ())), preferred_element_type=F32)


def dot_tn(a, b):
    return lax.dot_general(a, b, (((0,), (0,)), ((), ())), preferred_element_type=F32)


def pool_matrix(level, rows, tokens):
    row = lax.broadcasted_iota(jnp.int32, (rows, tokens), 0)
    token = lax.broadcasted_iota(jnp.int32, (rows, tokens), 1)
    return jnp.where(lax.shift_right_logical(token, level) == row, 0.5**level, 0.0).astype(BF16)


def pooled(level, tensor):
    tokens = tensor.shape[0]
    return dot_nn(pool_matrix(level, tokens >> level, tokens), tensor).astype(BF16)


def pool_kernel(k_ref, v_ref, two_ref, three_ref, four_ref):
    k = k_ref[...]
    v = v_ref[...]
    for level, out in ((2, two_ref), (3, three_ref), (4, four_ref)):
        rows = k.shape[0] >> level
        out[pl.ds(0, rows), :] = pooled(level, k)
        out[pl.ds(rows, rows), :] = pooled(level, v)


def pool_call(key, value):
    tokens, width = key.shape
    step = 256
    spec = pl.BlockSpec((tokens, step), lambda i: (0, i))
    rows = [2 * (tokens >> level) for level in (2, 3, 4)]
    return pl.pallas_call(
        pool_kernel,
        grid=(width // step,),
        in_specs=[spec, spec],
        out_specs=[pl.BlockSpec((r, step), lambda i: (0, i)) for r in rows],
        out_shape=[jax.ShapeDtypeStruct((r, width), BF16) for r in rows],
        compiler_params=pltpu.CompilerParams(vmem_limit_bytes=VMEM_LIMIT),
        name="pool_keys",
    )(key, value)


def fill_pool(pool, tokens):
    base = 0
    for level in range(1, LEVELS):
        rows = tokens >> level
        pool[pl.ds(base, rows), :] = pool_matrix(level, rows, tokens)
        base += rows


def expand_two(scratch, base, value):
    rows = value.shape[0]
    scratch[pl.ds(base, rows, stride=2), :] = value
    scratch[pl.ds(base + 1, rows, stride=2), :] = value
    return scratch[pl.ds(base, 2 * rows), :]


def partner_rows(near, three, four_a, four_b, columns):
    def cut(ref, base, half):
        return ref[pl.ds(base, half), columns], ref[pl.ds(base + half, half), columns]

    two = BLK
    join = lambda *pairs: tuple(jnp.concatenate(p, 0) for p in zip(*pairs))
    return {
        2: cut(near, 0, two),
        3: join(cut(three, 0, two // 2), cut(near, 2 * two, two // 2)),
        4: join(
            cut(four_a, 0, two // 4),
            cut(four_b, 0, two // 4),
            cut(near, 3 * two, two // 4),
            cut(near, 3 * two + two // 2, two // 4),
        ),
    }


def coarse_slices(tokens):
    base = 0
    found = {}
    for level in range(1, LEVELS):
        rows = tokens >> level
        found[level] = slice(base, base + rows)
        base += rows
    return found


def forward_kernel(
    q_ref, k_ref, v_ref, near, three, four_a, four_b, *rest, extra
):
    attn_ref, lse_ref, top_ref, pool, peak_s, total_s, summed_s = rest[extra:]
    tokens, width = q_ref.shape

    @pl.when(pl.program_id(0) == 0)
    def _():
        fill_pool(pool, tokens)

    q_all = dot_nn(pool[...], q_ref[...]).astype(BF16)
    half = pl.ds(0, tokens // 2)
    k_one = dot_nn(pool[half, :], k_ref[...]).astype(BF16)
    v_one = dot_nn(pool[half, :], v_ref[...]).astype(BF16)
    where = coarse_slices(tokens)
    heads = range(width // DH)
    columns = [pl.ds(h * DH, DH) for h in heads]
    lanes = [slice(h * DH, (h + 1) * DH) for h in heads]
    work = []
    for h in heads:
        partner = partner_rows(near, three, four_a, four_b, columns[h])
        for level in range(LEVELS - 1, -1, -1):
            if level >= 2:
                work.append((h, level, q_all[where[level], lanes[h]], *partner[level]))
            elif level == 1:
                qc, kc, vc = q_all[where[1], lanes[h]], k_one[:, lanes[h]], v_one[:, lanes[h]]
                for b in range(2):
                    mine = slice(b * BLK, (b + 1) * BLK)
                    other = slice((1 - b) * BLK, (2 - b) * BLK)
                    work.append((h, 1, qc[mine], kc[other], vc[other]))
            else:
                for b in range(tokens // (2 * BLK)):
                    both = pl.ds(b * 2 * BLK, 2 * BLK)
                    work.append(
                        (h, 0, q_ref[both, columns[h]], k_ref[both, columns[h]], v_ref[both, columns[h]])
                    )
    scores = [dot_nt(q, k) * SCALE for _, _, q, k, _ in work]
    peaks = [jnp.max(s, axis=-1, keepdims=True) for s in scores]
    weights = [jnp.exp(s - p).astype(BF16) for s, p in zip(scores, peaks)]
    sums = [
        dot_nn(w, jnp.concatenate([item[4], jnp.ones_like(item[4])], 1))
        for w, item in zip(weights, work)
    ]

    def joined(h, level, values):
        return jnp.concatenate([x for x, item in zip(values, work) if item[:2] == (h, level)], 0)

    row = lax.broadcasted_iota(jnp.int32, (8, 128), 0)
    tiles = [jnp.zeros((8, 128), F32) for _ in heads]
    state = {}
    base = 0
    for level in range(LEVELS - 1, -1, -1):
        rows = tokens >> level
        for h in heads:
            peak = joined(h, level, peaks)
            total = joined(h, level, sums)
            tiles[h] = jnp.where(row == level, jnp.max(peak), tiles[h])
            peak = jnp.broadcast_to(peak + level * LOG_TWO, (rows, DH))
            total, summed = total[:, DH:], total[:, :DH]
            if level < LEVELS - 1:
                place = h * 2 * tokens + base
                peak_up, total_up, summed_up = [
                    expand_two(scratch, place, value)
                    for scratch, value in zip((peak_s, total_s, summed_s), state[h])
                ]
                top = jnp.maximum(peak, peak_up)
                mine = jnp.exp(peak - top)
                other = jnp.exp(peak_up - top)
                total = mine * total + other * total_up
                summed = mine * summed + other * summed_up
                peak = top
            state[h] = (peak, total, summed)
        if level < LEVELS - 1:
            base += rows
    for h in heads:
        peak, total, summed = state[h]
        attn_ref[:, columns[h]] = (summed / total).astype(BF16)
        lse_ref[:, columns[h]] = peak + jnp.log(total)
        top_ref[h] = tiles[h]


def forward_call(query, key, value, received, after=(), step=2):
    tokens, width = query.shape
    heads = width // DH
    spec = pl.BlockSpec((tokens, step * DH), lambda h: (0, h))
    others = [pl.BlockSpec((r.shape[0], step * DH), lambda h: (0, h)) for r in received]
    others += [pl.BlockSpec(memory_space=pl.ANY)] * len(after)
    return pl.pallas_call(
        functools.partial(forward_kernel, extra=len(after)),
        grid=(heads // step,),
        in_specs=[spec, spec, spec] + others,
        out_specs=[spec, spec, pl.BlockSpec((step, 8, 128), lambda h: (h, 0, 0))],
        out_shape=[
            jax.ShapeDtypeStruct((tokens, width), BF16),
            jax.ShapeDtypeStruct((tokens, width), F32),
            jax.ShapeDtypeStruct((heads, 8, 128), F32),
        ],
        scratch_shapes=[
            pltpu.VMEM((tokens - tokens // 16, tokens), BF16),
            pltpu.VMEM((step * 2 * tokens, 128), F32),
            pltpu.VMEM((step * 2 * tokens, 128), F32),
            pltpu.VMEM((step * 2 * tokens, 128), F32),
        ],
        compiler_params=pltpu.CompilerParams(vmem_limit_bytes=VMEM_LIMIT),
        name="attention_forward",
    )(query, key, value, *received, *after)


def backward_kernel(
    q_ref, k_ref, v_ref, attn_ref, grad_ref, lse_ref, near, three, four_a, four_b, *rest, extra
):
    gq_ref, gk_ref, gv_ref, far, keep, pool, lse_s, grad_s, scal_s, gq_s, gk_s, gv_s = rest[extra:]
    tokens, width = q_ref.shape

    @pl.when(pl.program_id(0) == 0)
    def _():
        fill_pool(pool, tokens)

    q_all = dot_nn(pool[...], q_ref[...]).astype(BF16)
    half_rows = pl.ds(0, tokens // 2)
    k_one = dot_nn(pool[half_rows, :], k_ref[...]).astype(BF16)
    v_one = dot_nn(pool[half_rows, :], v_ref[...]).astype(BF16)
    where = coarse_slices(tokens)
    heads = range(width // DH)
    columns = [pl.ds(h * DH, DH) for h in heads]
    lanes = [slice(h * DH, (h + 1) * DH) for h in heads]
    scalars = []
    for h in heads:
        grad_f = grad_ref[:, columns[h]].astype(F32)
        scalar = jnp.sum(grad_f * attn_ref[:, columns[h]].astype(F32), axis=-1, keepdims=True)
        scalars.append(scalar)
        first = pl.ds(h * 2 * tokens, tokens)
        lse_s[first, :] = lse_ref[:, columns[h]]
        scal_s[first, :] = jnp.broadcast_to(scalar, (tokens, 128))
        grad_s[first, :] = grad_f
    places = {}
    base = 0
    rows = tokens
    for level in range(1, LEVELS):
        half = rows // 2
        for h in heads:
            start = h * 2 * tokens + base
            even = pl.ds(start, half, stride=2)
            odd = pl.ds(start + 1, half, stride=2)
            lse_even, lse_odd = lse_s[even, :], lse_s[odd, :]
            least = jnp.minimum(lse_even, lse_odd)
            factor_even = jnp.exp(least - lse_even)
            factor_odd = jnp.exp(least - lse_odd)
            summed = factor_even * grad_s[even, :] + factor_odd * grad_s[odd, :]
            summed_scalar = factor_even * scal_s[even, :] + factor_odd * scal_s[odd, :]
            if level < LEVELS - 1:
                nxt = pl.ds(start + rows, half)
                lse_s[nxt, :] = least
                grad_s[nxt, :] = summed
                scal_s[nxt, :] = summed_scalar
            places[h, level] = (least, summed.astype(BF16), summed_scalar)
        base += rows
        rows = half
    work = []
    for h in heads:
        partner = partner_rows(near, three, four_a, four_b, columns[h])
        for level in range(LEVELS - 1, -1, -1):
            if level >= 2:
                work.append(
                    (h, level, q_all[where[level], lanes[h]], *partner[level], *places[h, level])
                )
            elif level == 1:
                low, gr, sc = places[h, 1]
                qc, kc, vc = q_all[where[1], lanes[h]], k_one[:, lanes[h]], v_one[:, lanes[h]]
                for b in range(2):
                    mine = slice(b * BLK, (b + 1) * BLK)
                    other = slice((1 - b) * BLK, (2 - b) * BLK)
                    work.append((h, 1, qc[mine], kc[other], vc[other], low[mine], gr[mine], sc[mine]))
            else:
                for b in range(tokens // (2 * BLK)):
                    both = pl.ds(b * 2 * BLK, 2 * BLK)
                    part = slice(b * 2 * BLK, (b + 1) * 2 * BLK)
                    low = lse_ref[both, columns[h]]
                    work.append((
                        h, 0, q_ref[both, columns[h]], k_ref[both, columns[h]], v_ref[both, columns[h]],
                        jnp.concatenate([low, low], 1), grad_ref[both, columns[h]], scalars[h][part],
                    ))
    scores = [dot_nt(item[2], item[3]) for item in work]
    grads = [dot_nt(item[6], item[4]) for item in work]
    weights = [
        jnp.exp(s * SCALE + (item[1] * LOG_TWO - item[5])) for s, item in zip(scores, work)
    ]
    grad_scores = [
        (w * (g - item[7])).astype(BF16) for w, g, item in zip(weights, grads, work)
    ]
    weights = [w.astype(BF16) for w in weights]
    parts_q = [dot_nn(s, item[3]) * SCALE for s, item in zip(grad_scores, work)]
    parts_k = [dot_tn(s, item[2]) * SCALE for s, item in zip(grad_scores, work)]
    parts_v = [dot_tn(w, item[6]) for w, item in zip(weights, work)]
    found = {}
    for item, *parts in zip(work, parts_q, parts_k, parts_v):
        found.setdefault(item[:2], []).append(parts)
    state = {}
    up = 0
    for level in range(LEVELS - 1, -1, -1):
        rows = tokens >> level
        for h in heads:
            parts = found[h, level]
            if level >= 2:
                part_q, part_k, part_v = parts[0]
                part_k = part_k.astype(BF16)
                part_v = part_v.astype(BF16)
                outs = {
                    2: ((far, 0),),
                    3: ((keep, 0), (far, 2 * BLK)),
                    4: ((keep, BLK), (keep, BLK + BLK // 2), (far, 3 * BLK), (far, 3 * BLK + BLK // 2)),
                }[level]
                piece = BLK // len(outs)
                for i, (out, at) in enumerate(outs):
                    out[pl.ds(at, piece), columns[h]] = part_k[i * piece : (i + 1) * piece]
                    out[pl.ds(at + piece, piece), columns[h]] = part_v[i * piece : (i + 1) * piece]
            elif level == 1:
                part_q = jnp.concatenate([parts[0][0], parts[1][0]], 0)
                part_k = jnp.concatenate([parts[1][1], parts[0][1]], 0)
                part_v = jnp.concatenate([parts[1][2], parts[0][2]], 0)
                coarse_k = expand_two(gk_s, h * tokens, part_k * 0.5)
                coarse_v = expand_two(gv_s, h * tokens, part_v * 0.5)
                state[h, "k"], state[h, "v"] = coarse_k, coarse_v
            if level == 0:
                for b, (part_q, part_k, part_v) in enumerate(parts):
                    both = slice(b * 2 * BLK, (b + 1) * 2 * BLK)
                    here = pl.ds(b * 2 * BLK, 2 * BLK)
                    gq_ref[here, columns[h]] = part_q + state[h, "q"][both]
                    gk_ref[here, columns[h]] = part_k + state[h, "k"][both]
                    gv_ref[here, columns[h]] = part_v + state[h, "v"][both]
            else:
                grad_q = part_q if level == LEVELS - 1 else part_q + state[h, "q"]
                state[h, "q"] = expand_two(gq_s, h * 2 * tokens + up, grad_q * 0.5)
        up += 2 * rows


def backward_call(query, key, value, attn, grad, lse, received, after=(), step=2):
    tokens, width = query.shape
    heads = width // DH
    spec = pl.BlockSpec((tokens, step * DH), lambda h: (0, h))
    others = [pl.BlockSpec((r.shape[0], step * DH), lambda h: (0, h)) for r in received]
    others += [pl.BlockSpec(memory_space=pl.ANY)] * len(after)
    full = jax.ShapeDtypeStruct((tokens, width), F32)
    outs = [spec, pl.BlockSpec((tokens // 2, step * DH), lambda h: (0, h))]
    return pl.pallas_call(
        functools.partial(backward_kernel, extra=len(after)),
        grid=(heads // step,),
        in_specs=[spec] * 6 + others,
        out_specs=[spec] * 3 + outs,
        out_shape=[full] * 3
        + [jax.ShapeDtypeStruct((tokens, width), BF16), jax.ShapeDtypeStruct((tokens // 2, width), BF16)],
        scratch_shapes=[pltpu.VMEM((tokens - tokens // 16, tokens), BF16)]
        + [pltpu.VMEM((step * 2 * tokens, 128), F32)] * 6,
        compiler_params=pltpu.CompilerParams(vmem_limit_bytes=VMEM_LIMIT),
        name="attention_backward",
    )(query, key, value, attn, grad, lse, *received, *after)


def finish_kernel(gk_ref, gv_ref, near, three, four, ok_ref, ov_ref, k_s, v_s):
    for part, local, out, scr in ((0, gk_ref, ok_ref, k_s), (1, gv_ref, ov_ref, v_s)):
        state = None
        base = 0
        for ref, rows in ((four, BLK // 4), (three, BLK // 2), (near, BLK)):
            total = ref[pl.ds(part * rows, rows), :].astype(F32)
            state = total if state is None else total + state
            state = expand_two(scr, base, state * 0.5)
            base += 2 * rows
        state = expand_two(scr, base, state * 0.5)
        out[...] = local[...] + state


def finish_call(grad_k, grad_v, near, three, four):
    tokens, width = grad_k.shape
    step = 128
    spec = pl.BlockSpec((tokens, step), lambda h: (0, h))
    rows = (2 * BLK, BLK, BLK // 2)
    extra = [pl.BlockSpec((r, step), lambda h: (0, h)) for r in rows]
    full = jax.ShapeDtypeStruct((tokens, width), F32)
    scratch = pltpu.VMEM((2 * tokens, step), F32)
    return pl.pallas_call(
        finish_kernel,
        grid=(width // step,),
        in_specs=[spec, spec] + extra,
        out_specs=[spec, spec],
        out_shape=[full, full],
        scratch_shapes=[scratch, scratch],
        compiler_params=pltpu.CompilerParams(vmem_limit_bytes=VMEM_LIMIT),
        name="add_returned",
    )(grad_k, grad_v, near, three, four)


def assemble_kernel(core_ref, *refs, pairs, column):
    count = len(pairs)
    sources = refs[: sum(pairs)]
    outs = refs[sum(pairs) :]
    whole, mine_ref, send_ref = outs[:count], outs[count], outs[count + 1]
    first = core_ref[0] == 0
    at = 0
    for index, number in enumerate(pairs):
        chunk = sources[at][...]
        if number == 2:
            chunk = chunk + sources[at + 1][...]
        at += number
        whole[index][...] = chunk
        width = chunk.shape[1]
        for group in range(width // (2 * column)):
            low = chunk[:, 2 * group * column : (2 * group + 1) * column]
            high = chunk[:, (2 * group + 1) * column : (2 * group + 2) * column]
            here = pl.ds(index * width // 2 + group * column, column)
            mine_ref[:, here] = jnp.where(first, low, high)
            send_ref[:, here] = jnp.where(first, high, low)


def assemble_call(chunks, core, column):
    flat = [array for chunk in chunks for array in chunk]
    tokens, width = flat[0].shape
    count = len(chunks)
    rows = 128
    spec = pl.BlockSpec((rows, width), lambda i: (i, 0))
    half = pl.BlockSpec((rows, count * width // 2), lambda i: (i, 0))
    outs = pl.pallas_call(
        functools.partial(assemble_kernel, pairs=tuple(len(c) for c in chunks), column=column),
        grid=(tokens // rows,),
        in_specs=[pl.BlockSpec(memory_space=pltpu.SMEM)] + [spec] * len(flat),
        out_specs=[spec] * count + [half, half],
        out_shape=[jax.ShapeDtypeStruct((tokens, width), BF16)] * count
        + [jax.ShapeDtypeStruct((tokens, count * width // 2), BF16)] * 2,
        compiler_params=pltpu.CompilerParams(vmem_limit_bytes=VMEM_LIMIT),
        name="assemble",
    )(core.reshape(1).astype(jnp.int32), *flat)
    return outs[:count], outs[count], outs[count + 1]


def term_order(chips):
    top = chips // 2
    groups = {(1, 0): [], (1, 1): [], (0, 1): [], (0, 0): []}
    for i in range(chips):
        groups[i & 1, int(i & top != 0)].append(i)
    return [i for key in ((1, 0), (1, 1), (0, 1), (0, 0)) for i in groups[key]]


def term_kernel(place_ref, turned_ref, mine_ref, theirs_ref, a_send, a_keep, b_send, b_keep, *, chips):
    step = pl.program_id(0)
    tokens = mine_ref.shape[0]
    half = turned_ref.shape[0] // 2

    def rows(start):
        here = pl.ds(start, half)
        return dot_nn(turned_ref[here, pl.ds(0, tokens)], mine_ref[...]) + dot_nn(
            turned_ref[here, pl.ds(tokens, tokens)], theirs_ref[...]
        )

    top = rows(0).astype(BF16)
    bottom = rows(half).astype(BF16)

    @pl.when(step < chips // 2)
    def _():
        a_send[0] = top

    @pl.when(step >= chips // 2)
    def _():
        a_keep[0] = top

    middle = jnp.logical_and(step >= chips // 4, step < 3 * chips // 4)

    @pl.when(middle)
    def _():
        b_send[0] = bottom

    @pl.when(jnp.logical_not(middle))
    def _():
        b_keep[0] = bottom


def term_call(turned, mine, theirs, place, column):
    features = turned.shape[0]
    tokens = mine.shape[0]
    chips = place.shape[0]
    half, quarter = chips // 2, chips // 4
    source = pl.BlockSpec((tokens, column), lambda i, p: (0, p[i]))
    shape = (1, features // 2, column)
    outs = [
        pl.BlockSpec(shape, lambda i, p: (jnp.minimum(i, half - 1), 0, 0)),
        pl.BlockSpec(shape, lambda i, p: (jnp.maximum(i - half, 0), 0, 0)),
        pl.BlockSpec(shape, lambda i, p: (jnp.clip(i - quarter, 0, half - 1), 0, 0)),
        pl.BlockSpec(
            shape,
            lambda i, p: (jnp.where(i < 3 * quarter, jnp.minimum(i, quarter - 1), i - half), 0, 0),
        ),
    ]
    return pl.pallas_call(
        functools.partial(term_kernel, chips=chips),
        grid_spec=pltpu.PrefetchScalarGridSpec(
            num_scalar_prefetch=1,
            grid=(chips,),
            in_specs=[pl.BlockSpec((features, 2 * tokens), lambda i, p: (0, 0)), source, source],
            out_specs=outs,
        ),
        out_shape=[jax.ShapeDtypeStruct((half, features // 2, column), BF16)] * 4,
        compiler_params=pltpu.CompilerParams(vmem_limit_bytes=VMEM_LIMIT),
        name="weight_terms",
    )(place, turned, mine, theirs)


def halve(sent, kept, bits, mask_of):
    for n, bit in enumerate(bits):
        arrived = swap(sent[1], "ctx", mask_of(bit))
        names = [i ^ bit for i in sent[0]]
        parts = {}
        for k, i in enumerate(kept[0]):
            parts[i] = kept[1][k].astype(F32) + arrived[names.index(i)].astype(F32)
        if n + 1 == len(bits):
            return parts[0]
        cut = lambda flag: [i for i in kept[0] if (i & bits[n + 1] != 0) == flag]
        pack = lambda names: (names, jnp.stack([parts[i].astype(BF16) for i in names]))
        sent, kept = pack(cut(True)), pack(cut(False))


def swap(value, axis, mask):
    return lax.ppermute(value, axis, [(i, i ^ mask) for i in range(lax.axis_size(axis))])


def per_device(query, key, value, out_weight, cotangent):
    tokens, width = query.shape
    model = out_weight.shape[1]
    count = lax.axis_size("head")
    ctx_count = lax.axis_size("ctx")
    column = model // ctx_count
    me = lax.axis_index("ctx")
    z = lax.axis_index("head")

    right, left = cotangent, cotangent
    from_left, from_right = [None], [None]
    for step in range(1, count):
        right = lax.ppermute(right, "head", [(i, i + 1) for i in range(step - 1, count - 1)])
        left = lax.ppermute(left, "head", [(i, i - 1) for i in range(1, count - step + 1)])
        from_left.append(right)
        from_right.append(left)

    two, three, four = pool_call(key, value)
    three = swap(three, "ctx", 2)
    four_a = swap(four, "ctx", 4)
    four_b = swap(four, "ctx", 6)
    near = swap(jnp.concatenate([two, three, four_a, four_b], 0), "ctx", 1)
    received = (near, three, four_a, four_b)

    weights = [
        lax.dynamic_slice(
            out_weight, (0, lax.rem(z - s + count, count) * width), (out_weight.shape[0], width)
        )
        for s in range(count)
    ]

    attn, lse, tops = forward_call(query, key, value, received)
    level_max = jnp.max(lax.all_gather(jnp.transpose(tops[:, :LEVELS, 0]), "ctx"), axis=0)
    attn_other = swap(attn, "ctx", 1)
    turned = jnp.concatenate([attn.T, attn_other.T], 1)

    to_left = to_right = None
    for step in range(1, count):
        piece = dot_nn(attn, weights[count - step])
        to_left = (piece if to_left is None else piece + to_left).astype(BF16)
        to_left = lax.ppermute(to_left, "head", [(i, i - 1) for i in range(count - step, count)])
        piece = dot_nn(attn, weights[step])
        to_right = (piece if to_right is None else piece + to_right).astype(BF16)
        to_right = lax.ppermute(to_right, "head", [(i, i + 1) for i in range(0, step)])
    mixed = dot_nn(attn, weights[0]) + to_left + to_right

    core = me % 2
    early = [s for s in range(count) if s not in (1, count - 1)]
    late = sorted({1, count - 1})
    grad_attn = None
    mine, theirs = [], []
    for group in (early, late):
        chunks = [(cotangent,) if s == 0 else (from_left[s], from_right[count - s]) for s in group]
        whole, here, send = assemble_call(chunks, core, column)
        mine.append(here)
        theirs.append(swap(send, "ctx", 1))
        for s, chunk in zip(group, whole):
            part = dot_nt(chunk, weights[s])
            grad_attn = part if grad_attn is None else grad_attn + part
    grad_attn = grad_attn.astype(BF16)

    chips = ctx_count // 2
    per_chunk = chips // count
    slots = {s: n for n, s in enumerate(early + late)}
    slot = jnp.array([slots[s] for s in range(count)], jnp.int32)
    order = term_order(chips)
    chip = jnp.bitwise_xor(me // 2, jnp.array(order, jnp.int32))
    place = slot[lax.rem(z - chip // per_chunk + count, count)] * per_chunk + chip % per_chunk
    terms = term_call(
        turned, jnp.concatenate(mine, 1), jnp.concatenate(theirs, 1), place.astype(jnp.int32), column
    )
    half, quarter = chips // 2, chips // 4
    bits = [1 << n for n in range(chips.bit_length() - 1)]
    mask_of = lambda bit: 2 * bit
    top_rows = halve((order[:half], terms[0]), (order[half:], terms[1]), bits, mask_of)
    bottom_rows = halve(
        (order[quarter : 3 * quarter], terms[2]),
        (order[:quarter] + order[3 * quarter :], terms[3]),
        bits[::-1],
        mask_of,
    )
    weight_grad = jnp.concatenate([top_rows, bottom_rows], 0)

    outs = backward_call(query, key, value, attn, grad_attn, lse, received, after=terms)
    grad_q, grad_k, grad_v, far, keep = outs
    far = swap(far, "ctx", 1)
    half = tokens // 2
    keep = (keep.astype(F32) + far[half:].astype(F32)).astype(BF16)
    third = BLK + BLK // 2
    sent = jnp.concatenate([keep[:BLK], keep[third:]], 0)
    back = swap(sent, "ctx", 2)
    back_four = swap((keep[BLK:third].astype(F32) + back[BLK:].astype(F32)).astype(BF16), "ctx", 4)
    grad_k, grad_v = finish_call(grad_k, grad_v, far, back, back_four)
    return mixed, grad_q, grad_k, grad_v, weight_grad, level_max


def solution(mesh):
    tokens = P("ctx", "head")
    return jax.shard_map(
        per_device,
        mesh=mesh,
        in_specs=(tokens, tokens, tokens, P("head", None), tokens),
        out_specs=(tokens, tokens, tokens, tokens, P("head", "ctx"), P(None, "head")),
        check_vma=False,
    )
```

```python
import functools
import math

import jax
import jax.numpy as jnp
from jax import lax
from jax.experimental import pallas as pl
from jax.experimental.pallas import tpu as pltpu
from jax.sharding import PartitionSpec as P

DH = 128
BLK = 128
LEVELS = 5
SCALE = DH ** (-0.5)
LOG_TWO = math.log(2.0)
F32 = jnp.float32
BF16 = jnp.bfloat16
VMEM_LIMIT = 60 * 1024 * 1024


def dot_nn(a, b):
    return lax.dot_general(a, b, (((1,), (0,)), ((), ())), preferred_element_type=F32)


def dot_nt(a, b):
    return lax.dot_general(a, b, (((1,), (1,)), ((), ())), preferred_element_type=F32)


def dot_tn(a, b):
    return lax.dot_general(a, b, (((0,), (0,)), ((), ())), preferred_element_type=F32)


def pool_matrix(level, rows, tokens):
    row = lax.broadcasted_iota(jnp.int32, (rows, tokens), 0)
    token = lax.broadcasted_iota(jnp.int32, (rows, tokens), 1)
    return jnp.where(lax.shift_right_logical(token, level) == row, 0.5**level, 0.0).astype(BF16)


def fill_pool(pool, tokens):
    base = 0
    for level in range(1, LEVELS):
        rows = tokens >> level
        pool[pl.ds(base, rows), :] = pool_matrix(level, rows, tokens)
        base += rows


def pool_kernel(k_ref, v_ref, near_ref, three_ref, four_ref):
    tokens = k_ref.shape[0]
    matrix = jnp.concatenate([pool_matrix(l, tokens >> l, tokens) for l in (2, 3, 4)], 0)
    for part, ref in enumerate((k_ref, v_ref)):
        rows = dot_nn(matrix, ref[...]).astype(BF16)
        base = 0
        for level, out in ((2, near_ref), (3, three_ref), (4, four_ref)):
            size = tokens >> level
            out[pl.ds(part * size, size), :] = rows[base : base + size]
            base += size


def pool_call(key, value):
    tokens, width = key.shape
    step = min(512, width)
    spec = pl.BlockSpec((tokens, step), lambda i: (0, i))
    rows = [2 * (tokens >> level) for level in (2, 3, 4)]
    return pl.pallas_call(
        pool_kernel,
        grid=(width // step,),
        in_specs=[spec, spec],
        out_specs=[pl.BlockSpec((r, step), lambda i: (0, i)) for r in rows],
        out_shape=[jax.ShapeDtypeStruct((r, width), BF16) for r in (tokens, *rows[1:])],
        compiler_params=pltpu.CompilerParams(vmem_limit_bytes=VMEM_LIMIT),
        name="pool_keys",
    )(key, value)


def lower_kernel(near_in, three_ref, four_a, four_b, near_out):
    base = 0
    for ref in (three_ref, four_a, four_b):
        near_out[pl.ds(base, ref.shape[0]), :] = ref[...]
        base += ref.shape[0]


def lower_call(near, three, four_a, four_b):
    tokens, width = near.shape
    spec = lambda r: pl.BlockSpec((r.shape[0], width), lambda i: (0, 0))
    return pl.pallas_call(
        lower_kernel,
        grid=(1,),
        in_specs=[pl.BlockSpec(memory_space=pl.ANY), spec(three), spec(four_a), spec(four_b)],
        out_specs=pl.BlockSpec((tokens // 2, width), lambda i: (1, 0)),
        out_shape=jax.ShapeDtypeStruct((tokens, width), BF16),
        input_output_aliases={0: 0},
        compiler_params=pltpu.CompilerParams(vmem_limit_bytes=VMEM_LIMIT),
        name="lower_rows",
    )(near, three, four_a, four_b)


def expand_two(scratch, base, value):
    rows = value.shape[0]
    scratch[pl.ds(base, rows, stride=2), :] = value
    scratch[pl.ds(base + 1, rows, stride=2), :] = value
    return scratch[pl.ds(base, 2 * rows), :]


def partner_rows(near, three, four_a, four_b, columns):
    def cut(ref, base, half):
        return ref[pl.ds(base, half), columns], ref[pl.ds(base + half, half), columns]

    two = BLK
    join = lambda *pairs: tuple(jnp.concatenate(p, 0) for p in zip(*pairs))
    return {
        2: cut(near, 0, two),
        3: join(cut(three, 0, two // 2), cut(near, 2 * two, two // 2)),
        4: join(
            cut(four_a, 0, two // 4),
            cut(four_b, 0, two // 4),
            cut(near, 3 * two, two // 4),
            cut(near, 3 * two + two // 2, two // 4),
        ),
    }


def coarse_slices(tokens):
    base = 0
    found = {}
    for level in range(1, LEVELS):
        rows = tokens >> level
        found[level] = slice(base, base + rows)
        base += rows
    return found


def forward_kernel(
    q_ref, k_ref, v_ref, near, three, four_a, four_b, *rest, extra
):
    attn_ref, turned_ref, lse_ref, top_ref, pool, peak_s, total_s, summed_s = rest[extra:]
    tokens, width = q_ref.shape

    @pl.when(pl.program_id(0) == 0)
    def _():
        fill_pool(pool, tokens)

    q_all = dot_nn(pool[...], q_ref[...]).astype(BF16)
    half = pl.ds(0, tokens // 2)
    k_one = dot_nn(pool[half, :], k_ref[...]).astype(BF16)
    v_one = dot_nn(pool[half, :], v_ref[...]).astype(BF16)
    where = coarse_slices(tokens)
    heads = range(width // DH)
    columns = [pl.ds(h * DH, DH) for h in heads]
    lanes = [slice(h * DH, (h + 1) * DH) for h in heads]
    work = []
    for h in heads:
        partner = partner_rows(near, three, four_a, four_b, columns[h])
        for level in range(LEVELS - 1, -1, -1):
            if level >= 2:
                work.append((h, level, q_all[where[level], lanes[h]], *partner[level]))
            elif level == 1:
                qc, kc, vc = q_all[where[1], lanes[h]], k_one[:, lanes[h]], v_one[:, lanes[h]]
                for b in range(2):
                    mine = slice(b * BLK, (b + 1) * BLK)
                    other = slice((1 - b) * BLK, (2 - b) * BLK)
                    work.append((h, 1, qc[mine], kc[other], vc[other]))
            else:
                for b in range(tokens // (2 * BLK)):
                    both = pl.ds(b * 2 * BLK, 2 * BLK)
                    work.append(
                        (h, 0, q_ref[both, columns[h]], k_ref[both, columns[h]], v_ref[both, columns[h]])
                    )
    scores = [dot_nt(q, k) * SCALE for _, _, q, k, _ in work]
    peaks = [jnp.max(s, axis=-1, keepdims=True) for s in scores]
    weights = [jnp.exp(s - p).astype(BF16) for s, p in zip(scores, peaks)]
    sums = [
        dot_nn(w, jnp.concatenate([item[4], jnp.ones_like(item[4])], 1))
        for w, item in zip(weights, work)
    ]

    def joined(h, level, values):
        return jnp.concatenate([x for x, item in zip(values, work) if item[:2] == (h, level)], 0)

    row = lax.broadcasted_iota(jnp.int32, (8, 128), 0)
    tiles = [jnp.zeros((8, 128), F32) for _ in heads]
    state = {}
    base = 0
    for level in range(LEVELS - 1, -1, -1):
        rows = tokens >> level
        for h in heads:
            peak = joined(h, level, peaks)
            total = joined(h, level, sums)
            tiles[h] = jnp.where(row == level, jnp.max(peak), tiles[h])
            peak = jnp.broadcast_to(peak + level * LOG_TWO, (rows, DH))
            total, summed = total[:, DH:], total[:, :DH]
            if level < LEVELS - 1:
                place = h * 2 * tokens + base
                peak_up, total_up, summed_up = [
                    expand_two(scratch, place, value)
                    for scratch, value in zip((peak_s, total_s, summed_s), state[h])
                ]
                top = jnp.maximum(peak, peak_up)
                mine = jnp.exp(peak - top)
                other = jnp.exp(peak_up - top)
                total = mine * total + other * total_up
                summed = mine * summed + other * summed_up
                peak = top
            state[h] = (peak, total, summed)
        if level < LEVELS - 1:
            base += rows
    for h in heads:
        peak, total, summed = state[h]
        attn = (summed / total).astype(BF16)
        attn_ref[:, columns[h]] = attn
        turned_ref[columns[h], :] = attn.T
        lse_ref[:, columns[h]] = peak + jnp.log(total)
        top_ref[h] = tiles[h]


def forward_call(query, key, value, received, after=(), step=4):
    tokens, width = query.shape
    heads = width // DH
    spec = pl.BlockSpec((tokens, step * DH), lambda h: (0, h))
    others = [pl.BlockSpec((r.shape[0], step * DH), lambda h: (0, h)) for r in received]
    others += [pl.BlockSpec(memory_space=pl.ANY)] * len(after)
    return pl.pallas_call(
        functools.partial(forward_kernel, extra=len(after)),
        grid=(heads // step,),
        in_specs=[spec, spec, spec] + others,
        out_specs=[
            spec,
            pl.BlockSpec((step * DH, tokens), lambda h: (h, 0)),
            spec,
            pl.BlockSpec((step, 8, 128), lambda h: (h, 0, 0)),
        ],
        out_shape=[
            jax.ShapeDtypeStruct((tokens, width), BF16),
            jax.ShapeDtypeStruct((width, tokens), BF16),
            jax.ShapeDtypeStruct((tokens, width), F32),
            jax.ShapeDtypeStruct((heads, 8, 128), F32),
        ],
        scratch_shapes=[
            pltpu.VMEM((tokens - tokens // 16, tokens), BF16),
            pltpu.VMEM((step * 2 * tokens, 128), F32),
            pltpu.VMEM((step * 2 * tokens, 128), F32),
            pltpu.VMEM((step * 2 * tokens, 128), F32),
        ],
        compiler_params=pltpu.CompilerParams(vmem_limit_bytes=VMEM_LIMIT),
        name="attention_forward",
    )(query, key, value, *received, *after)


def backward_kernel(
    q_ref, k_ref, v_ref, attn_ref, grad_ref, lse_ref, near, three, four_a, four_b, *rest, extra
):
    gq_ref, gk_ref, gv_ref, far, keep, four, pool, lse_s, grad_s, scal_s, gq_s, gk_s, gv_s = rest[extra:]
    tokens, width = q_ref.shape

    @pl.when(pl.program_id(0) == 0)
    def _():
        fill_pool(pool, tokens)

    q_all = dot_nn(pool[...], q_ref[...]).astype(BF16)
    half_rows = pl.ds(0, tokens // 2)
    k_one = dot_nn(pool[half_rows, :], k_ref[...]).astype(BF16)
    v_one = dot_nn(pool[half_rows, :], v_ref[...]).astype(BF16)
    where = coarse_slices(tokens)
    heads = range(width // DH)
    columns = [pl.ds(h * DH, DH) for h in heads]
    lanes = [slice(h * DH, (h + 1) * DH) for h in heads]
    scalars = []
    for h in heads:
        grad_f = grad_ref[:, columns[h]].astype(F32)
        scalar = jnp.sum(grad_f * attn_ref[:, columns[h]].astype(F32), axis=-1, keepdims=True)
        scalars.append(scalar)
        first = pl.ds(h * 2 * tokens, tokens)
        lse_s[first, :] = lse_ref[:, columns[h]]
        scal_s[first, :] = jnp.broadcast_to(scalar, (tokens, 128))
        grad_s[first, :] = grad_f
    places = {}
    base = 0
    rows = tokens
    for level in range(1, LEVELS):
        half = rows // 2
        for h in heads:
            start = h * 2 * tokens + base
            even = pl.ds(start, half, stride=2)
            odd = pl.ds(start + 1, half, stride=2)
            lse_even, lse_odd = lse_s[even, :], lse_s[odd, :]
            least = jnp.minimum(lse_even, lse_odd)
            factor_even = jnp.exp(least - lse_even)
            factor_odd = jnp.exp(least - lse_odd)
            summed = factor_even * grad_s[even, :] + factor_odd * grad_s[odd, :]
            summed_scalar = factor_even * scal_s[even, :] + factor_odd * scal_s[odd, :]
            if level < LEVELS - 1:
                nxt = pl.ds(start + rows, half)
                lse_s[nxt, :] = least
                grad_s[nxt, :] = summed
                scal_s[nxt, :] = summed_scalar
            places[h, level] = (least, summed.astype(BF16), summed_scalar)
        base += rows
        rows = half
    work = []
    for h in heads:
        partner = partner_rows(near, three, four_a, four_b, columns[h])
        for level in range(LEVELS - 1, -1, -1):
            if level >= 2:
                work.append(
                    (h, level, q_all[where[level], lanes[h]], *partner[level], *places[h, level])
                )
            elif level == 1:
                low, gr, sc = places[h, 1]
                qc, kc, vc = q_all[where[1], lanes[h]], k_one[:, lanes[h]], v_one[:, lanes[h]]
                for b in range(2):
                    mine = slice(b * BLK, (b + 1) * BLK)
                    other = slice((1 - b) * BLK, (2 - b) * BLK)
                    work.append((h, 1, qc[mine], kc[other], vc[other], low[mine], gr[mine], sc[mine]))
            else:
                for b in range(tokens // (2 * BLK)):
                    both = pl.ds(b * 2 * BLK, 2 * BLK)
                    part = slice(b * 2 * BLK, (b + 1) * 2 * BLK)
                    low = lse_ref[both, columns[h]]
                    work.append((
                        h, 0, q_ref[both, columns[h]], k_ref[both, columns[h]], v_ref[both, columns[h]],
                        jnp.concatenate([low, low], 1), grad_ref[both, columns[h]], scalars[h][part],
                    ))
    scores = [dot_nt(item[2], item[3]) for item in work]
    grads = [dot_nt(item[6], item[4]) for item in work]
    weights = [
        jnp.exp(s * SCALE + (item[1] * LOG_TWO - item[5])) for s, item in zip(scores, work)
    ]
    grad_scores = [
        (w * (g - item[7])).astype(BF16) for w, g, item in zip(weights, grads, work)
    ]
    weights = [w.astype(BF16) for w in weights]
    parts_q = [dot_nn(s, item[3]) * SCALE for s, item in zip(grad_scores, work)]
    parts_k = [dot_tn(s, item[2]) * SCALE for s, item in zip(grad_scores, work)]
    parts_v = [dot_tn(w, item[6]) for w, item in zip(weights, work)]
    found = {}
    for item, *parts in zip(work, parts_q, parts_k, parts_v):
        found.setdefault(item[:2], []).append(parts)
    state = {}
    up = 0
    for level in range(LEVELS - 1, -1, -1):
        rows = tokens >> level
        for h in heads:
            parts = found[h, level]
            if level >= 2:
                part_q, part_k, part_v = parts[0]
                part_k = part_k.astype(BF16)
                part_v = part_v.astype(BF16)
                outs = {
                    2: ((far, 0),),
                    3: ((keep, 0), (far, 2 * BLK)),
                    4: ((four, 0), (keep, BLK), (far, 3 * BLK + BLK // 2), (far, 3 * BLK)),
                }[level]
                piece = BLK // len(outs)
                for i, (out, at) in enumerate(outs):
                    out[pl.ds(at, piece), columns[h]] = part_k[i * piece : (i + 1) * piece]
                    out[pl.ds(at + piece, piece), columns[h]] = part_v[i * piece : (i + 1) * piece]
            elif level == 1:
                part_q = jnp.concatenate([parts[0][0], parts[1][0]], 0)
                part_k = jnp.concatenate([parts[1][1], parts[0][1]], 0)
                part_v = jnp.concatenate([parts[1][2], parts[0][2]], 0)
                coarse_k = expand_two(gk_s, h * tokens, part_k * 0.5)
                coarse_v = expand_two(gv_s, h * tokens, part_v * 0.5)
                state[h, "k"], state[h, "v"] = coarse_k, coarse_v
            if level == 0:
                for b, (part_q, part_k, part_v) in enumerate(parts):
                    both = slice(b * 2 * BLK, (b + 1) * 2 * BLK)
                    here = pl.ds(b * 2 * BLK, 2 * BLK)
                    gq_ref[here, columns[h]] = part_q + state[h, "q"][both]
                    gk_ref[here, columns[h]] = part_k + state[h, "k"][both]
                    gv_ref[here, columns[h]] = part_v + state[h, "v"][both]
            else:
                grad_q = part_q if level == LEVELS - 1 else part_q + state[h, "q"]
                state[h, "q"] = expand_two(gq_s, h * 2 * tokens + up, grad_q * 0.5)
        up += 2 * rows


def backward_call(query, key, value, attn, grad, lse, received, after=(), step=2):
    tokens, width = query.shape
    heads = width // DH
    spec = pl.BlockSpec((tokens, step * DH), lambda h: (0, h))
    others = [pl.BlockSpec((r.shape[0], step * DH), lambda h: (0, h)) for r in received]
    others += [pl.BlockSpec(memory_space=pl.ANY)] * len(after)
    full = jax.ShapeDtypeStruct((tokens, width), F32)
    back_rows = (tokens, BLK + BLK // 2, BLK // 2)
    outs = [pl.BlockSpec((r, step * DH), lambda h: (0, h)) for r in back_rows]
    return pl.pallas_call(
        functools.partial(backward_kernel, extra=len(after)),
        grid=(heads // step,),
        in_specs=[spec] * 6 + others,
        out_specs=[spec] * 3 + outs,
        out_shape=[full] * 3
        + [jax.ShapeDtypeStruct((r, width), BF16) for r in back_rows],
        scratch_shapes=[pltpu.VMEM((tokens - tokens // 16, tokens), BF16)]
        + [pltpu.VMEM((step * 2 * tokens, 128), F32)] * 6,
        compiler_params=pltpu.CompilerParams(vmem_limit_bytes=VMEM_LIMIT),
        name="attention_backward",
    )(query, key, value, attn, grad, lse, *received, *after)


def finish_kernel(gk_ref, gv_ref, near, three, four, ok_ref, ov_ref, k_s, v_s):
    heads = range(gk_ref.shape[1] // DH)
    tokens = gk_ref.shape[0]
    state = {}
    base = 0
    for ref, rows in ((four, BLK // 4), (three, BLK // 2), (near, BLK), (None, 2 * BLK)):
        for h in heads:
            for part, scr in ((0, k_s), (1, v_s)):
                total = state.get((h, part))
                if ref is not None:
                    own = ref[pl.ds(part * rows, rows), pl.ds(h * DH, DH)].astype(F32)
                    total = own if total is None else total + own
                state[h, part] = expand_two(scr, h * 2 * tokens + base, total * 0.5)
        base += 2 * rows
    for h in heads:
        here = pl.ds(h * DH, DH)
        ok_ref[:, here] = gk_ref[:, here] + state[h, 0]
        ov_ref[:, here] = gv_ref[:, here] + state[h, 1]


def finish_call(grad_k, grad_v, near, three, four):
    tokens, width = grad_k.shape
    step = 2 * DH
    spec = pl.BlockSpec((tokens, step), lambda h: (0, h))
    rows = (2 * BLK, BLK, BLK // 2)
    extra = [pl.BlockSpec((r, step), lambda h: (0, h)) for r in rows]
    full = jax.ShapeDtypeStruct((tokens, width), F32)
    scratch = pltpu.VMEM((2 * 2 * tokens, DH), F32)
    return pl.pallas_call(
        finish_kernel,
        grid=(width // step,),
        in_specs=[spec, spec] + extra,
        out_specs=[spec, spec],
        out_shape=[full, full],
        scratch_shapes=[scratch, scratch],
        compiler_params=pltpu.CompilerParams(vmem_limit_bytes=VMEM_LIMIT),
        name="add_returned",
    )(grad_k, grad_v, near, three, four)


def chunk_of(refs, number):
    return refs[0][...] if number == 1 else refs[0][...] + refs[1][...]


def split_kernel(core_ref, *refs, pairs, column, extra):
    sources = refs[: sum(pairs)]
    mine_ref, send_ref = refs[sum(pairs) + extra :]
    first = core_ref[0] == 0
    at = 0
    for index, number in enumerate(pairs):
        chunk = chunk_of(sources[at:], number)
        at += number
        width = chunk.shape[1]
        for group in range(width // (2 * column)):
            low = chunk[:, 2 * group * column : (2 * group + 1) * column]
            high = chunk[:, (2 * group + 1) * column : (2 * group + 2) * column]
            here = pl.ds(index * width // 2 + group * column, column)
            mine_ref[:, here] = jnp.where(first, low, high)
            send_ref[:, here] = jnp.where(first, high, low)


def split_call(chunks, core, column, after=()):
    flat = [array for chunk in chunks for array in chunk]
    tokens, width = flat[0].shape
    count = len(chunks)
    rows = 256
    spec = pl.BlockSpec((rows, width), lambda i: (i, 0))
    half = pl.BlockSpec((rows, count * width // 2), lambda i: (i, 0))
    return pl.pallas_call(
        functools.partial(
            split_kernel, pairs=tuple(len(c) for c in chunks), column=column, extra=len(after)
        ),
        grid=(tokens // rows,),
        in_specs=[pl.BlockSpec(memory_space=pltpu.SMEM)]
        + [spec] * len(flat)
        + [pl.BlockSpec(memory_space=pl.ANY)] * len(after),
        out_specs=[half, half],
        out_shape=[jax.ShapeDtypeStruct((tokens, count * width // 2), BF16)] * 2,
        compiler_params=pltpu.CompilerParams(vmem_limit_bytes=VMEM_LIMIT),
        name="split_columns",
    )(core.reshape(1).astype(jnp.int32), *flat, *after)


def grad_kernel(place_ref, *refs, pairs, has_sum):
    total = sum(pairs)
    count = len(pairs)
    sources = refs[:total]
    weights = refs[total : total + count]
    out = refs[-1]
    result = refs[total + count][...] if has_sum else None
    at = 0
    for index, number in enumerate(pairs):
        part = dot_nt(chunk_of(sources[at:], number), weights[index][...])
        result = part if result is None else result + part
        at += number
    out[...] = result.astype(out.dtype)


def grad_call(chunks, out_weight, place, partial_sum, dtype):
    flat = [array for chunk in chunks for array in chunk]
    tokens, width = flat[0].shape
    features = out_weight.shape[0]
    step = 256
    chunk_spec = pl.BlockSpec((tokens, width), lambda i, p: (0, 0))
    out_spec = pl.BlockSpec((tokens, step), lambda i, p: (0, i))
    weight_specs = [
        pl.BlockSpec((step, width), lambda i, p, n=n: (i, p[n])) for n in range(len(chunks))
    ]
    sums = () if partial_sum is None else (partial_sum,)
    return pl.pallas_call(
        functools.partial(
            grad_kernel, pairs=tuple(len(c) for c in chunks), has_sum=partial_sum is not None
        ),
        grid_spec=pltpu.PrefetchScalarGridSpec(
            num_scalar_prefetch=1,
            grid=(features // step,),
            in_specs=[chunk_spec] * len(flat) + weight_specs + [out_spec] * len(sums),
            out_specs=out_spec,
        ),
        out_shape=jax.ShapeDtypeStruct((tokens, features), dtype),
        compiler_params=pltpu.CompilerParams(vmem_limit_bytes=VMEM_LIMIT),
        name="grad_products",
    )(place.astype(jnp.int32), *flat, *[out_weight] * len(chunks), *sums)


def project_kernel(place_ref, attn_ref, left_w, right_w, *refs, has_sum):
    left_out, right_out = refs[-2:]
    left = dot_nn(attn_ref[...], left_w[...])
    right = dot_nn(attn_ref[...], right_w[...])
    if has_sum:
        left = left + refs[0][...].astype(F32)
        right = right + refs[1][...].astype(F32)
    left_out[...] = left.astype(BF16)
    right_out[...] = right.astype(BF16)


def project_call(attn, out_weight, place, sums):
    tokens, width = attn.shape
    features = out_weight.shape[0]
    step = 256
    per = width // step
    spec = pl.BlockSpec((tokens, step), lambda i, p: (0, i))
    return pl.pallas_call(
        functools.partial(project_kernel, has_sum=bool(sums)),
        grid_spec=pltpu.PrefetchScalarGridSpec(
            num_scalar_prefetch=1,
            grid=(per,),
            in_specs=[pl.BlockSpec((tokens, width), lambda i, p: (0, 0))]
            + [pl.BlockSpec((features, step), lambda i, p, n=n: (0, p[n] * per + i)) for n in (0, 1)]
            + [spec] * len(sums),
            out_specs=[spec, spec],
        ),
        out_shape=[jax.ShapeDtypeStruct((tokens, width), BF16)] * 2,
        compiler_params=pltpu.CompilerParams(vmem_limit_bytes=VMEM_LIMIT),
        name="mixed_products",
    )(place.astype(jnp.int32), attn, out_weight, out_weight, *sums)


def mixed_kernel(place_ref, attn_ref, weight_ref, left_ref, right_ref, out_ref):
    total = left_ref[...].astype(F32) + right_ref[...].astype(F32)
    out_ref[...] = dot_nn(attn_ref[...], weight_ref[...]) + total


def mixed_call(attn, out_weight, place, left, right):
    tokens, width = attn.shape
    features = out_weight.shape[0]
    step = 256
    per = width // step
    spec = pl.BlockSpec((tokens, step), lambda i, p: (0, i))
    return pl.pallas_call(
        mixed_kernel,
        grid_spec=pltpu.PrefetchScalarGridSpec(
            num_scalar_prefetch=1,
            grid=(per,),
            in_specs=[
                pl.BlockSpec((tokens, width), lambda i, p: (0, 0)),
                pl.BlockSpec((features, step), lambda i, p: (0, p[0] * per + i)),
                spec,
                spec,
            ],
            out_specs=spec,
        ),
        out_shape=jax.ShapeDtypeStruct((tokens, width), F32),
        compiler_params=pltpu.CompilerParams(vmem_limit_bytes=VMEM_LIMIT),
        name="mixed_last",
    )(place.astype(jnp.int32), attn, out_weight, left, right)


def term_order(chips):
    top = chips // 2
    groups = {(1, 0): [], (1, 1): [], (0, 1): [], (0, 0): []}
    for i in range(chips):
        groups[i & 1, int(i & top != 0)].append(i)
    return [i for key in ((1, 0), (1, 1), (0, 1), (0, 0)) for i in groups[key]]


def term_kernel(
    place_ref, own_ref, other_ref, mine_a, theirs_a, mine_b, theirs_b,
    a_send, a_keep, b_send, b_keep, turned, both, *, chips, first,
):
    step = pl.program_id(0)
    features, tokens = own_ref.shape

    @pl.when(step == 0)
    def _():
        turned[:, pl.ds(0, tokens)] = own_ref[...]
        turned[:, pl.ds(tokens, tokens)] = other_ref[...]

    is_first = place_ref[step] < first

    @pl.when(is_first)
    def _():
        both[pl.ds(0, tokens), :] = mine_a[...]
        both[pl.ds(tokens, tokens), :] = theirs_a[...]

    @pl.when(jnp.logical_not(is_first))
    def _():
        both[pl.ds(0, tokens), :] = mine_b[...]
        both[pl.ds(tokens, tokens), :] = theirs_b[...]

    half = features // 2
    in_a = step < chips // 2
    in_b = jnp.logical_and(step >= chips // 4, step < 3 * chips // 4)
    for start, flag, send, keep in ((0, in_a, a_send, a_keep), (half, in_b, b_send, b_keep)):
        rows = dot_nn(turned[pl.ds(start, half), :], both[...]).astype(BF16)

        @pl.when(flag)
        def _():
            send[0] = rows

        @pl.when(jnp.logical_not(flag))
        def _():
            keep[0] = rows


def term_call(own, other, early, late, place, column):
    features, tokens = own.shape
    chips = place.shape[0]
    half, quarter = chips // 2, chips // 4
    first = early[0].shape[1] // column
    whole = pl.BlockSpec((features, tokens), lambda i, p: (0, 0))
    spec_a = pl.BlockSpec((tokens, column), lambda i, p: (0, jnp.minimum(p[i], first - 1)))
    spec_b = pl.BlockSpec((tokens, column), lambda i, p: (0, jnp.maximum(p[i] - first, 0)))
    shape = (1, features // 2, column)
    outs = [
        pl.BlockSpec(shape, lambda i, p: (jnp.minimum(i, half - 1), 0, 0)),
        pl.BlockSpec(shape, lambda i, p: (jnp.maximum(i - half, 0), 0, 0)),
        pl.BlockSpec(shape, lambda i, p: (jnp.clip(i - quarter, 0, half - 1), 0, 0)),
        pl.BlockSpec(
            shape,
            lambda i, p: (jnp.where(i < 3 * quarter, jnp.minimum(i, quarter - 1), i - half), 0, 0),
        ),
    ]
    return pl.pallas_call(
        functools.partial(term_kernel, chips=chips, first=first),
        grid_spec=pltpu.PrefetchScalarGridSpec(
            num_scalar_prefetch=1,
            grid=(chips,),
            in_specs=[whole, whole, spec_a, spec_a, spec_b, spec_b],
            out_specs=outs,
            scratch_shapes=[
                pltpu.VMEM((features, 2 * tokens), BF16),
                pltpu.VMEM((2 * tokens, column), BF16),
            ],
        ),
        out_shape=[jax.ShapeDtypeStruct((half, features // 2, column), BF16)] * 4,
        compiler_params=pltpu.CompilerParams(vmem_limit_bytes=VMEM_LIMIT),
        name="weight_terms",
    )(place, own, other, *early, *late)


def total_kernel(top_a, top_b, bottom_a, bottom_b, out):
    half = top_a.shape[0]
    out[pl.ds(0, half), :] = top_a[...].astype(F32) + top_b[...].astype(F32)
    out[pl.ds(half, half), :] = bottom_a[...].astype(F32) + bottom_b[...].astype(F32)


def total_call(top, bottom):
    rows, column = top[0].shape
    return pl.pallas_call(
        total_kernel,
        out_shape=jax.ShapeDtypeStruct((2 * rows, column), F32),
        compiler_params=pltpu.CompilerParams(vmem_limit_bytes=VMEM_LIMIT),
        name="weight_total",
    )(*top, *bottom)


def halve(sent, kept, bits):
    for n, bit in enumerate(bits):
        arrived = swap(sent[1], "ctx", 2 * bit)
        names = [i ^ bit for i in sent[0]]
        if n + 1 == len(bits):
            return kept[1][0], arrived[0]

        def added(flag):
            here = [i for i in kept[0] if (i & bits[n + 1] != 0) == flag]
            parts = [
                kept[1][kept[0].index(i)].astype(F32) + arrived[names.index(i)].astype(F32)
                for i in here
            ]
            return here, jnp.stack([p.astype(BF16) for p in parts])

        sent, kept = added(True), added(False)


def swap(value, axis, mask):
    return lax.ppermute(value, axis, [(i, i ^ mask) for i in range(lax.axis_size(axis))])


def per_device(query, key, value, out_weight, cotangent):
    tokens, width = query.shape
    model = out_weight.shape[1]
    count = lax.axis_size("head")
    ctx_count = lax.axis_size("ctx")
    column = model // ctx_count
    me = lax.axis_index("ctx")
    z = lax.axis_index("head")

    right, left = cotangent, cotangent
    from_left, from_right = [None], [None]
    for step in range(1, count):
        right = lax.ppermute(right, "head", [(i, i + 1) for i in range(step - 1, count - 1)])
        left = lax.ppermute(left, "head", [(i, i - 1) for i in range(1, count - step + 1)])
        from_left.append(right)
        from_right.append(left)

    near, three, four = pool_call(key, value)
    three = swap(three, "ctx", 2)
    four_a = swap(four, "ctx", 4)
    four_b = swap(four, "ctx", 6)
    near = swap(lower_call(near, three, four_a, four_b), "ctx", 1)
    received = (near, three, four_a, four_b)

    attn, turned, lse, tops = forward_call(query, key, value, received)
    turned_other = swap(turned, "ctx", 1)

    def chunk(*distances):
        return jnp.stack([lax.rem(z + d + count, count) for d in distances])

    sums = ()
    summed = []
    for step in range(1, count):
        left, right = project_call(attn, out_weight, chunk(step, -step), sums)
        left = lax.ppermute(left, "head", [(i, i - 1) for i in range(count - step, count)])
        right = lax.ppermute(right, "head", [(i, i + 1) for i in range(0, step)])
        sums = (left, right)
        summed.append(sums)
    mixed = mixed_call(attn, out_weight, chunk(0), *sums)

    core = me % 2
    early = [s for s in range(count) if s not in (1, count - 1)]
    late = sorted({1, count - 1})
    grad_attn = None
    columns = []
    for group in (early, late):
        chunks = [(cotangent,) if s == 0 else (from_left[s], from_right[count - s]) for s in group]
        mine, send = split_call(chunks, core, column, after=() if group is early else summed[0])
        columns.append((mine, swap(send, "ctx", 1)))
        dtype = F32 if group is early else BF16
        grad_attn = grad_call(chunks, out_weight, chunk(*[-s for s in group]), grad_attn, dtype)

    chips = ctx_count // 2
    per_chunk = chips // count
    slots = {s: n for n, s in enumerate(early + late)}
    slot = jnp.array([slots[s] for s in range(count)], jnp.int32)
    order = term_order(chips)
    chip = jnp.bitwise_xor(me // 2, jnp.array(order, jnp.int32))
    place = slot[lax.rem(z - chip // per_chunk + count, count)] * per_chunk + chip % per_chunk
    terms = term_call(turned, turned_other, *columns, place.astype(jnp.int32), column)
    half, quarter = chips // 2, chips // 4
    bits = [1 << n for n in range(chips.bit_length() - 1)]
    top = halve((order[:half], terms[0]), (order[half:], terms[1]), bits)
    bottom = halve(
        (order[quarter : 3 * quarter], terms[2]),
        (order[:quarter] + order[3 * quarter :], terms[3]),
        bits[::-1],
    )
    weight_grad = total_call(top, bottom)

    outs = backward_call(query, key, value, attn, grad_attn, lse, received, after=terms)
    grad_q, grad_k, grad_v, far, keep, four = outs
    far = swap(far, "ctx", 1)
    third = BLK + BLK // 2
    back = swap((keep.astype(F32) + far[2 * BLK : 2 * BLK + third]).astype(BF16), "ctx", 2)
    four = four.astype(F32) + far[2 * BLK + third :] + back[BLK:]
    four = swap(four.astype(BF16), "ctx", 4)
    grad_k, grad_v = finish_call(grad_k, grad_v, far, back, four)

    level_max = jnp.transpose(tops[:, :LEVELS, 0])
    mask = 1
    while mask < ctx_count:
        level_max = jnp.maximum(level_max, swap(level_max, "ctx", mask))
        mask *= 2
    return mixed, grad_q, grad_k, grad_v, weight_grad, level_max


def solution(mesh):
    tokens = P("ctx", "head")
    return jax.shard_map(
        per_device,
        mesh=mesh,
        in_specs=(tokens, tokens, tokens, P("head", None), tokens),
        out_specs=(tokens, tokens, tokens, tokens, P("head", "ctx"), P(None, "head")),
        check_vma=False,
    )
```

```python
import functools
import math

import jax
import jax.numpy as jnp
import numpy as np
from jax import lax
from jax.experimental import pallas as pl
from jax.experimental.pallas import tpu as pltpu
from jax.sharding import PartitionSpec as P

DH = 128
BLK = 128
LEVELS = 5
SCALE = DH ** (-0.5)
LOG_TWO = math.log(2.0)
F32 = jnp.float32
BF16 = jnp.bfloat16
VMEM_LIMIT = 20 * 1024 * 1024


OPT = {'fp': True, 'se': True, 'sl': True, 'g': True, 'b': True, 'lm': 1, 'sa': True, 'b3': True, 'bar': True}


def dot_nn(a, b):
    return lax.dot_general(a, b, (((1,), (0,)), ((), ())), preferred_element_type=F32)


def dot_nt(a, b):
    return lax.dot_general(a, b, (((1,), (1,)), ((), ())), preferred_element_type=F32)


def dot_tn(a, b):
    return lax.dot_general(a, b, (((0,), (0,)), ((), ())), preferred_element_type=F32)


def pool_matrix(level, rows, tokens):
    row = lax.broadcasted_iota(jnp.int32, (rows, tokens), 0)
    token = lax.broadcasted_iota(jnp.int32, (rows, tokens), 1)
    return jnp.where(lax.shift_right_logical(token, level) == row, 0.5**level, 0.0).astype(BF16)


def fill_pool(pool, tokens):
    base = 0
    for level in range(1, LEVELS):
        rows = tokens >> level
        pool[pl.ds(base, rows), :] = pool_matrix(level, rows, tokens)
        base += rows


def pool_kernel(k_ref, v_ref, near_ref, three_ref, four_ref):
    tokens = k_ref.shape[0]
    matrix = jnp.concatenate([pool_matrix(l, tokens >> l, tokens) for l in (2, 3, 4)], 0)
    for part, ref in enumerate((k_ref, v_ref)):
        rows = dot_nn(matrix, ref[...]).astype(BF16)
        base = 0
        for level, out in ((2, near_ref), (3, three_ref), (4, four_ref)):
            size = tokens >> level
            out[pl.ds(part * size, size), :] = rows[base : base + size]
            base += size


def pool_call(key, value):
    tokens, width = key.shape
    step = min(512, width)
    spec = pl.BlockSpec((tokens, step), lambda i: (0, i))
    rows = [2 * (tokens >> level) for level in (2, 3, 4)]
    return pl.pallas_call(
        pool_kernel,
        grid=(width // step,),
        in_specs=[spec, spec],
        out_specs=[pl.BlockSpec((r, step), lambda i: (0, i)) for r in rows],
        out_shape=[jax.ShapeDtypeStruct((r, width), BF16) for r in (tokens, *rows[1:])],
        compiler_params=pltpu.CompilerParams(vmem_limit_bytes=VMEM_LIMIT),
        name="pool_keys",
    )(key, value)


def lower_kernel(near_in, three_ref, four_a, four_b, near_out):
    base = 0
    for ref in (three_ref, four_a, four_b):
        near_out[pl.ds(base, ref.shape[0]), :] = ref[...]
        base += ref.shape[0]


def lower_call(near, three, four_a, four_b):
    tokens, width = near.shape
    spec = lambda r: pl.BlockSpec((r.shape[0], width), lambda i: (0, 0))
    return pl.pallas_call(
        lower_kernel,
        grid=(1,),
        in_specs=[pl.BlockSpec(memory_space=pl.ANY), spec(three), spec(four_a), spec(four_b)],
        out_specs=pl.BlockSpec((tokens // 2, width), lambda i: (1, 0)),
        out_shape=jax.ShapeDtypeStruct((tokens, width), BF16),
        input_output_aliases={0: 0},
        compiler_params=pltpu.CompilerParams(vmem_limit_bytes=VMEM_LIMIT),
        name="lower_rows",
    )(near, three, four_a, four_b)


def expand_two(scratch, base, value):
    rows = value.shape[0]
    scratch[pl.ds(base, rows, stride=2), :] = value
    scratch[pl.ds(base + 1, rows, stride=2), :] = value
    return scratch[pl.ds(base, 2 * rows), :]


def partner_rows(near, three, four_a, four_b, columns):
    def cut(ref, base, half):
        return ref[pl.ds(base, half), columns], ref[pl.ds(base + half, half), columns]

    two = BLK
    join = lambda *pairs: tuple(jnp.concatenate(p, 0) for p in zip(*pairs))
    return {
        2: cut(near, 0, two),
        3: join(cut(three, 0, two // 2), cut(near, 2 * two, two // 2)),
        4: join(
            cut(four_a, 0, two // 4),
            cut(four_b, 0, two // 4),
            cut(near, 3 * two, two // 4),
            cut(near, 3 * two + two // 2, two // 4),
        ),
    }


def coarse_slices(tokens):
    base = 0
    found = {}
    for level in range(1, LEVELS):
        rows = tokens >> level
        found[level] = slice(base, base + rows)
        base += rows
    return found


def forward_kernel(
    q_ref, k_ref, v_ref, near, three, four_a, four_b, *rest, extra
):
    attn_ref, turned_ref, lse_ref, top_ref, pool, peak_s, total_s, summed_s = rest[extra:]
    tokens, width = q_ref.shape

    @pl.when(pl.program_id(0) == 0)
    def _():
        fill_pool(pool, tokens)

    q_all = dot_nn(pool[...], q_ref[...]).astype(BF16)
    half = pl.ds(0, tokens // 2)
    k_one = dot_nn(pool[half, :], k_ref[...]).astype(BF16)
    v_one = dot_nn(pool[half, :], v_ref[...]).astype(BF16)
    where = coarse_slices(tokens)
    heads = range(width // DH)
    columns = [pl.ds(h * DH, DH) for h in heads]
    lanes = [slice(h * DH, (h + 1) * DH) for h in heads]
    work = []
    for h in heads:
        partner = partner_rows(near, three, four_a, four_b, columns[h])
        for level in range(LEVELS - 1, -1, -1):
            if level >= 2:
                work.append((h, level, q_all[where[level], lanes[h]], *partner[level]))
            elif level == 1:
                qc, kc, vc = q_all[where[1], lanes[h]], k_one[:, lanes[h]], v_one[:, lanes[h]]
                for b in range(2):
                    mine = slice(b * BLK, (b + 1) * BLK)
                    other = slice((1 - b) * BLK, (2 - b) * BLK)
                    work.append((h, 1, qc[mine], kc[other], vc[other]))
            else:
                for b in range(tokens // (2 * BLK)):
                    both = pl.ds(b * 2 * BLK, 2 * BLK)
                    work.append(
                        (h, 0, q_ref[both, columns[h]], k_ref[both, columns[h]], v_ref[both, columns[h]])
                    )
    scores = [dot_nt(q, k) * SCALE for _, _, q, k, _ in work]
    peaks = [jnp.max(s, axis=-1, keepdims=True) for s in scores]
    weights = [jnp.exp(s - p).astype(BF16) for s, p in zip(scores, peaks)]
    sums = [
        dot_nn(w, jnp.concatenate([item[4], jnp.ones_like(item[4])], 1))
        for w, item in zip(weights, work)
    ]

    def joined(h, level, values):
        return jnp.concatenate([x for x, item in zip(values, work) if item[:2] == (h, level)], 0)

    row = lax.broadcasted_iota(jnp.int32, (8, 128), 0)
    tiles = [jnp.zeros((8, 128), F32) for _ in heads]
    state = {}
    base = 0
    for level in range(LEVELS - 1, -1, -1):
        rows = tokens >> level
        for h in heads:
            peak = joined(h, level, peaks)
            total = joined(h, level, sums)
            tiles[h] = jnp.where(row == level, jnp.max(peak), tiles[h])
            peak = jnp.broadcast_to(peak + level * LOG_TWO, (rows, DH))
            total, summed = total[:, DH:], total[:, :DH]
            if level < LEVELS - 1:
                place = h * 2 * tokens + base
                peak_up, total_up, summed_up = [
                    expand_two(scratch, place, value)
                    for scratch, value in zip((peak_s, total_s, summed_s), state[h])
                ]
                top = jnp.maximum(peak, peak_up)
                mine = jnp.exp(peak - top)
                other = jnp.exp(peak_up - top)
                total = mine * total + other * total_up
                summed = mine * summed + other * summed_up
                peak = top
            state[h] = (peak, total, summed)
        if level < LEVELS - 1:
            base += rows
    for h in heads:
        peak, total, summed = state[h]
        attn = (summed / total).astype(BF16)
        attn_ref[:, columns[h]] = attn
        turned_ref[columns[h], :] = attn.T
        lse_ref[:, columns[h]] = peak + jnp.log(total)
        top_ref[h] = tiles[h]


def forward_call(query, key, value, received, after=(), step=4):
    tokens, width = query.shape
    heads = width // DH
    spec = pl.BlockSpec((tokens, step * DH), lambda h: (0, h))
    others = [pl.BlockSpec((r.shape[0], step * DH), lambda h: (0, h)) for r in received]
    others += [pl.BlockSpec(memory_space=pl.ANY)] * len(after)
    return pl.pallas_call(
        functools.partial(forward_kernel, extra=len(after)),
        grid=(heads // step,),
        in_specs=[spec, spec, spec] + others,
        out_specs=[
            spec,
            pl.BlockSpec((step * DH, tokens), lambda h: (h, 0)),
            spec,
            pl.BlockSpec((step, 8, 128), lambda h: (h, 0, 0)),
        ],
        out_shape=[
            jax.ShapeDtypeStruct((tokens, width), BF16),
            jax.ShapeDtypeStruct((width, tokens), BF16),
            jax.ShapeDtypeStruct((tokens, width), F32),
            jax.ShapeDtypeStruct((heads, 8, 128), F32),
        ],
        scratch_shapes=[
            pltpu.VMEM((tokens - tokens // 16, tokens), BF16),
            pltpu.VMEM((step * 2 * tokens, 128), F32),
            pltpu.VMEM((step * 2 * tokens, 128), F32),
            pltpu.VMEM((step * 2 * tokens, 128), F32),
        ],
        compiler_params=pltpu.CompilerParams(vmem_limit_bytes=VMEM_LIMIT),
        name="attention_forward",
    )(query, key, value, *received, *after)


def backward_kernel(
    q_ref, k_ref, v_ref, attn_ref, grad_ref, lse_ref, near, three, four_a, four_b, *rest, extra
):
    gq_ref, gk_ref, gv_ref, far, keep, four, pool, lse_s, grad_s, scal_s, gq_s, gk_s, gv_s = rest[extra:]
    tokens, width = q_ref.shape

    @pl.when(pl.program_id(0) == 0)
    def _():
        fill_pool(pool, tokens)

    q_all = dot_nn(pool[...], q_ref[...]).astype(BF16)
    half_rows = pl.ds(0, tokens // 2)
    k_one = dot_nn(pool[half_rows, :], k_ref[...]).astype(BF16)
    v_one = dot_nn(pool[half_rows, :], v_ref[...]).astype(BF16)
    where = coarse_slices(tokens)
    heads = range(width // DH)
    columns = [pl.ds(h * DH, DH) for h in heads]
    lanes = [slice(h * DH, (h + 1) * DH) for h in heads]
    scalars = []
    for h in heads:
        grad_f = grad_ref[:, columns[h]].astype(F32)
        scalar = jnp.sum(grad_f * attn_ref[:, columns[h]].astype(F32), axis=-1, keepdims=True)
        scalars.append(scalar)
        first = pl.ds(h * 2 * tokens, tokens)
        lse_s[first, :] = lse_ref[:, columns[h]]
        scal_s[first, :] = jnp.broadcast_to(scalar, (tokens, 128))
        grad_s[first, :] = grad_f
    places = {}
    base = 0
    rows = tokens
    for level in range(1, LEVELS):
        half = rows // 2
        for h in heads:
            start = h * 2 * tokens + base
            even = pl.ds(start, half, stride=2)
            odd = pl.ds(start + 1, half, stride=2)
            lse_even, lse_odd = lse_s[even, :], lse_s[odd, :]
            least = jnp.minimum(lse_even, lse_odd)
            factor_even = jnp.exp(least - lse_even)
            factor_odd = jnp.exp(least - lse_odd)
            summed = factor_even * grad_s[even, :] + factor_odd * grad_s[odd, :]
            summed_scalar = factor_even * scal_s[even, :] + factor_odd * scal_s[odd, :]
            if level < LEVELS - 1:
                nxt = pl.ds(start + rows, half)
                lse_s[nxt, :] = least
                grad_s[nxt, :] = summed
                scal_s[nxt, :] = summed_scalar
            places[h, level] = (least, summed.astype(BF16), summed_scalar)
        base += rows
        rows = half
    work = []
    for h in heads:
        partner = partner_rows(near, three, four_a, four_b, columns[h])
        for level in range(LEVELS - 1, -1, -1):
            if level >= 2:
                work.append(
                    (h, level, q_all[where[level], lanes[h]], *partner[level], *places[h, level])
                )
            elif level == 1:
                low, gr, sc = places[h, 1]
                qc, kc, vc = q_all[where[1], lanes[h]], k_one[:, lanes[h]], v_one[:, lanes[h]]
                for b in range(2):
                    mine = slice(b * BLK, (b + 1) * BLK)
                    other = slice((1 - b) * BLK, (2 - b) * BLK)
                    work.append((h, 1, qc[mine], kc[other], vc[other], low[mine], gr[mine], sc[mine]))
            else:
                for b in range(tokens // (2 * BLK)):
                    both = pl.ds(b * 2 * BLK, 2 * BLK)
                    part = slice(b * 2 * BLK, (b + 1) * 2 * BLK)
                    low = lse_ref[both, columns[h]]
                    work.append((
                        h, 0, q_ref[both, columns[h]], k_ref[both, columns[h]], v_ref[both, columns[h]],
                        jnp.concatenate([low, low], 1), grad_ref[both, columns[h]], scalars[h][part],
                    ))
    scores = [dot_nt(item[2], item[3]) for item in work]
    grads = [dot_nt(item[6], item[4]) for item in work]
    weights = [
        jnp.exp(s * SCALE + (item[1] * LOG_TWO - item[5])) for s, item in zip(scores, work)
    ]
    grad_scores = [
        (w * (g - item[7])).astype(BF16) for w, g, item in zip(weights, grads, work)
    ]
    weights = [w.astype(BF16) for w in weights]
    parts_q = [dot_nn(s, item[3]) * SCALE for s, item in zip(grad_scores, work)]
    parts_k = [dot_tn(s, item[2]) * SCALE for s, item in zip(grad_scores, work)]
    parts_v = [dot_tn(w, item[6]) for w, item in zip(weights, work)]
    found = {}
    for item, *parts in zip(work, parts_q, parts_k, parts_v):
        found.setdefault(item[:2], []).append(parts)
    state = {}
    up = 0
    for level in range(LEVELS - 1, -1, -1):
        rows = tokens >> level
        for h in heads:
            parts = found[h, level]
            if level >= 2:
                part_q, part_k, part_v = parts[0]
                part_k = part_k.astype(BF16)
                part_v = part_v.astype(BF16)
                outs = {
                    2: ((far, 0),),
                    3: ((keep, 0), (far, 2 * BLK)),
                    4: ((four, 0), (keep, BLK), (far, 3 * BLK + BLK // 2), (far, 3 * BLK)),
                }[level]
                piece = BLK // len(outs)
                for i, (out, at) in enumerate(outs):
                    out[pl.ds(at, piece), columns[h]] = part_k[i * piece : (i + 1) * piece]
                    out[pl.ds(at + piece, piece), columns[h]] = part_v[i * piece : (i + 1) * piece]
            elif level == 1:
                part_q = jnp.concatenate([parts[0][0], parts[1][0]], 0)
                part_k = jnp.concatenate([parts[1][1], parts[0][1]], 0)
                part_v = jnp.concatenate([parts[1][2], parts[0][2]], 0)
                coarse_k = expand_two(gk_s, h * tokens, part_k * 0.5)
                coarse_v = expand_two(gv_s, h * tokens, part_v * 0.5)
                state[h, "k"], state[h, "v"] = coarse_k, coarse_v
            if level == 0:
                for b, (part_q, part_k, part_v) in enumerate(parts):
                    both = slice(b * 2 * BLK, (b + 1) * 2 * BLK)
                    here = pl.ds(b * 2 * BLK, 2 * BLK)
                    gq_ref[here, columns[h]] = part_q + state[h, "q"][both]
                    gk_ref[here, columns[h]] = (part_k + state[h, "k"][both]).astype(BF16)
                    gv_ref[here, columns[h]] = (part_v + state[h, "v"][both]).astype(BF16)
            else:
                grad_q = part_q if level == LEVELS - 1 else part_q + state[h, "q"]
                state[h, "q"] = expand_two(gq_s, h * 2 * tokens + up, grad_q * 0.5)
        up += 2 * rows


def backward_call(query, key, value, attn, grad, lse, received, after=(), step=2):
    tokens, width = query.shape
    steps = width // DH // step
    spec = pl.BlockSpec((tokens, step * DH), lambda h: (0, h))
    others = [pl.BlockSpec((r.shape[0], step * DH), lambda h: (0, h)) for r in received]
    others += [pl.BlockSpec(memory_space=pl.ANY)] * len(after)
    full = jax.ShapeDtypeStruct((tokens, width), F32)
    back_rows = (tokens, BLK + BLK // 2, BLK // 2)
    outs = [pl.BlockSpec((r, step * DH), lambda h: (0, h)) for r in back_rows]
    return pl.pallas_call(
        functools.partial(backward_kernel, extra=len(after)),
        grid=(steps,),
        in_specs=[spec] * 6 + others,
        out_specs=[spec] * 3 + outs,
        out_shape=[full] + [jax.ShapeDtypeStruct((tokens, width), BF16)] * 2
        + [jax.ShapeDtypeStruct((r, width), BF16) for r in back_rows],
        scratch_shapes=[pltpu.VMEM((tokens - tokens // 16, tokens), BF16)]
        + [pltpu.VMEM((step * 2 * tokens, 128), F32)] * 6,
        compiler_params=pltpu.CompilerParams(vmem_limit_bytes=VMEM_LIMIT),
        name="attention_backward",
    )(query, key, value, attn, grad, lse, *received, *after)


def finish_kernel(gk_ref, gv_ref, near, three, four, ok_ref, ov_ref, k_s, v_s):
    heads = range(gk_ref.shape[1] // DH)
    tokens = gk_ref.shape[0]
    state = {}
    base = 0
    for ref, rows in ((four, BLK // 4), (three, BLK // 2), (near, BLK), (None, 2 * BLK)):
        for h in heads:
            for part, scr in ((0, k_s), (1, v_s)):
                total = state.get((h, part))
                if ref is not None:
                    own = ref[pl.ds(part * rows, rows), pl.ds(h * DH, DH)].astype(F32)
                    total = own if total is None else total + own
                state[h, part] = expand_two(scr, h * 2 * tokens + base, total * 0.5)
        base += 2 * rows
    for h in heads:
        here = pl.ds(h * DH, DH)
        ok_ref[:, here] = gk_ref[:, here].astype(F32) + state[h, 0]
        ov_ref[:, here] = gv_ref[:, here].astype(F32) + state[h, 1]


def finish_call(grad_k, grad_v, near, three, four):
    tokens, width = grad_k.shape
    step = 2 * DH
    spec = pl.BlockSpec((tokens, step), lambda h: (0, h))
    rows = (2 * BLK, BLK, BLK // 2)
    extra = [pl.BlockSpec((r, step), lambda h: (0, h)) for r in rows]
    full = jax.ShapeDtypeStruct((tokens, width), F32)
    scratch = pltpu.VMEM((2 * 2 * tokens, DH), F32)
    return pl.pallas_call(
        finish_kernel,
        grid=(width // step,),
        in_specs=[spec, spec] + extra,
        out_specs=[spec, spec],
        out_shape=[full, full],
        scratch_shapes=[scratch, scratch],
        compiler_params=pltpu.CompilerParams(vmem_limit_bytes=VMEM_LIMIT),
        name="add_returned",
    )(grad_k, grad_v, near, three, four)


def chunk_of(refs, number):
    return refs[0][...] if number == 1 else refs[0][...] + refs[1][...]


def split_kernel(core_ref, *refs, pairs, column, extra):
    sources = refs[: sum(pairs)]
    mine_ref, send_ref = refs[sum(pairs) + extra :]
    first = core_ref[0] == 0
    at = 0
    for index, number in enumerate(pairs):
        chunk = chunk_of(sources[at:], number)
        at += number
        width = chunk.shape[1]
        for group in range(width // (2 * column)):
            low = chunk[:, 2 * group * column : (2 * group + 1) * column]
            high = chunk[:, (2 * group + 1) * column : (2 * group + 2) * column]
            here = pl.ds(index * width // 2 + group * column, column)
            mine_ref[:, here] = jnp.where(first, low, high)
            send_ref[:, here] = jnp.where(first, high, low)


def split_call(chunks, core, column, after=()):
    flat = [array for chunk in chunks for array in chunk]
    tokens, width = flat[0].shape
    count = len(chunks)
    rows = 256
    spec = pl.BlockSpec((rows, width), lambda i: (i, 0))
    half = pl.BlockSpec((rows, count * width // 2), lambda i: (i, 0))
    return pl.pallas_call(
        functools.partial(
            split_kernel, pairs=tuple(len(c) for c in chunks), column=column, extra=len(after)
        ),
        grid=(tokens // rows,),
        in_specs=[pl.BlockSpec(memory_space=pltpu.SMEM)]
        + [spec] * len(flat)
        + [pl.BlockSpec(memory_space=pl.ANY)] * len(after),
        out_specs=[half, half],
        out_shape=[jax.ShapeDtypeStruct((tokens, count * width // 2), BF16)] * 2,
        compiler_params=pltpu.CompilerParams(vmem_limit_bytes=VMEM_LIMIT),
        name="split_columns",
    )(core.reshape(1).astype(jnp.int32), *flat, *after)


def grad_kernel(place_ref, *refs, pairs, has_sum):
    total = sum(pairs)
    count = len(pairs)
    sources = refs[:total]
    weights = refs[total : total + count]
    out = refs[-1]
    result = refs[total + count][...] if has_sum else None
    at = 0
    for index, number in enumerate(pairs):
        part = dot_nt(chunk_of(sources[at:], number), weights[index][...])
        result = part if result is None else result + part
        at += number
    out[...] = result.astype(out.dtype)


def grad_call(chunks, out_weight, place, distances, partial_sum, dtype, after=()):
    flat = [array for chunk in chunks for array in chunk]
    tokens, width = flat[0].shape
    features = out_weight.shape[0]
    step = min(512, features)
    chunk_spec = pl.BlockSpec((tokens, width), lambda i, p: (0, 0))
    out_spec = pl.BlockSpec((tokens, step), lambda i, p: (0, i))
    weight_specs = [
        pl.BlockSpec((step, width), lambda i, p, d=d: (i, p[d])) for d in distances
    ]
    sums = () if partial_sum is None else (partial_sum,)
    return pl.pallas_call(
        functools.partial(
            grad_kernel, pairs=tuple(len(c) for c in chunks), has_sum=partial_sum is not None
        ),
        grid_spec=pltpu.PrefetchScalarGridSpec(
            num_scalar_prefetch=1,
            grid=(features // step,),
            in_specs=[chunk_spec] * len(flat)
            + weight_specs
            + [out_spec] * len(sums)
            + [pl.BlockSpec(memory_space=pl.ANY)] * len(after),
            out_specs=out_spec,
        ),
        out_shape=jax.ShapeDtypeStruct((tokens, features), dtype),
        compiler_params=pltpu.CompilerParams(vmem_limit_bytes=VMEM_LIMIT),
        name="grad_products",
    )(place, *flat, *[out_weight] * len(chunks), *sums, *after)


def product_kernel(place_ref, attn_ref, *refs, count):
    for weight, out in zip(refs[:count], refs[-count:]):
        out[...] = dot_nn(attn_ref[...], weight[...]).astype(out.dtype)


def product_call(attn, out_weight, place, count, after=()):
    tokens, width = attn.shape
    features = out_weight.shape[0]
    step = min(256, width)
    per = width // step
    spec = pl.BlockSpec((tokens, step), lambda i, p: (0, i))
    return pl.pallas_call(
        functools.partial(product_kernel, count=count),
        grid_spec=pltpu.PrefetchScalarGridSpec(
            num_scalar_prefetch=1,
            grid=(per,),
            in_specs=[pl.BlockSpec((tokens, width), lambda i, p: (0, 0))]
            + [
                pl.BlockSpec((features, step), lambda i, p, d=d: (0, p[d] * per + i))
                for d in range(count)
            ]
            + [pl.BlockSpec(memory_space=pl.ANY)] * len(after),
            out_specs=[spec] * count,
        ),
        out_shape=[jax.ShapeDtypeStruct((tokens, width), BF16)] * count,
        compiler_params=pltpu.CompilerParams(vmem_limit_bytes=VMEM_LIMIT),
        name="mixed_products",
    )(place, attn, *[out_weight] * count, *after)


def add_kernel(left_a, left_b, right_a, right_b, left, right):
    left[...] = (left_a[...].astype(F32) + left_b[...].astype(F32)).astype(left.dtype)
    right[...] = (right_a[...].astype(F32) + right_b[...].astype(F32)).astype(right.dtype)


def add_call(left, right):
    tokens, width = left[0].shape
    spec = pl.BlockSpec((tokens // 2, width), lambda i: (i, 0))
    return pl.pallas_call(
        add_kernel,
        grid=(2,),
        in_specs=[spec] * 4,
        out_specs=[spec] * 2,
        out_shape=[jax.ShapeDtypeStruct((tokens, width), BF16)] * 2,
        compiler_params=pltpu.CompilerParams(vmem_limit_bytes=VMEM_LIMIT),
        name="mixed_add",
    )(*left, *right)


def last_kernel(own, left, right, out):
    out[...] = own[...].astype(F32) + left[...].astype(F32) + right[...].astype(F32)


def last_call(own, left, right):
    tokens, width = own.shape
    spec = pl.BlockSpec((tokens // 4, width), lambda i: (i, 0))
    return pl.pallas_call(
        last_kernel,
        grid=(4,),
        in_specs=[spec] * 3,
        out_specs=spec,
        out_shape=jax.ShapeDtypeStruct((tokens, width), F32),
        compiler_params=pltpu.CompilerParams(vmem_limit_bytes=VMEM_LIMIT),
        name="mixed_last",
    )(own, left, right)


def term_kernel(place_ref, own_ref, other_ref, mine_ref, theirs_ref, out):
    out[0] = (
        dot_nn(own_ref[...], mine_ref[...]) + dot_nn(other_ref[...], theirs_ref[...])
    ).astype(BF16)


def term_call(own, other, mine, theirs, place, column):
    features, tokens = own.shape
    count = mine.shape[1] // column
    rows = features // 2
    whole = pl.BlockSpec((rows, tokens), lambda i, j, p: (j, 0))
    source = pl.BlockSpec((tokens, column), lambda i, j, p: (0, i))
    return pl.pallas_call(
        term_kernel,
        grid_spec=pltpu.PrefetchScalarGridSpec(
            num_scalar_prefetch=1,
            grid=(count, 2),
            in_specs=[whole, whole, source, source],
            out_specs=pl.BlockSpec((1, rows, column), lambda i, j, p: (i, j, 0)),
        ),
        out_shape=jax.ShapeDtypeStruct((count, features, column), BF16),
        compiler_params=pltpu.CompilerParams(vmem_limit_bytes=VMEM_LIMIT),
        name="weight_terms",
    )(place, own, other, mine, theirs)


def late_kernel(place_ref, own_ref, other_ref, mine_ref, theirs_ref, early_ref, *refs, chips, base, first):
    a_send, a_keep, b_send, b_keep = refs[-4:]
    step = pl.program_id(0)
    half = own_ref.shape[0] // 2
    in_a = step < chips // 2
    in_b = jnp.logical_and(step >= chips // 4, step < 3 * chips // 4)
    is_early = place_ref[base + step] < first
    for start, flag, send, keep in ((0, in_a, a_send, a_keep), (half, in_b, b_send, b_keep)):
        here = pl.ds(start, half)

        def store(rows):
            @pl.when(flag)
            def _():
                send[0] = rows

            @pl.when(jnp.logical_not(flag))
            def _():
                keep[0] = rows

        @pl.when(is_early)
        def _():
            store(early_ref[0, here, :])

        @pl.when(jnp.logical_not(is_early))
        def _():
            rows = dot_nn(own_ref[here, :], mine_ref[...]) + dot_nn(
                other_ref[here, :], theirs_ref[...]
            )
            store(rows.astype(BF16))


def late_call(own, other, mine, theirs, early, place, base, chips, column, after):
    features, tokens = own.shape
    first = early.shape[0]
    half, quarter = chips // 2, chips // 4
    whole = pl.BlockSpec((features, tokens), lambda i, p: (0, 0))
    source = pl.BlockSpec((tokens, column), lambda i, p: (0, jnp.maximum(p[base + i] - first, 0)))
    shape = (1, features // 2, column)
    outs = [
        pl.BlockSpec(shape, lambda i, p: (jnp.minimum(i, half - 1), 0, 0)),
        pl.BlockSpec(shape, lambda i, p: (jnp.maximum(i - half, 0), 0, 0)),
        pl.BlockSpec(shape, lambda i, p: (jnp.clip(i - quarter, 0, half - 1), 0, 0)),
        pl.BlockSpec(
            shape,
            lambda i, p: (jnp.where(i < 3 * quarter, jnp.minimum(i, quarter - 1), i - half), 0, 0),
        ),
    ]
    early_spec = pl.BlockSpec(
        (1, features, column), lambda i, p: (jnp.minimum(p[base + i], first - 1), 0, 0)
    )
    return pl.pallas_call(
        functools.partial(late_kernel, chips=chips, base=base, first=first),
        grid_spec=pltpu.PrefetchScalarGridSpec(
            num_scalar_prefetch=1,
            grid=(chips,),
            in_specs=[whole, whole, source, source, early_spec]
            + [pl.BlockSpec(memory_space=pl.ANY)] * len(after),
            out_specs=outs,
        ),
        out_shape=[jax.ShapeDtypeStruct((half, features // 2, column), BF16)] * 4,
        compiler_params=pltpu.CompilerParams(vmem_limit_bytes=VMEM_LIMIT),
        name="weight_terms_late",
    )(place, own, other, mine, theirs, early, *after)


def total_kernel(top_a, top_b, bottom_a, bottom_b, out):
    half = top_a.shape[0]
    out[pl.ds(0, half), :] = top_a[...].astype(F32) + top_b[...].astype(F32)
    out[pl.ds(half, half), :] = bottom_a[...].astype(F32) + bottom_b[...].astype(F32)


def total_call(top, bottom):
    rows, column = top[0].shape
    return pl.pallas_call(
        total_kernel,
        out_shape=jax.ShapeDtypeStruct((2 * rows, column), F32),
        compiler_params=pltpu.CompilerParams(vmem_limit_bytes=VMEM_LIMIT),
        name="weight_total",
    )(*top, *bottom)


def term_order(chips):
    top = chips // 2
    groups = {(1, 0): [], (1, 1): [], (0, 1): [], (0, 0): []}
    for i in range(chips):
        groups[i & 1, int(i & top != 0)].append(i)
    return [i for key in ((1, 0), (1, 1), (0, 1), (0, 0)) for i in groups[key]]


def fold_kernel(*refs, plans):
    at = 0
    out_at = 2 * len(plans)
    for plan in plans:
        kept, arrived = refs[at : at + 2]
        for out, pairs in zip(refs[out_at : out_at + 2], plan):
            for n, (k, m) in enumerate(pairs):
                out[n] = (kept[k].astype(F32) + arrived[m].astype(F32)).astype(BF16)
        at += 2
        out_at += 2


def fold_call(sides):
    plans, operands, names, shapes = [], [], [], []
    for sent, arrived, keep, kept, bit, following in sides:
        source = [i ^ bit for i in sent]
        parts = [[i for i in keep if (i & following != 0) == flag] for flag in (True, False)]
        plans.append([[(keep.index(i), source.index(i)) for i in part] for part in parts])
        operands += [kept, arrived]
        names.append(parts)
        shapes += [jax.ShapeDtypeStruct((len(p), *kept.shape[1:]), BF16) for p in parts]
    outs = pl.pallas_call(
        functools.partial(fold_kernel, plans=plans),
        out_shape=shapes,
        compiler_params=pltpu.CompilerParams(vmem_limit_bytes=VMEM_LIMIT),
        name="fold_terms",
    )(*operands)
    return [(names[n], outs[2 * n : 2 * n + 2]) for n in range(len(sides))]


def top_kernel(tops_ref, *refs):
    refs[-1][...] = tops_ref[...]


def held_back(value, after):
    spec = pl.BlockSpec(value.shape, lambda: (0,) * value.ndim)
    return pl.pallas_call(
        top_kernel,
        in_specs=[spec] + [pl.BlockSpec(memory_space=pl.ANY)] * len(after),
        out_specs=spec,
        out_shape=jax.ShapeDtypeStruct(value.shape, value.dtype),
        name="held_back",
    )(value, *after)


def swap(value, axis, mask):
    return lax.ppermute(value, axis, [(i, i ^ mask) for i in range(lax.axis_size(axis))])


def per_device(query, key, value, out_weight, cotangent):
    tokens, width = query.shape
    model = out_weight.shape[1]
    count = lax.axis_size("head")
    ctx_count = lax.axis_size("ctx")
    column = model // ctx_count
    me = lax.axis_index("ctx")
    z = lax.axis_index("head")

    core = me % 2
    chips = ctx_count // 2
    per_chunk = chips // count
    early = [s for s in range(count) if s not in (1, count - 1)]
    late = sorted({1, count - 1})
    bits = [1 << n for n in range(chips.bit_length() - 1)]
    order = term_order(chips)
    slots = {s: n for n, s in enumerate(early + late)}
    table = np.zeros((count, ctx_count, count + chips), np.int32)
    for i in range(count):
        for j in range(ctx_count):
            table[i, j, :count] = [(i + d) % count for d in range(count)]
            for n, distance in enumerate(order):
                chip = (j // 2) ^ distance
                s = (i - chip // per_chunk) % count
                table[i, j, count + n] = slots[s] * per_chunk + chip % per_chunk
    place = lax.dynamic_slice(jnp.asarray(table), (z, me, 0), (1, 1, count + chips)).reshape(-1)

    from_left, from_right = [cotangent], [cotangent]

    def pass_on(step):
        right, left = from_left[-1], from_right[-1]
        right = lax.ppermute(right, "head", [(i, i + 1) for i in range(step - 1, count - 1)])
        left = lax.ppermute(left, "head", [(i, i - 1) for i in range(1, count - step + 1)])
        from_left.append(right)
        from_right.append(left)

    def send_on(step, left, right):
        return (
            lax.ppermute(left, "head", [(i, i - 1) for i in range(count - step, count)]),
            lax.ppermute(right, "head", [(i, i + 1) for i in range(0, step)]),
        )

    def chunks_of(group):
        return [(cotangent,) if s == 0 else (from_left[s], from_right[count - s]) for s in group]

    back_by = lambda group: tuple(-s % count for s in group)

    pass_on(1)
    if OPT.get("x0"):
        tiny = swap(key[:16, :128], "ctx", 1)
        key_in = lax.optimization_barrier((key, tiny))[0]
    else:
        key_in = key
    near, three, four = pool_call(key_in, value)
    three = swap(three, "ctx", 2)
    four_a = swap(four, "ctx", 4)
    four_b = swap(four, "ctx", 6)
    near = lower_call(near, three, four_a, four_b)
    if OPT.get("bar"):
        near, from_left[1], from_right[1] = lax.optimization_barrier((near, from_left[1], from_right[1]))
    if OPT.get("bar2"):
        lower, from_left[1], from_right[1] = lax.optimization_barrier((near, from_left[1], from_right[1]))
        received_after = (lower,)
    near = swap(near, "ctx", 1)
    if OPT.get("bar3"):
        near, from_left[1], from_right[1] = lax.optimization_barrier((near, from_left[1], from_right[1]))
    received = (near, three, four_a, four_b)

    attn, turned, lse, tops = forward_call(query, key, value, received, after=((place,) if OPT.get("fp") else ()) + ((lower,) if OPT.get("bar2f") else ()) + ((from_left[1], from_right[1]) if OPT.get("f") else ()))
    if OPT.get("barF"):
        attn, from_left[1], from_right[1] = lax.optimization_barrier((attn, from_left[1], from_right[1]))
    pass_on(2)
    turned_other = swap(turned, "ctx", 1)
    lm = OPT.get("lm")
    def lmax(after):
        level_max = jnp.transpose((held_back(tops, after) if after else tops)[:, :LEVELS, 0])
        mask = 1
        while mask < ctx_count:
            level_max = jnp.maximum(level_max, swap(level_max, "ctx", mask))
            mask *= 2
        return level_max
    if lm == 3:
        level_max = lmax((turned_other,))
    if lm == 4:
        level_max = lmax(())
    products = product_call(attn, out_weight, place, count, after=(turned_other,) if OPT.get("p2") else ())
    left, right = send_on(1, products[1], products[count - 1])
    for step in range(3, count):
        pass_on(step)
    chunks = chunks_of(early)
    mine, send = split_call(chunks, core, column, after=(products[1],) if OPT.get("se") else ())
    theirs = swap(send, "ctx", 1)
    grad_attn = grad_call(chunks, out_weight, place, back_by(early), None, F32)
    terms = term_call(turned, turned_other, mine, theirs, place, column)

    chunks = chunks_of(late)
    if lm == 1:
        level_max = lmax((terms, grad_attn))
    first_arrived = (left, right)
    for step in range(2, count - 1):
        sums = add_call((products[step], left), (products[count - step], right))
        left, right = send_on(step, *sums)
    mine, send = split_call(chunks, core, column, after=((terms, grad_attn) if OPT.get("sl") else ()) + ((level_max,) if lm == 1 else ()) + (first_arrived if OPT.get("slr") else ()) + (tuple(sums) if OPT.get("sa") else ()) + ())
    theirs = swap(send, "ctx", 1)
    terms = late_call(turned, turned_other, mine, theirs, terms, place, count, chips, column, sums if OPT.get("t") else ())
    grad_attn = grad_call(
        chunks, out_weight, place, back_by(late), grad_attn, BF16, after=terms if OPT.get("g") else ()
    )
    half, quarter = chips // 2, chips // 4
    first = [swap(terms[0], "ctx", 2 * bits[0]), swap(terms[2], "ctx", 2 * bits[-1])]
    if lm == 2:
        level_max = lmax((terms[0],))
    outs = backward_call(query, key, value, attn, grad_attn, lse, received, after=(tuple(terms) if OPT.get("b") else ()) + ((level_max,) if lm == 2 else ()) + ((left, right) if OPT.get("bl") else ()))

    sums = add_call((products[count - 1], left), (products[1], right))
    if OPT.get("b3"):
        sums, first = lax.optimization_barrier((tuple(sums), first))
    left, right = send_on(count - 1, *sums)
    ways = [bits, bits[::-1]]
    sent = [order[:half], order[quarter : 3 * quarter]]
    held = [order[half:], order[:quarter] + order[3 * quarter :]]
    kept = [terms[1], terms[3]]
    for n in range(len(bits) - 1):
        folded = fold_call(
            [
                (sent[k], first[k], held[k], kept[k], ways[k][n], ways[k][n + 1])
                for k in (0, 1)
            ]
        )
        sent, held = [[f[0][k] for f in folded] for k in (0, 1)]
        kept = [f[1][1] for f in folded]
        first = [swap(f[1][0], "ctx", 2 * ways[k][n + 1]) for k, f in enumerate(folded)]
    top, bottom = [(kept[k][0], first[k][0]) for k in (0, 1)]
    grad_q, grad_k, grad_v, far, keep, four = outs
    far = swap(far, "ctx", 1)
    third = BLK + BLK // 2
    if OPT.get("ret2"):
        sums3 = (keep.astype(F32) + far[2 * BLK : 2 * BLK + third]).astype(BF16)
        sums4 = (four.astype(F32) + far[2 * BLK + third :]).astype(BF16)
        back = swap(sums3[:BLK], "ctx", 2)
        four = (swap(sums4, "ctx", 4), swap(sums3[BLK:], "ctx", 6))
        four = (four[0].astype(F32) + four[1]).astype(BF16)
    else:
      back = swap((keep.astype(F32) + far[2 * BLK : 2 * BLK + third]).astype(BF16), "ctx", 2)
      four = four.astype(F32) + far[2 * BLK + third :] + back[BLK:]
      four = swap(four.astype(BF16), "ctx", 4)
    weight_grad = total_call(top, bottom)
    mixed = last_call(products[0], left, right)
    grad_k, grad_v = finish_call(grad_k, grad_v, far, back, four)

    if lm == 0:
        level_max = lmax((terms[0],))
    return mixed, grad_q, grad_k, grad_v, weight_grad, level_max


def solution(mesh):
    tokens = P("ctx", "head")
    return jax.shard_map(
        per_device,
        mesh=mesh,
        in_specs=(tokens, tokens, tokens, P("head", None), tokens),
        out_specs=(tokens, tokens, tokens, tokens, P("head", "ctx"), P(None, "head")),
        check_vma=False,
    )
```

```python
import functools
import math

import jax
import jax.numpy as jnp
import numpy as np
from jax import lax
from jax.experimental import pallas as pl
from jax.experimental.pallas import tpu as pltpu
from jax.sharding import PartitionSpec as P

DH = 128
BLK = 128
LEVELS = 5
SCALE = DH ** (-0.5)
LOG_TWO = math.log(2.0)
F32 = jnp.float32
BF16 = jnp.bfloat16
VMEM_LIMIT = 20 * 1024 * 1024


def dot_nn(a, b):
    return lax.dot_general(a, b, (((1,), (0,)), ((), ())), preferred_element_type=F32)


def dot_nt(a, b):
    return lax.dot_general(a, b, (((1,), (1,)), ((), ())), preferred_element_type=F32)


def dot_tn(a, b):
    return lax.dot_general(a, b, (((0,), (0,)), ((), ())), preferred_element_type=F32)


def pool_matrix(level, rows, tokens):
    row = lax.broadcasted_iota(jnp.int32, (rows, tokens), 0)
    token = lax.broadcasted_iota(jnp.int32, (rows, tokens), 1)
    return jnp.where(lax.shift_right_logical(token, level) == row, 0.5**level, 0.0).astype(BF16)


def fill_pool(pool, tokens):
    base = 0
    for level in range(1, LEVELS):
        rows = tokens >> level
        pool[pl.ds(base, rows), :] = pool_matrix(level, rows, tokens)
        base += rows


def pool_kernel(k_ref, v_ref, near_ref, three_ref, four_ref):
    tokens = k_ref.shape[0]
    matrix = jnp.concatenate([pool_matrix(l, tokens >> l, tokens) for l in (2, 3, 4)], 0)
    for part, ref in enumerate((k_ref, v_ref)):
        rows = dot_nn(matrix, ref[...]).astype(BF16)
        base = 0
        for level, out in ((2, near_ref), (3, three_ref), (4, four_ref)):
            size = tokens >> level
            out[pl.ds(part * size, size), :] = rows[base : base + size]
            base += size


def pool_call(key, value):
    tokens, width = key.shape
    step = min(512, width)
    spec = pl.BlockSpec((tokens, step), lambda i: (0, i))
    rows = [2 * (tokens >> level) for level in (2, 3, 4)]
    return pl.pallas_call(
        pool_kernel,
        grid=(width // step,),
        in_specs=[spec, spec],
        out_specs=[pl.BlockSpec((r, step), lambda i: (0, i)) for r in rows],
        out_shape=[jax.ShapeDtypeStruct((r, width), BF16) for r in (tokens, *rows[1:])],
        compiler_params=pltpu.CompilerParams(vmem_limit_bytes=VMEM_LIMIT),
        name="pool_keys",
    )(key, value)


def lower_kernel(near_in, three_ref, four_a, four_b, near_out):
    base = 0
    for ref in (three_ref, four_a, four_b):
        near_out[pl.ds(base, ref.shape[0]), :] = ref[...]
        base += ref.shape[0]


def lower_call(near, three, four_a, four_b):
    tokens, width = near.shape
    spec = lambda r: pl.BlockSpec((r.shape[0], width), lambda i: (0, 0))
    return pl.pallas_call(
        lower_kernel,
        grid=(1,),
        in_specs=[pl.BlockSpec(memory_space=pl.ANY), spec(three), spec(four_a), spec(four_b)],
        out_specs=pl.BlockSpec((tokens // 2, width), lambda i: (1, 0)),
        out_shape=jax.ShapeDtypeStruct((tokens, width), BF16),
        input_output_aliases={0: 0},
        compiler_params=pltpu.CompilerParams(vmem_limit_bytes=VMEM_LIMIT),
        name="lower_rows",
    )(near, three, four_a, four_b)


def expand_two(scratch, base, value):
    rows = value.shape[0]
    scratch[pl.ds(base, rows, stride=2), :] = value
    scratch[pl.ds(base + 1, rows, stride=2), :] = value
    return scratch[pl.ds(base, 2 * rows), :]


def partner_rows(near, three, four_a, four_b, columns):
    def cut(ref, base, half):
        return ref[pl.ds(base, half), columns], ref[pl.ds(base + half, half), columns]

    two = BLK
    join = lambda *pairs: tuple(jnp.concatenate(p, 0) for p in zip(*pairs))
    return {
        2: cut(near, 0, two),
        3: join(cut(three, 0, two // 2), cut(near, 2 * two, two // 2)),
        4: join(
            cut(four_a, 0, two // 4),
            cut(four_b, 0, two // 4),
            cut(near, 3 * two, two // 4),
            cut(near, 3 * two + two // 2, two // 4),
        ),
    }


def coarse_slices(tokens):
    base = 0
    found = {}
    for level in range(1, LEVELS):
        rows = tokens >> level
        found[level] = slice(base, base + rows)
        base += rows
    return found


def forward_kernel(
    q_ref, k_ref, v_ref, near, three, four_a, four_b, *rest, extra
):
    attn_ref, turned_ref, lse_ref, top_ref, pool, peak_s, total_s, summed_s = rest[extra:]
    tokens, width = q_ref.shape

    @pl.when(pl.program_id(0) == 0)
    def _():
        fill_pool(pool, tokens)

    q_all = dot_nn(pool[...], q_ref[...]).astype(BF16)
    half = pl.ds(0, tokens // 2)
    k_one = dot_nn(pool[half, :], k_ref[...]).astype(BF16)
    v_one = dot_nn(pool[half, :], v_ref[...]).astype(BF16)
    where = coarse_slices(tokens)
    heads = range(width // DH)
    columns = [pl.ds(h * DH, DH) for h in heads]
    lanes = [slice(h * DH, (h + 1) * DH) for h in heads]
    work = []
    for h in heads:
        partner = partner_rows(near, three, four_a, four_b, columns[h])
        for level in range(LEVELS - 1, -1, -1):
            if level >= 2:
                work.append((h, level, q_all[where[level], lanes[h]], *partner[level]))
            elif level == 1:
                qc, kc, vc = q_all[where[1], lanes[h]], k_one[:, lanes[h]], v_one[:, lanes[h]]
                for b in range(2):
                    mine = slice(b * BLK, (b + 1) * BLK)
                    other = slice((1 - b) * BLK, (2 - b) * BLK)
                    work.append((h, 1, qc[mine], kc[other], vc[other]))
            else:
                for b in range(tokens // (2 * BLK)):
                    both = pl.ds(b * 2 * BLK, 2 * BLK)
                    work.append(
                        (h, 0, q_ref[both, columns[h]], k_ref[both, columns[h]], v_ref[both, columns[h]])
                    )
    scores = [dot_nt(q, k) * SCALE for _, _, q, k, _ in work]
    peaks = [jnp.max(s, axis=-1, keepdims=True) for s in scores]
    weights = [jnp.exp(s - p).astype(BF16) for s, p in zip(scores, peaks)]
    sums = [
        dot_nn(w, jnp.concatenate([item[4], jnp.ones_like(item[4])], 1))
        for w, item in zip(weights, work)
    ]

    def joined(h, level, values):
        return jnp.concatenate([x for x, item in zip(values, work) if item[:2] == (h, level)], 0)

    row = lax.broadcasted_iota(jnp.int32, (8, 128), 0)
    tiles = [jnp.zeros((8, 128), F32) for _ in heads]
    state = {}
    base = 0
    for level in range(LEVELS - 1, -1, -1):
        rows = tokens >> level
        for h in heads:
            peak = joined(h, level, peaks)
            total = joined(h, level, sums)
            tiles[h] = jnp.where(row == level, jnp.max(peak), tiles[h])
            peak = jnp.broadcast_to(peak + level * LOG_TWO, (rows, DH))
            total, summed = total[:, DH:], total[:, :DH]
            if level < LEVELS - 1:
                place = h * 2 * tokens + base
                peak_up, total_up, summed_up = [
                    expand_two(scratch, place, value)
                    for scratch, value in zip((peak_s, total_s, summed_s), state[h])
                ]
                top = jnp.maximum(peak, peak_up)
                mine = jnp.exp(peak - top)
                other = jnp.exp(peak_up - top)
                total = mine * total + other * total_up
                summed = mine * summed + other * summed_up
                peak = top
            state[h] = (peak, total, summed)
        if level < LEVELS - 1:
            base += rows
    for h in heads:
        peak, total, summed = state[h]
        attn = (summed / total).astype(BF16)
        attn_ref[:, columns[h]] = attn
        turned_ref[columns[h], :] = attn.T
        lse_ref[:, columns[h]] = peak + jnp.log(total)
        top_ref[h] = tiles[h]


def forward_call(query, key, value, received, after=(), step=4):
    tokens, width = query.shape
    heads = width // DH
    spec = pl.BlockSpec((tokens, step * DH), lambda h: (0, h))
    others = [pl.BlockSpec((r.shape[0], step * DH), lambda h: (0, h)) for r in received]
    others += [pl.BlockSpec(memory_space=pl.ANY)] * len(after)
    return pl.pallas_call(
        functools.partial(forward_kernel, extra=len(after)),
        grid=(heads // step,),
        in_specs=[spec, spec, spec] + others,
        out_specs=[
            spec,
            pl.BlockSpec((step * DH, tokens), lambda h: (h, 0)),
            spec,
            pl.BlockSpec((step, 8, 128), lambda h: (h, 0, 0)),
        ],
        out_shape=[
            jax.ShapeDtypeStruct((tokens, width), BF16),
            jax.ShapeDtypeStruct((width, tokens), BF16),
            jax.ShapeDtypeStruct((tokens, width), F32),
            jax.ShapeDtypeStruct((heads, 8, 128), F32),
        ],
        scratch_shapes=[
            pltpu.VMEM((tokens - tokens // 16, tokens), BF16),
            pltpu.VMEM((step * 2 * tokens, 128), F32),
            pltpu.VMEM((step * 2 * tokens, 128), F32),
            pltpu.VMEM((step * 2 * tokens, 128), F32),
        ],
        compiler_params=pltpu.CompilerParams(vmem_limit_bytes=VMEM_LIMIT),
        name="attention_forward",
    )(query, key, value, *received, *after)


def backward_kernel(
    q_ref, k_ref, v_ref, attn_ref, grad_ref, lse_ref, near, three, four_a, four_b, *rest, extra
):
    gq_ref, gk_ref, gv_ref, far, keep, four, pool, lse_s, grad_s, scal_s, gq_s, gk_s, gv_s = rest[extra:]
    tokens, width = q_ref.shape

    @pl.when(pl.program_id(0) == 0)
    def _():
        fill_pool(pool, tokens)

    q_all = dot_nn(pool[...], q_ref[...]).astype(BF16)
    half_rows = pl.ds(0, tokens // 2)
    k_one = dot_nn(pool[half_rows, :], k_ref[...]).astype(BF16)
    v_one = dot_nn(pool[half_rows, :], v_ref[...]).astype(BF16)
    where = coarse_slices(tokens)
    heads = range(width // DH)
    columns = [pl.ds(h * DH, DH) for h in heads]
    lanes = [slice(h * DH, (h + 1) * DH) for h in heads]
    scalars = []
    for h in heads:
        grad_f = grad_ref[:, columns[h]].astype(F32)
        scalar = jnp.sum(grad_f * attn_ref[:, columns[h]].astype(F32), axis=-1, keepdims=True)
        scalars.append(scalar)
        first = pl.ds(h * 2 * tokens, tokens)
        lse_s[first, :] = lse_ref[:, columns[h]]
        scal_s[first, :] = jnp.broadcast_to(scalar, (tokens, 128))
        grad_s[first, :] = grad_f
    places = {}
    base = 0
    rows = tokens
    for level in range(1, LEVELS):
        half = rows // 2
        for h in heads:
            start = h * 2 * tokens + base
            even = pl.ds(start, half, stride=2)
            odd = pl.ds(start + 1, half, stride=2)
            lse_even, lse_odd = lse_s[even, :], lse_s[odd, :]
            least = jnp.minimum(lse_even, lse_odd)
            factor_even = jnp.exp(least - lse_even)
            factor_odd = jnp.exp(least - lse_odd)
            summed = factor_even * grad_s[even, :] + factor_odd * grad_s[odd, :]
            summed_scalar = factor_even * scal_s[even, :] + factor_odd * scal_s[odd, :]
            if level < LEVELS - 1:
                nxt = pl.ds(start + rows, half)
                lse_s[nxt, :] = least
                grad_s[nxt, :] = summed
                scal_s[nxt, :] = summed_scalar
            places[h, level] = (least, summed.astype(BF16), summed_scalar)
        base += rows
        rows = half
    work = []
    for h in heads:
        partner = partner_rows(near, three, four_a, four_b, columns[h])
        for level in range(LEVELS - 1, -1, -1):
            if level >= 2:
                work.append(
                    (h, level, q_all[where[level], lanes[h]], *partner[level], *places[h, level])
                )
            elif level == 1:
                low, gr, sc = places[h, 1]
                qc, kc, vc = q_all[where[1], lanes[h]], k_one[:, lanes[h]], v_one[:, lanes[h]]
                for b in range(2):
                    mine = slice(b * BLK, (b + 1) * BLK)
                    other = slice((1 - b) * BLK, (2 - b) * BLK)
                    work.append((h, 1, qc[mine], kc[other], vc[other], low[mine], gr[mine], sc[mine]))
            else:
                for b in range(tokens // (2 * BLK)):
                    both = pl.ds(b * 2 * BLK, 2 * BLK)
                    part = slice(b * 2 * BLK, (b + 1) * 2 * BLK)
                    low = lse_ref[both, columns[h]]
                    work.append((
                        h, 0, q_ref[both, columns[h]], k_ref[both, columns[h]], v_ref[both, columns[h]],
                        jnp.concatenate([low, low], 1), grad_ref[both, columns[h]], scalars[h][part],
                    ))
    scores = [dot_nt(item[2], item[3]) for item in work]
    grads = [dot_nt(item[6], item[4]) for item in work]
    weights = [
        jnp.exp(s * SCALE + (item[1] * LOG_TWO - item[5])) for s, item in zip(scores, work)
    ]
    grad_scores = [
        (w * (g - item[7])).astype(BF16) for w, g, item in zip(weights, grads, work)
    ]
    weights = [w.astype(BF16) for w in weights]
    parts_q = [dot_nn(s, item[3]) * SCALE for s, item in zip(grad_scores, work)]
    parts_k = [dot_tn(s, item[2]) * SCALE for s, item in zip(grad_scores, work)]
    parts_v = [dot_tn(w, item[6]) for w, item in zip(weights, work)]
    found = {}
    for item, *parts in zip(work, parts_q, parts_k, parts_v):
        found.setdefault(item[:2], []).append(parts)
    state = {}
    up = 0
    for level in range(LEVELS - 1, -1, -1):
        rows = tokens >> level
        for h in heads:
            parts = found[h, level]
            if level >= 2:
                part_q, part_k, part_v = parts[0]
                part_k = part_k.astype(BF16)
                part_v = part_v.astype(BF16)
                outs = {
                    2: ((far, 0),),
                    3: ((keep, 0), (far, 2 * BLK)),
                    4: ((four, 0), (keep, BLK), (far, 3 * BLK + BLK // 2), (far, 3 * BLK)),
                }[level]
                piece = BLK // len(outs)
                for i, (out, at) in enumerate(outs):
                    out[pl.ds(at, piece), columns[h]] = part_k[i * piece : (i + 1) * piece]
                    out[pl.ds(at + piece, piece), columns[h]] = part_v[i * piece : (i + 1) * piece]
            elif level == 1:
                part_q = jnp.concatenate([parts[0][0], parts[1][0]], 0)
                part_k = jnp.concatenate([parts[1][1], parts[0][1]], 0)
                part_v = jnp.concatenate([parts[1][2], parts[0][2]], 0)
                coarse_k = expand_two(gk_s, h * tokens, part_k * 0.5)
                coarse_v = expand_two(gv_s, h * tokens, part_v * 0.5)
                state[h, "k"], state[h, "v"] = coarse_k, coarse_v
            if level == 0:
                for b, (part_q, part_k, part_v) in enumerate(parts):
                    both = slice(b * 2 * BLK, (b + 1) * 2 * BLK)
                    here = pl.ds(b * 2 * BLK, 2 * BLK)
                    gq_ref[here, columns[h]] = part_q + state[h, "q"][both]
                    gk_ref[here, columns[h]] = (part_k + state[h, "k"][both]).astype(BF16)
                    gv_ref[here, columns[h]] = (part_v + state[h, "v"][both]).astype(BF16)
            else:
                grad_q = part_q if level == LEVELS - 1 else part_q + state[h, "q"]
                state[h, "q"] = expand_two(gq_s, h * 2 * tokens + up, grad_q * 0.5)
        up += 2 * rows


def backward_call(query, key, value, attn, grad, lse, received, after=(), step=2):
    tokens, width = query.shape
    steps = width // DH // step
    spec = pl.BlockSpec((tokens, step * DH), lambda h: (0, h))
    others = [pl.BlockSpec((r.shape[0], step * DH), lambda h: (0, h)) for r in received]
    others += [pl.BlockSpec(memory_space=pl.ANY)] * len(after)
    full = jax.ShapeDtypeStruct((tokens, width), F32)
    back_rows = (tokens, BLK + BLK // 2, BLK // 2)
    outs = [pl.BlockSpec((r, step * DH), lambda h: (0, h)) for r in back_rows]
    return pl.pallas_call(
        functools.partial(backward_kernel, extra=len(after)),
        grid=(steps,),
        in_specs=[spec] * 6 + others,
        out_specs=[spec] * 3 + outs,
        out_shape=[full] + [jax.ShapeDtypeStruct((tokens, width), BF16)] * 2
        + [jax.ShapeDtypeStruct((r, width), BF16) for r in back_rows],
        scratch_shapes=[pltpu.VMEM((tokens - tokens // 16, tokens), BF16)]
        + [pltpu.VMEM((step * 2 * tokens, 128), F32)] * 6,
        compiler_params=pltpu.CompilerParams(vmem_limit_bytes=VMEM_LIMIT),
        name="attention_backward",
    )(query, key, value, attn, grad, lse, *received, *after)


def finish_kernel(gk_ref, gv_ref, near, three, four, ok_ref, ov_ref, k_s, v_s):
    heads = range(gk_ref.shape[1] // DH)
    tokens = gk_ref.shape[0]
    state = {}
    base = 0
    for ref, rows in ((four, BLK // 4), (three, BLK // 2), (near, BLK), (None, 2 * BLK)):
        for h in heads:
            for part, scr in ((0, k_s), (1, v_s)):
                total = state.get((h, part))
                if ref is not None:
                    own = ref[pl.ds(part * rows, rows), pl.ds(h * DH, DH)].astype(F32)
                    total = own if total is None else total + own
                state[h, part] = expand_two(scr, h * 2 * tokens + base, total * 0.5)
        base += 2 * rows
    for h in heads:
        here = pl.ds(h * DH, DH)
        ok_ref[:, here] = gk_ref[:, here].astype(F32) + state[h, 0]
        ov_ref[:, here] = gv_ref[:, here].astype(F32) + state[h, 1]


def finish_call(grad_k, grad_v, near, three, four):
    tokens, width = grad_k.shape
    step = 2 * DH
    spec = pl.BlockSpec((tokens, step), lambda h: (0, h))
    rows = (2 * BLK, BLK, BLK // 2)
    extra = [pl.BlockSpec((r, step), lambda h: (0, h)) for r in rows]
    full = jax.ShapeDtypeStruct((tokens, width), F32)
    scratch = pltpu.VMEM((2 * 2 * tokens, DH), F32)
    return pl.pallas_call(
        finish_kernel,
        grid=(width // step,),
        in_specs=[spec, spec] + extra,
        out_specs=[spec, spec],
        out_shape=[full, full],
        scratch_shapes=[scratch, scratch],
        compiler_params=pltpu.CompilerParams(vmem_limit_bytes=VMEM_LIMIT),
        name="add_returned",
    )(grad_k, grad_v, near, three, four)


def chunk_of(refs, number):
    return refs[0][...] if number == 1 else refs[0][...] + refs[1][...]


def split_kernel(core_ref, *refs, pairs, column, extra):
    sources = refs[: sum(pairs)]
    mine_ref, send_ref = refs[sum(pairs) + extra :]
    first = core_ref[0] == 0
    at = 0
    for index, number in enumerate(pairs):
        chunk = chunk_of(sources[at:], number)
        at += number
        width = chunk.shape[1]
        for group in range(width // (2 * column)):
            low = chunk[:, 2 * group * column : (2 * group + 1) * column]
            high = chunk[:, (2 * group + 1) * column : (2 * group + 2) * column]
            here = pl.ds(index * width // 2 + group * column, column)
            mine_ref[:, here] = jnp.where(first, low, high)
            send_ref[:, here] = jnp.where(first, high, low)


def split_call(chunks, core, column, after=()):
    flat = [array for chunk in chunks for array in chunk]
    tokens, width = flat[0].shape
    count = len(chunks)
    rows = 256
    spec = pl.BlockSpec((rows, width), lambda i: (i, 0))
    half = pl.BlockSpec((rows, count * width // 2), lambda i: (i, 0))
    return pl.pallas_call(
        functools.partial(
            split_kernel, pairs=tuple(len(c) for c in chunks), column=column, extra=len(after)
        ),
        grid=(tokens // rows,),
        in_specs=[pl.BlockSpec(memory_space=pltpu.SMEM)]
        + [spec] * len(flat)
        + [pl.BlockSpec(memory_space=pl.ANY)] * len(after),
        out_specs=[half, half],
        out_shape=[jax.ShapeDtypeStruct((tokens, count * width // 2), BF16)] * 2,
        compiler_params=pltpu.CompilerParams(vmem_limit_bytes=VMEM_LIMIT),
        name="split_columns",
    )(core.reshape(1).astype(jnp.int32), *flat, *after)


def grad_kernel(place_ref, *refs, pairs, has_sum):
    total = sum(pairs)
    count = len(pairs)
    sources = refs[:total]
    weights = refs[total : total + count]
    out = refs[-1]
    result = refs[total + count][...] if has_sum else None
    at = 0
    for index, number in enumerate(pairs):
        part = dot_nt(chunk_of(sources[at:], number), weights[index][...])
        result = part if result is None else result + part
        at += number
    out[...] = result.astype(out.dtype)


def grad_call(chunks, out_weight, place, distances, partial_sum, dtype, after=()):
    flat = [array for chunk in chunks for array in chunk]
    tokens, width = flat[0].shape
    features = out_weight.shape[0]
    step = min(512, features)
    chunk_spec = pl.BlockSpec((tokens, width), lambda i, p: (0, 0))
    out_spec = pl.BlockSpec((tokens, step), lambda i, p: (0, i))
    weight_specs = [
        pl.BlockSpec((step, width), lambda i, p, d=d: (i, p[d])) for d in distances
    ]
    sums = () if partial_sum is None else (partial_sum,)
    return pl.pallas_call(
        functools.partial(
            grad_kernel, pairs=tuple(len(c) for c in chunks), has_sum=partial_sum is not None
        ),
        grid_spec=pltpu.PrefetchScalarGridSpec(
            num_scalar_prefetch=1,
            grid=(features // step,),
            in_specs=[chunk_spec] * len(flat)
            + weight_specs
            + [out_spec] * len(sums)
            + [pl.BlockSpec(memory_space=pl.ANY)] * len(after),
            out_specs=out_spec,
        ),
        out_shape=jax.ShapeDtypeStruct((tokens, features), dtype),
        compiler_params=pltpu.CompilerParams(vmem_limit_bytes=VMEM_LIMIT),
        name="grad_products",
    )(place, *flat, *[out_weight] * len(chunks), *sums, *after)


def product_kernel(place_ref, attn_ref, *refs, count):
    for weight, out in zip(refs[:count], refs[-count:]):
        out[...] = dot_nn(attn_ref[...], weight[...]).astype(out.dtype)


def product_call(attn, out_weight, place, count, after=()):
    tokens, width = attn.shape
    features = out_weight.shape[0]
    step = min(256, width)
    per = width // step
    spec = pl.BlockSpec((tokens, step), lambda i, p: (0, i))
    return pl.pallas_call(
        functools.partial(product_kernel, count=count),
        grid_spec=pltpu.PrefetchScalarGridSpec(
            num_scalar_prefetch=1,
            grid=(per,),
            in_specs=[pl.BlockSpec((tokens, width), lambda i, p: (0, 0))]
            + [
                pl.BlockSpec((features, step), lambda i, p, d=d: (0, p[d] * per + i))
                for d in range(count)
            ]
            + [pl.BlockSpec(memory_space=pl.ANY)] * len(after),
            out_specs=[spec] * count,
        ),
        out_shape=[jax.ShapeDtypeStruct((tokens, width), BF16)] * count,
        compiler_params=pltpu.CompilerParams(vmem_limit_bytes=VMEM_LIMIT),
        name="mixed_products",
    )(place, attn, *[out_weight] * count, *after)


def add_kernel(*refs):
    half = len(refs) // 3
    for n in range(half):
        a, b = refs[2 * n : 2 * n + 2]
        refs[2 * half + n][...] = (a[...].astype(F32) + b[...].astype(F32)).astype(BF16)


def add_call(*pairs):
    full = [p for p in pairs if p[1] is not None]
    tokens, width = pairs[0][0].shape
    spec = pl.BlockSpec((tokens // 2, width), lambda i: (i, 0))
    sums = pl.pallas_call(
        add_kernel,
        grid=(2,),
        in_specs=[spec] * (2 * len(full)),
        out_specs=[spec] * len(full),
        out_shape=[jax.ShapeDtypeStruct((tokens, width), BF16)] * len(full),
        compiler_params=pltpu.CompilerParams(vmem_limit_bytes=VMEM_LIMIT),
        name="mixed_add",
    )(*[x for p in full for x in p])
    sums = iter(sums)
    return [p[0] if p[1] is None else next(sums) for p in pairs]


def last_kernel(own, left, right, out):
    out[...] = own[...].astype(F32) + left[...].astype(F32) + right[...].astype(F32)


def last_call(own, left, right):
    tokens, width = own.shape
    spec = pl.BlockSpec((tokens // 4, width), lambda i: (i, 0))
    return pl.pallas_call(
        last_kernel,
        grid=(4,),
        in_specs=[spec] * 3,
        out_specs=spec,
        out_shape=jax.ShapeDtypeStruct((tokens, width), F32),
        compiler_params=pltpu.CompilerParams(vmem_limit_bytes=VMEM_LIMIT),
        name="mixed_last",
    )(own, left, right)


def term_kernel(place_ref, own_ref, other_ref, mine_ref, theirs_ref, out):
    out[0] = (
        dot_nn(own_ref[...], mine_ref[...]) + dot_nn(other_ref[...], theirs_ref[...])
    ).astype(BF16)


def term_call(own, other, mine, theirs, place, column):
    features, tokens = own.shape
    count = mine.shape[1] // column
    rows = features // 2
    whole = pl.BlockSpec((rows, tokens), lambda i, j, p: (j, 0))
    source = pl.BlockSpec((tokens, column), lambda i, j, p: (0, i))
    return pl.pallas_call(
        term_kernel,
        grid_spec=pltpu.PrefetchScalarGridSpec(
            num_scalar_prefetch=1,
            grid=(count, 2),
            in_specs=[whole, whole, source, source],
            out_specs=pl.BlockSpec((1, rows, column), lambda i, j, p: (i, j, 0)),
        ),
        out_shape=jax.ShapeDtypeStruct((count, features, column), BF16),
        compiler_params=pltpu.CompilerParams(vmem_limit_bytes=VMEM_LIMIT),
        name="weight_terms",
    )(place, own, other, mine, theirs)


def late_kernel(place_ref, own_ref, other_ref, mine_ref, theirs_ref, early_ref, *refs, chips, base, first):
    a_send, a_keep, b_send, b_keep = refs[-4:]
    step = pl.program_id(0)
    half = own_ref.shape[0] // 2
    in_a = step < chips // 2
    in_b = jnp.logical_and(step >= chips // 4, step < 3 * chips // 4)
    is_early = place_ref[base + step] < first
    for start, flag, send, keep in ((0, in_a, a_send, a_keep), (half, in_b, b_send, b_keep)):
        here = pl.ds(start, half)

        def store(rows):
            @pl.when(flag)
            def _():
                send[0] = rows

            @pl.when(jnp.logical_not(flag))
            def _():
                keep[0] = rows

        @pl.when(is_early)
        def _():
            store(early_ref[0, here, :])

        @pl.when(jnp.logical_not(is_early))
        def _():
            rows = dot_nn(own_ref[here, :], mine_ref[...]) + dot_nn(
                other_ref[here, :], theirs_ref[...]
            )
            store(rows.astype(BF16))


def late_call(own, other, mine, theirs, early, place, base, chips, column, after):
    features, tokens = own.shape
    first = early.shape[0]
    half, quarter = chips // 2, chips // 4
    whole = pl.BlockSpec((features, tokens), lambda i, p: (0, 0))
    source = pl.BlockSpec((tokens, column), lambda i, p: (0, jnp.maximum(p[base + i] - first, 0)))
    shape = (1, features // 2, column)
    outs = [
        pl.BlockSpec(shape, lambda i, p: (jnp.minimum(i, half - 1), 0, 0)),
        pl.BlockSpec(shape, lambda i, p: (jnp.maximum(i - half, 0), 0, 0)),
        pl.BlockSpec(shape, lambda i, p: (jnp.clip(i - quarter, 0, half - 1), 0, 0)),
        pl.BlockSpec(
            shape,
            lambda i, p: (jnp.where(i < 3 * quarter, jnp.minimum(i, quarter - 1), i - half), 0, 0),
        ),
    ]
    early_spec = pl.BlockSpec(
        (1, features, column), lambda i, p: (jnp.minimum(p[base + i], first - 1), 0, 0)
    )
    return pl.pallas_call(
        functools.partial(late_kernel, chips=chips, base=base, first=first),
        grid_spec=pltpu.PrefetchScalarGridSpec(
            num_scalar_prefetch=1,
            grid=(chips,),
            in_specs=[whole, whole, source, source, early_spec]
            + [pl.BlockSpec(memory_space=pl.ANY)] * len(after),
            out_specs=outs,
        ),
        out_shape=[jax.ShapeDtypeStruct((half, features // 2, column), BF16)] * 4,
        compiler_params=pltpu.CompilerParams(vmem_limit_bytes=VMEM_LIMIT),
        name="weight_terms_late",
    )(place, own, other, mine, theirs, early, *after)


def total_kernel(top_a, top_b, bottom_a, bottom_b, out):
    half = top_a.shape[0]
    out[pl.ds(0, half), :] = top_a[...].astype(F32) + top_b[...].astype(F32)
    out[pl.ds(half, half), :] = bottom_a[...].astype(F32) + bottom_b[...].astype(F32)


def total_call(top, bottom):
    rows, column = top[0].shape
    return pl.pallas_call(
        total_kernel,
        out_shape=jax.ShapeDtypeStruct((2 * rows, column), F32),
        compiler_params=pltpu.CompilerParams(vmem_limit_bytes=VMEM_LIMIT),
        name="weight_total",
    )(*top, *bottom)


def term_order(chips):
    top = chips // 2
    groups = {(1, 0): [], (1, 1): [], (0, 1): [], (0, 0): []}
    for i in range(chips):
        groups[i & 1, int(i & top != 0)].append(i)
    return [i for key in ((1, 0), (1, 1), (0, 1), (0, 0)) for i in groups[key]]


def fold_kernel(*refs, plans):
    at = 0
    out_at = 2 * len(plans)
    for plan in plans:
        kept, arrived = refs[at : at + 2]
        for out, pairs in zip(refs[out_at : out_at + 2], plan):
            for n, (k, m) in enumerate(pairs):
                out[n] = (kept[k].astype(F32) + arrived[m].astype(F32)).astype(BF16)
        at += 2
        out_at += 2


def fold_call(sides):
    plans, operands, names, shapes = [], [], [], []
    for sent, arrived, keep, kept, bit, following in sides:
        source = [i ^ bit for i in sent]
        parts = [[i for i in keep if (i & following != 0) == flag] for flag in (True, False)]
        plans.append([[(keep.index(i), source.index(i)) for i in part] for part in parts])
        operands += [kept, arrived]
        names.append(parts)
        shapes += [jax.ShapeDtypeStruct((len(p), *kept.shape[1:]), BF16) for p in parts]
    outs = pl.pallas_call(
        functools.partial(fold_kernel, plans=plans),
        out_shape=shapes,
        compiler_params=pltpu.CompilerParams(vmem_limit_bytes=VMEM_LIMIT),
        name="fold_terms",
    )(*operands)
    return [(names[n], outs[2 * n : 2 * n + 2]) for n in range(len(sides))]


def top_kernel(tops_ref, *refs):
    refs[-1][...] = tops_ref[...]


def held_back(value, after):
    spec = pl.BlockSpec(value.shape, lambda: (0,) * value.ndim)
    return pl.pallas_call(
        top_kernel,
        in_specs=[spec] + [pl.BlockSpec(memory_space=pl.ANY)] * len(after),
        out_specs=spec,
        out_shape=jax.ShapeDtypeStruct(value.shape, value.dtype),
        name="held_back",
    )(value, *after)


def swap(value, axis, mask):
    return lax.ppermute(value, axis, [(i, i ^ mask) for i in range(lax.axis_size(axis))])


def line_pairs(count, rightward, leftward):
    pairs = [(i, i + 1) for i in rightward] + [(i, i - 1) for i in leftward]
    even = [p for p in pairs if min(p) % 2 == 0]
    return even, [p for p in pairs if min(p) % 2 == 1]


def along(value, pairs):
    return lax.ppermute(value, "head", pairs) if pairs else None


def per_device(query, key, value, out_weight, cotangent):
    tokens, width = query.shape
    model = out_weight.shape[1]
    count = lax.axis_size("head")
    ctx_count = lax.axis_size("ctx")
    column = model // ctx_count
    me = lax.axis_index("ctx")
    z = lax.axis_index("head")

    core = me % 2
    chips = ctx_count // 2
    per_chunk = chips // count
    late = sorted({1, count - 1})
    early = [s for s in range(count) if s not in late]
    bits = [1 << n for n in range(chips.bit_length() - 1)]
    order = term_order(chips)
    slots = {s: n for n, s in enumerate(early + late)}
    table = np.zeros((count, ctx_count, count + chips), np.int32)
    for i in range(count):
        sign = 1 if i % 2 else -1
        for j in range(ctx_count):
            table[i, j, :count] = [(i + sign * d) % count for d in range(count)]
            for n, distance in enumerate(order):
                chip = (j // 2) ^ distance
                s = sign * (chip // per_chunk - i) % count
                table[i, j, count + n] = slots[s] * per_chunk + chip % per_chunk
    place = lax.dynamic_slice(jnp.asarray(table), (z, me, 0), (1, 1, count + chips)).reshape(-1)

    even, odd = [cotangent], [cotangent]

    def pass_on(step):
        pairs = line_pairs(count, range(step - 1, count - 1), range(1, count - step + 1))
        even_next = along(odd[-1], pairs[0])
        odd.append(along(even[-1], pairs[1]))
        even.append(even_next)

    def send_on(step, values):
        pairs = line_pairs(count, range(0, step), range(count - step, count))
        return tuple(along(v, p) for v, p in zip(values, pairs))

    def chunks_of(group):
        found = [(cotangent,) if s == 0 else (odd[s], even[count - s]) for s in group]
        return [tuple(c for c in chunk if c is not None) for chunk in found]

    pass_on(1)
    near, three, four = pool_call(key, value)
    three = swap(three, "ctx", 2)
    four_a = swap(four, "ctx", 4)
    four_b = swap(four, "ctx", 6)
    near = lower_call(near, three, four_a, four_b)
    near, even[1], odd[1] = lax.optimization_barrier((near, even[1], odd[1]))
    near = swap(near, "ctx", 1)
    received = (near, three, four_a, four_b)

    pass_on(2)
    attn, turned, lse, tops = forward_call(query, key, value, received, after=(place,))
    turned_other = swap(turned, "ctx", 1)
    products = product_call(attn, out_weight, place, count)
    arrived = send_on(1, (products[1], products[count - 1]))
    for step in range(3, count):
        pass_on(step)

    chunks = chunks_of(early)
    mine, send = split_call(chunks, core, column, after=(products[1],))
    theirs = swap(send, "ctx", 1)
    grad_attn = grad_call(chunks, out_weight, place, early, None, F32)
    terms = term_call(turned, turned_other, mine, theirs, place, column)

    level_max = jnp.transpose(held_back(tops, (terms, grad_attn))[:, :LEVELS, 0])
    mask = 1
    while mask < ctx_count:
        level_max = jnp.maximum(level_max, swap(level_max, "ctx", mask))
        mask *= 2

    def add_products(step, arrived):
        return add_call((products[step], arrived[1]), (products[count - step], arrived[0]))

    for step in range(2, count - 1):
        sums = add_products(step, arrived)
        arrived = send_on(step, sums)
    chunks = chunks_of(late)
    mine, send = split_call(
        chunks, core, column, after=(terms, grad_attn, level_max, *[x for x in sums if x is not None])
    )
    theirs = swap(send, "ctx", 1)
    terms = late_call(turned, turned_other, mine, theirs, terms, place, count, chips, column, ())
    grad_attn = grad_call(
        chunks, out_weight, place, late, grad_attn, BF16, after=tuple(terms)
    )
    half, quarter = chips // 2, chips // 4
    first = [swap(terms[0], "ctx", 2 * bits[0]), swap(terms[2], "ctx", 2 * bits[-1])]
    outs = backward_call(
        query, key, value, attn, grad_attn, lse, received, after=tuple(terms)
    )

    sums = add_products(count - 1, arrived)
    sums, first = lax.optimization_barrier((tuple(sums), first))
    arrived = send_on(count - 1, sums)
    ways = [bits, bits[::-1]]
    sent = [order[:half], order[quarter : 3 * quarter]]
    held = [order[half:], order[:quarter] + order[3 * quarter :]]
    kept = [terms[1], terms[3]]
    for n in range(len(bits) - 1):
        folded = fold_call(
            [
                (sent[k], first[k], held[k], kept[k], ways[k][n], ways[k][n + 1])
                for k in (0, 1)
            ]
        )
        sent, held = [[f[0][k] for f in folded] for k in (0, 1)]
        kept = [f[1][1] for f in folded]
        first = [swap(f[1][0], "ctx", 2 * ways[k][n + 1]) for k, f in enumerate(folded)]
    top, bottom = [(kept[k][0], first[k][0]) for k in (0, 1)]
    weight_grad = total_call(top, bottom)
    mixed = last_call(products[0], *arrived)

    grad_q, grad_k, grad_v, far, keep, four = outs
    far = swap(far, "ctx", 1)
    third = BLK + BLK // 2
    back = swap((keep.astype(F32) + far[2 * BLK : 2 * BLK + third]).astype(BF16), "ctx", 2)
    four = four.astype(F32) + far[2 * BLK + third :] + back[BLK:]
    four = swap(four.astype(BF16), "ctx", 4)
    grad_k, grad_v = finish_call(grad_k, grad_v, far, back, four)
    return mixed, grad_q, grad_k, grad_v, weight_grad, level_max


def solution(mesh):
    tokens = P("ctx", "head")
    return jax.shard_map(
        per_device,
        mesh=mesh,
        in_specs=(tokens, tokens, tokens, P("head", None), tokens),
        out_specs=(tokens, tokens, tokens, tokens, P("head", "ctx"), P(None, "head")),
        check_vma=False,
    )
```

```python
import functools
import math

import jax
import jax.numpy as jnp
import numpy as np
from jax import lax
from jax.experimental import pallas as pl
from jax.experimental.pallas import tpu as pltpu
from jax.sharding import PartitionSpec as P

DH = 128
BLK = 128
LEVELS = 5
SCALE = DH ** (-0.5)
LOG_TWO = math.log(2.0)
F32 = jnp.float32
BF16 = jnp.bfloat16
VMEM_LIMIT = 20 * 1024 * 1024


def dot_nn(a, b):
    return lax.dot_general(a, b, (((1,), (0,)), ((), ())), preferred_element_type=F32)


def dot_nt(a, b):
    return lax.dot_general(a, b, (((1,), (1,)), ((), ())), preferred_element_type=F32)


def dot_tn(a, b):
    return lax.dot_general(a, b, (((0,), (0,)), ((), ())), preferred_element_type=F32)


def pool_matrix(level, rows, tokens):
    row = lax.broadcasted_iota(jnp.int32, (rows, tokens), 0)
    token = lax.broadcasted_iota(jnp.int32, (rows, tokens), 1)
    return jnp.where(lax.shift_right_logical(token, level) == row, 0.5**level, 0.0).astype(BF16)


def fill_pool(pool, tokens):
    base = 0
    for level in range(1, LEVELS):
        rows = tokens >> level
        pool[pl.ds(base, rows), :] = pool_matrix(level, rows, tokens)
        base += rows


def pool_kernel(k_ref, v_ref, near_ref, three_ref, four_ref):
    tokens = k_ref.shape[0]
    matrix = jnp.concatenate([pool_matrix(l, tokens >> l, tokens) for l in (2, 3, 4)], 0)
    for part, ref in enumerate((k_ref, v_ref)):
        rows = dot_nn(matrix, ref[...]).astype(BF16)
        base = 0
        for level, out in ((2, near_ref), (3, three_ref), (4, four_ref)):
            size = tokens >> level
            out[pl.ds(part * size, size), :] = rows[base : base + size]
            base += size


def pool_call(key, value):
    tokens, width = key.shape
    step = min(512, width)
    spec = pl.BlockSpec((tokens, step), lambda i: (0, i))
    rows = [2 * (tokens >> level) for level in (2, 3, 4)]
    return pl.pallas_call(
        pool_kernel,
        grid=(width // step,),
        in_specs=[spec, spec],
        out_specs=[pl.BlockSpec((r, step), lambda i: (0, i)) for r in rows],
        out_shape=[jax.ShapeDtypeStruct((r, width), BF16) for r in (tokens, *rows[1:])],
        compiler_params=pltpu.CompilerParams(vmem_limit_bytes=VMEM_LIMIT),
        name="pool_keys",
    )(key, value)


def lower_kernel(near_in, three_ref, four_a, four_b, near_out):
    base = 0
    for ref in (three_ref, four_a, four_b):
        near_out[pl.ds(base, ref.shape[0]), :] = ref[...]
        base += ref.shape[0]


def lower_call(near, three, four_a, four_b):
    tokens, width = near.shape
    spec = lambda r: pl.BlockSpec((r.shape[0], width), lambda i: (0, 0))
    return pl.pallas_call(
        lower_kernel,
        grid=(1,),
        in_specs=[pl.BlockSpec(memory_space=pl.ANY), spec(three), spec(four_a), spec(four_b)],
        out_specs=pl.BlockSpec((tokens // 2, width), lambda i: (1, 0)),
        out_shape=jax.ShapeDtypeStruct((tokens, width), BF16),
        input_output_aliases={0: 0},
        compiler_params=pltpu.CompilerParams(vmem_limit_bytes=VMEM_LIMIT),
        name="lower_rows",
    )(near, three, four_a, four_b)


def expand_two(scratch, base, value):
    rows = value.shape[0]
    scratch[pl.ds(base, rows, stride=2), :] = value
    scratch[pl.ds(base + 1, rows, stride=2), :] = value
    return scratch[pl.ds(base, 2 * rows), :]


def partner_rows(near, three, four_a, four_b, columns):
    def cut(ref, base, half):
        return ref[pl.ds(base, half), columns], ref[pl.ds(base + half, half), columns]

    two = BLK
    join = lambda *pairs: tuple(jnp.concatenate(p, 0) for p in zip(*pairs))
    return {
        2: cut(near, 0, two),
        3: join(cut(three, 0, two // 2), cut(near, 2 * two, two // 2)),
        4: join(
            cut(four_a, 0, two // 4),
            cut(four_b, 0, two // 4),
            cut(near, 3 * two, two // 4),
            cut(near, 3 * two + two // 2, two // 4),
        ),
    }


def coarse_slices(tokens):
    base = 0
    found = {}
    for level in range(1, LEVELS):
        rows = tokens >> level
        found[level] = slice(base, base + rows)
        base += rows
    return found


def forward_kernel(
    q_ref, k_ref, v_ref, near, three, four_a, four_b, *rest, extra
):
    attn_ref, turned_ref, lse_ref, top_ref, pool, peak_s, total_s, summed_s = rest[extra:]
    tokens, width = q_ref.shape

    @pl.when(pl.program_id(0) == 0)
    def _():
        fill_pool(pool, tokens)

    q_all = dot_nn(pool[...], q_ref[...]).astype(BF16)
    half = pl.ds(0, tokens // 2)
    k_one = dot_nn(pool[half, :], k_ref[...]).astype(BF16)
    v_one = dot_nn(pool[half, :], v_ref[...]).astype(BF16)
    where = coarse_slices(tokens)
    heads = range(width // DH)
    columns = [pl.ds(h * DH, DH) for h in heads]
    lanes = [slice(h * DH, (h + 1) * DH) for h in heads]
    work = []
    for h in heads:
        partner = partner_rows(near, three, four_a, four_b, columns[h])
        for level in range(LEVELS - 1, -1, -1):
            if level >= 2:
                work.append((h, level, q_all[where[level], lanes[h]], *partner[level]))
            elif level == 1:
                qc, kc, vc = q_all[where[1], lanes[h]], k_one[:, lanes[h]], v_one[:, lanes[h]]
                for b in range(2):
                    mine = slice(b * BLK, (b + 1) * BLK)
                    other = slice((1 - b) * BLK, (2 - b) * BLK)
                    work.append((h, 1, qc[mine], kc[other], vc[other]))
            else:
                for b in range(tokens // (2 * BLK)):
                    both = pl.ds(b * 2 * BLK, 2 * BLK)
                    work.append(
                        (h, 0, q_ref[both, columns[h]], k_ref[both, columns[h]], v_ref[both, columns[h]])
                    )
    scores = [dot_nt(q, k) * SCALE for _, _, q, k, _ in work]
    peaks = [jnp.max(s, axis=-1, keepdims=True) for s in scores]
    weights = [jnp.exp(s - p).astype(BF16) for s, p in zip(scores, peaks)]
    sums = [
        dot_nn(w, jnp.concatenate([item[4], jnp.ones_like(item[4])], 1))
        for w, item in zip(weights, work)
    ]

    def joined(h, level, values):
        return jnp.concatenate([x for x, item in zip(values, work) if item[:2] == (h, level)], 0)

    row = lax.broadcasted_iota(jnp.int32, (8, 128), 0)
    tiles = [jnp.zeros((8, 128), F32) for _ in heads]
    state = {}
    base = 0
    for level in range(LEVELS - 1, -1, -1):
        rows = tokens >> level
        for h in heads:
            peak = joined(h, level, peaks)
            total = joined(h, level, sums)
            tiles[h] = jnp.where(row == level, jnp.max(peak), tiles[h])
            peak = jnp.broadcast_to(peak + level * LOG_TWO, (rows, DH))
            total, summed = total[:, DH:], total[:, :DH]
            if level < LEVELS - 1:
                place = h * 2 * tokens + base
                peak_up, total_up, summed_up = [
                    expand_two(scratch, place, value)
                    for scratch, value in zip((peak_s, total_s, summed_s), state[h])
                ]
                top = jnp.maximum(peak, peak_up)
                mine = jnp.exp(peak - top)
                other = jnp.exp(peak_up - top)
                total = mine * total + other * total_up
                summed = mine * summed + other * summed_up
                peak = top
            state[h] = (peak, total, summed)
        if level < LEVELS - 1:
            base += rows
    for h in heads:
        peak, total, summed = state[h]
        attn = (summed / total).astype(BF16)
        attn_ref[:, columns[h]] = attn
        turned_ref[columns[h], :] = attn.T
        lse_ref[:, columns[h]] = peak + jnp.log(total)
        top_ref[h] = tiles[h]


def forward_call(query, key, value, received, after=(), step=4):
    tokens, width = query.shape
    heads = width // DH
    spec = pl.BlockSpec((tokens, step * DH), lambda h: (0, h))
    others = [pl.BlockSpec((r.shape[0], step * DH), lambda h: (0, h)) for r in received]
    others += [pl.BlockSpec(memory_space=pl.ANY)] * len(after)
    return pl.pallas_call(
        functools.partial(forward_kernel, extra=len(after)),
        grid=(heads // step,),
        in_specs=[spec, spec, spec] + others,
        out_specs=[
            spec,
            pl.BlockSpec((step * DH, tokens), lambda h: (h, 0)),
            spec,
            pl.BlockSpec((step, 8, 128), lambda h: (h, 0, 0)),
        ],
        out_shape=[
            jax.ShapeDtypeStruct((tokens, width), BF16),
            jax.ShapeDtypeStruct((width, tokens), BF16),
            jax.ShapeDtypeStruct((tokens, width), F32),
            jax.ShapeDtypeStruct((heads, 8, 128), F32),
        ],
        scratch_shapes=[
            pltpu.VMEM((tokens - tokens // 16, tokens), BF16),
            pltpu.VMEM((step * 2 * tokens, 128), F32),
            pltpu.VMEM((step * 2 * tokens, 128), F32),
            pltpu.VMEM((step * 2 * tokens, 128), F32),
        ],
        compiler_params=pltpu.CompilerParams(vmem_limit_bytes=VMEM_LIMIT),
        name="attention_forward",
    )(query, key, value, *received, *after)


def backward_kernel(
    q_ref, k_ref, v_ref, attn_ref, grad_ref, lse_ref, near, three, four_a, four_b, *rest, extra
):
    gq_ref, gk_ref, gv_ref, far, keep, four, pool, lse_s, grad_s, scal_s, gq_s, gk_s, gv_s = rest[extra:]
    tokens, width = q_ref.shape

    @pl.when(pl.program_id(0) == 0)
    def _():
        fill_pool(pool, tokens)

    q_all = dot_nn(pool[...], q_ref[...]).astype(BF16)
    half_rows = pl.ds(0, tokens // 2)
    k_one = dot_nn(pool[half_rows, :], k_ref[...]).astype(BF16)
    v_one = dot_nn(pool[half_rows, :], v_ref[...]).astype(BF16)
    where = coarse_slices(tokens)
    heads = range(width // DH)
    columns = [pl.ds(h * DH, DH) for h in heads]
    lanes = [slice(h * DH, (h + 1) * DH) for h in heads]
    scalars = []
    for h in heads:
        grad_f = grad_ref[:, columns[h]].astype(F32)
        scalar = jnp.sum(grad_f * attn_ref[:, columns[h]].astype(F32), axis=-1, keepdims=True)
        scalars.append(scalar)
        first = pl.ds(h * 2 * tokens, tokens)
        lse_s[first, :] = lse_ref[:, columns[h]]
        scal_s[first, :] = jnp.broadcast_to(scalar, (tokens, 128))
        grad_s[first, :] = grad_f
    places = {}
    base = 0
    rows = tokens
    for level in range(1, LEVELS):
        half = rows // 2
        for h in heads:
            start = h * 2 * tokens + base
            even = pl.ds(start, half, stride=2)
            odd = pl.ds(start + 1, half, stride=2)
            lse_even, lse_odd = lse_s[even, :], lse_s[odd, :]
            least = jnp.minimum(lse_even, lse_odd)
            factor_even = jnp.exp(least - lse_even)
            factor_odd = jnp.exp(least - lse_odd)
            summed = factor_even * grad_s[even, :] + factor_odd * grad_s[odd, :]
            summed_scalar = factor_even * scal_s[even, :] + factor_odd * scal_s[odd, :]
            if level < LEVELS - 1:
                nxt = pl.ds(start + rows, half)
                lse_s[nxt, :] = least
                grad_s[nxt, :] = summed
                scal_s[nxt, :] = summed_scalar
            places[h, level] = (least, summed.astype(BF16), summed_scalar)
        base += rows
        rows = half
    work = []
    for h in heads:
        partner = partner_rows(near, three, four_a, four_b, columns[h])
        for level in range(LEVELS - 1, -1, -1):
            if level >= 2:
                work.append(
                    (h, level, q_all[where[level], lanes[h]], *partner[level], *places[h, level])
                )
            elif level == 1:
                low, gr, sc = places[h, 1]
                qc, kc, vc = q_all[where[1], lanes[h]], k_one[:, lanes[h]], v_one[:, lanes[h]]
                for b in range(2):
                    mine = slice(b * BLK, (b + 1) * BLK)
                    other = slice((1 - b) * BLK, (2 - b) * BLK)
                    work.append((h, 1, qc[mine], kc[other], vc[other], low[mine], gr[mine], sc[mine]))
            else:
                for b in range(tokens // (2 * BLK)):
                    both = pl.ds(b * 2 * BLK, 2 * BLK)
                    part = slice(b * 2 * BLK, (b + 1) * 2 * BLK)
                    low = lse_ref[both, columns[h]]
                    work.append((
                        h, 0, q_ref[both, columns[h]], k_ref[both, columns[h]], v_ref[both, columns[h]],
                        jnp.concatenate([low, low], 1), grad_ref[both, columns[h]], scalars[h][part],
                    ))
    scores = [dot_nt(item[2], item[3]) for item in work]
    grads = [dot_nt(item[6], item[4]) for item in work]
    weights = [
        jnp.exp(s * SCALE + (item[1] * LOG_TWO - item[5])) for s, item in zip(scores, work)
    ]
    grad_scores = [
        (w * (g - item[7])).astype(BF16) for w, g, item in zip(weights, grads, work)
    ]
    weights = [w.astype(BF16) for w in weights]
    parts_q = [dot_nn(s, item[3]) * SCALE for s, item in zip(grad_scores, work)]
    parts_k = [dot_tn(s, item[2]) * SCALE for s, item in zip(grad_scores, work)]
    parts_v = [dot_tn(w, item[6]) for w, item in zip(weights, work)]
    found = {}
    for item, *parts in zip(work, parts_q, parts_k, parts_v):
        found.setdefault(item[:2], []).append(parts)
    state = {}
    up = 0
    for level in range(LEVELS - 1, -1, -1):
        rows = tokens >> level
        for h in heads:
            parts = found[h, level]
            if level >= 2:
                part_q, part_k, part_v = parts[0]
                part_k = part_k.astype(BF16)
                part_v = part_v.astype(BF16)
                outs = {
                    2: ((far, 0),),
                    3: ((keep, 0), (far, 2 * BLK)),
                    4: ((four, 0), (keep, BLK), (far, 3 * BLK + BLK // 2), (far, 3 * BLK)),
                }[level]
                piece = BLK // len(outs)
                for i, (out, at) in enumerate(outs):
                    out[pl.ds(at, piece), columns[h]] = part_k[i * piece : (i + 1) * piece]
                    out[pl.ds(at + piece, piece), columns[h]] = part_v[i * piece : (i + 1) * piece]
            elif level == 1:
                part_q = jnp.concatenate([parts[0][0], parts[1][0]], 0)
                part_k = jnp.concatenate([parts[1][1], parts[0][1]], 0)
                part_v = jnp.concatenate([parts[1][2], parts[0][2]], 0)
                coarse_k = expand_two(gk_s, h * tokens, part_k * 0.5)
                coarse_v = expand_two(gv_s, h * tokens, part_v * 0.5)
                state[h, "k"], state[h, "v"] = coarse_k, coarse_v
            if level == 0:
                for b, (part_q, part_k, part_v) in enumerate(parts):
                    both = slice(b * 2 * BLK, (b + 1) * 2 * BLK)
                    here = pl.ds(b * 2 * BLK, 2 * BLK)
                    gq_ref[here, columns[h]] = part_q + state[h, "q"][both]
                    gk_ref[here, columns[h]] = (part_k + state[h, "k"][both]).astype(BF16)
                    gv_ref[here, columns[h]] = (part_v + state[h, "v"][both]).astype(BF16)
            else:
                grad_q = part_q if level == LEVELS - 1 else part_q + state[h, "q"]
                state[h, "q"] = expand_two(gq_s, h * 2 * tokens + up, grad_q * 0.5)
        up += 2 * rows


def backward_call(query, key, value, attn, grad, lse, received, after=(), step=2):
    tokens, width = query.shape
    steps = width // DH // step
    spec = pl.BlockSpec((tokens, step * DH), lambda h: (0, h))
    others = [pl.BlockSpec((r.shape[0], step * DH), lambda h: (0, h)) for r in received]
    others += [pl.BlockSpec(memory_space=pl.ANY)] * len(after)
    full = jax.ShapeDtypeStruct((tokens, width), F32)
    back_rows = (tokens, BLK + BLK // 2, BLK // 2)
    outs = [pl.BlockSpec((r, step * DH), lambda h: (0, h)) for r in back_rows]
    return pl.pallas_call(
        functools.partial(backward_kernel, extra=len(after)),
        grid=(steps,),
        in_specs=[spec] * 6 + others,
        out_specs=[spec] * 3 + outs,
        out_shape=[full] + [jax.ShapeDtypeStruct((tokens, width), BF16)] * 2
        + [jax.ShapeDtypeStruct((r, width), BF16) for r in back_rows],
        scratch_shapes=[pltpu.VMEM((tokens - tokens // 16, tokens), BF16)]
        + [pltpu.VMEM((step * 2 * tokens, 128), F32)] * 6,
        compiler_params=pltpu.CompilerParams(vmem_limit_bytes=VMEM_LIMIT),
        name="attention_backward",
    )(query, key, value, attn, grad, lse, *received, *after)


def finish_kernel(gk_ref, gv_ref, near, three, four, ok_ref, ov_ref, k_s, v_s):
    heads = range(gk_ref.shape[1] // DH)
    tokens = gk_ref.shape[0]
    state = {}
    base = 0
    for ref, rows in ((four, BLK // 4), (three, BLK // 2), (near, BLK), (None, 2 * BLK)):
        for h in heads:
            for part, scr in ((0, k_s), (1, v_s)):
                total = state.get((h, part))
                if ref is not None:
                    own = ref[pl.ds(part * rows, rows), pl.ds(h * DH, DH)].astype(F32)
                    total = own if total is None else total + own
                state[h, part] = expand_two(scr, h * 2 * tokens + base, total * 0.5)
        base += 2 * rows
    for h in heads:
        here = pl.ds(h * DH, DH)
        ok_ref[:, here] = gk_ref[:, here].astype(F32) + state[h, 0]
        ov_ref[:, here] = gv_ref[:, here].astype(F32) + state[h, 1]


def finish_call(grad_k, grad_v, near, three, four):
    tokens, width = grad_k.shape
    step = 2 * DH
    spec = pl.BlockSpec((tokens, step), lambda h: (0, h))
    rows = (2 * BLK, BLK, BLK // 2)
    extra = [pl.BlockSpec((r, step), lambda h: (0, h)) for r in rows]
    full = jax.ShapeDtypeStruct((tokens, width), F32)
    scratch = pltpu.VMEM((2 * 2 * tokens, DH), F32)
    return pl.pallas_call(
        finish_kernel,
        grid=(width // step,),
        in_specs=[spec, spec] + extra,
        out_specs=[spec, spec],
        out_shape=[full, full],
        scratch_shapes=[scratch, scratch],
        compiler_params=pltpu.CompilerParams(vmem_limit_bytes=VMEM_LIMIT),
        name="add_returned",
    )(grad_k, grad_v, near, three, four)


SUM, PICK = "sum", "pick"


def chunk_of(refs, mode, at_end):
    if mode is None:
        return refs[0][...]
    if mode == SUM:
        return refs[0][...] + refs[1][...]
    return jnp.where(at_end, refs[1][...], refs[0][...])


def used(mode):
    return 1 if mode is None else 2


def split_kernel(place_ref, *refs, modes, column, flags, extra):
    total = sum(used(m) for m in modes)
    sources = refs[:total]
    mine_ref, send_ref = refs[total + extra :]
    at_end = place_ref[flags] == 1
    first = place_ref[flags + 1] == 0
    at = 0
    for index, mode in enumerate(modes):
        chunk = chunk_of(sources[at:], mode, at_end)
        at += used(mode)
        width = chunk.shape[1]
        for group in range(width // (2 * column)):
            low = chunk[:, 2 * group * column : (2 * group + 1) * column]
            high = chunk[:, (2 * group + 1) * column : (2 * group + 2) * column]
            here = pl.ds(index * width // 2 + group * column, column)
            mine_ref[:, here] = jnp.where(first, low, high)
            send_ref[:, here] = jnp.where(first, high, low)


def split_call(chunks, place, flags, column, after=()):
    flat = [array for _, *arrays in chunks for array in arrays]
    tokens, width = flat[0].shape
    count = len(chunks)
    rows = 256
    spec = pl.BlockSpec((rows, width), lambda i: (i, 0))
    half = pl.BlockSpec((rows, count * width // 2), lambda i: (i, 0))
    return pl.pallas_call(
        functools.partial(
            split_kernel,
            modes=tuple(c[0] for c in chunks), column=column, flags=flags, extra=len(after),
        ),
        grid=(tokens // rows,),
        in_specs=[pl.BlockSpec(memory_space=pltpu.SMEM)]
        + [spec] * len(flat)
        + [pl.BlockSpec(memory_space=pl.ANY)] * len(after),
        out_specs=[half, half],
        out_shape=[jax.ShapeDtypeStruct((tokens, count * width // 2), BF16)] * 2,
        compiler_params=pltpu.CompilerParams(vmem_limit_bytes=VMEM_LIMIT),
        name="split_columns",
    )(place, *flat, *after)


def grad_kernel(place_ref, *refs, modes, flags, has_sum):
    total = sum(used(m) for m in modes)
    count = len(modes)
    sources = refs[:total]
    weights = refs[total : total + count]
    out = refs[-1]
    at_end = place_ref[flags] == 1
    result = refs[total + count][...] if has_sum else None
    at = 0
    for index, mode in enumerate(modes):
        part = dot_nt(chunk_of(sources[at:], mode, at_end), weights[index][...])
        result = part if result is None else result + part
        at += used(mode)
    out[...] = result.astype(out.dtype)


def grad_call(chunks, out_weight, place, flags, distances, partial_sum, dtype, after=()):
    flat = [array for _, *arrays in chunks for array in arrays]
    tokens, width = flat[0].shape
    features = out_weight.shape[0]
    step = min(512, features)
    chunk_spec = pl.BlockSpec((tokens, width), lambda i, p: (0, 0))
    out_spec = pl.BlockSpec((tokens, step), lambda i, p: (0, i))
    weight_specs = [
        pl.BlockSpec((step, width), lambda i, p, d=d: (i, p[d])) for d in distances
    ]
    sums = () if partial_sum is None else (partial_sum,)
    return pl.pallas_call(
        functools.partial(
            grad_kernel,
            modes=tuple(c[0] for c in chunks), flags=flags, has_sum=partial_sum is not None,
        ),
        grid_spec=pltpu.PrefetchScalarGridSpec(
            num_scalar_prefetch=1,
            grid=(features // step,),
            in_specs=[chunk_spec] * len(flat)
            + weight_specs
            + [out_spec] * len(sums)
            + [pl.BlockSpec(memory_space=pl.ANY)] * len(after),
            out_specs=out_spec,
        ),
        out_shape=jax.ShapeDtypeStruct((tokens, features), dtype),
        compiler_params=pltpu.CompilerParams(vmem_limit_bytes=VMEM_LIMIT),
        name="grad_products",
    )(place, *flat, *[out_weight] * len(chunks), *sums, *after)


def product_kernel(place_ref, attn_ref, *refs, count):
    for weight, out in zip(refs[:count], refs[-count:]):
        out[...] = dot_nn(attn_ref[...], weight[...]).astype(out.dtype)


def product_call(attn, out_weight, place, count, after=()):
    tokens, width = attn.shape
    features = out_weight.shape[0]
    step = min(256, width)
    per = width // step
    spec = pl.BlockSpec((tokens, step), lambda i, p: (0, i))
    return pl.pallas_call(
        functools.partial(product_kernel, count=count),
        grid_spec=pltpu.PrefetchScalarGridSpec(
            num_scalar_prefetch=1,
            grid=(per,),
            in_specs=[pl.BlockSpec((tokens, width), lambda i, p: (0, 0))]
            + [
                pl.BlockSpec((features, step), lambda i, p, d=d: (0, p[d] * per + i))
                for d in range(count)
            ]
            + [pl.BlockSpec(memory_space=pl.ANY)] * len(after),
            out_specs=[spec] * count,
        ),
        out_shape=[jax.ShapeDtypeStruct((tokens, width), BF16)] * count,
        compiler_params=pltpu.CompilerParams(vmem_limit_bytes=VMEM_LIMIT),
        name="mixed_products",
    )(place, attn, *[out_weight] * count, *after)


def add_kernel(*refs):
    half = len(refs) // 3
    for n in range(half):
        a, b = refs[2 * n : 2 * n + 2]
        refs[2 * half + n][...] = (a[...].astype(F32) + b[...].astype(F32)).astype(BF16)


def add_call(*pairs):
    full = [p for p in pairs if p[1] is not None]
    tokens, width = pairs[0][0].shape
    spec = pl.BlockSpec((tokens // 2, width), lambda i: (i, 0))
    sums = pl.pallas_call(
        add_kernel,
        grid=(2,),
        in_specs=[spec] * (2 * len(full)),
        out_specs=[spec] * len(full),
        out_shape=[jax.ShapeDtypeStruct((tokens, width), BF16)] * len(full),
        compiler_params=pltpu.CompilerParams(vmem_limit_bytes=VMEM_LIMIT),
        name="mixed_add",
    )(*[x for p in full for x in p])
    sums = iter(sums)
    return [p[0] if p[1] is None else next(sums) for p in pairs]


def last_kernel(own, left, right, out):
    out[...] = own[...].astype(F32) + left[...].astype(F32) + right[...].astype(F32)


def last_call(own, left, right):
    tokens, width = own.shape
    spec = pl.BlockSpec((tokens // 4, width), lambda i: (i, 0))
    return pl.pallas_call(
        last_kernel,
        grid=(4,),
        in_specs=[spec] * 3,
        out_specs=spec,
        out_shape=jax.ShapeDtypeStruct((tokens, width), F32),
        compiler_params=pltpu.CompilerParams(vmem_limit_bytes=VMEM_LIMIT),
        name="mixed_last",
    )(own, left, right)


def term_kernel(own_ref, other_ref, mine_ref, theirs_ref, *refs):
    refs[-1][0] = (
        dot_nn(own_ref[...], mine_ref[...]) + dot_nn(other_ref[...], theirs_ref[...])
    ).astype(BF16)


def term_call(own, other, mine, theirs, column, after):
    features, tokens = own.shape
    count = mine.shape[1] // column
    whole = pl.BlockSpec((features, tokens), lambda i: (0, 0))
    source = pl.BlockSpec((tokens, column), lambda i: (0, i))
    return pl.pallas_call(
        term_kernel,
        grid=(count,),
        in_specs=[whole, whole, source, source] + [pl.BlockSpec(memory_space=pl.ANY)] * len(after),
        out_specs=pl.BlockSpec((1, features, column), lambda i: (i, 0, 0)),
        out_shape=jax.ShapeDtypeStruct((count, features, column), BF16),
        compiler_params=pltpu.CompilerParams(vmem_limit_bytes=VMEM_LIMIT),
        name="weight_terms",
    )(own, other, mine, theirs, *after)


def late_kernel(place_ref, own_ref, other_ref, mine_ref, theirs_ref, early_ref, *refs, chips, base, first):
    a_send, a_keep, b_send, b_keep = refs[-4:]
    step = pl.program_id(0)
    half = own_ref.shape[0] // 2
    in_a = step < chips // 2
    in_b = jnp.logical_and(step >= chips // 4, step < 3 * chips // 4)
    is_early = place_ref[base + step] < first
    for start, flag, send, keep in ((0, in_a, a_send, a_keep), (half, in_b, b_send, b_keep)):
        here = pl.ds(start, half)

        def store(rows):
            @pl.when(flag)
            def _():
                send[0] = rows

            @pl.when(jnp.logical_not(flag))
            def _():
                keep[0] = rows

        @pl.when(is_early)
        def _():
            store(early_ref[0, here, :])

        @pl.when(jnp.logical_not(is_early))
        def _():
            rows = dot_nn(own_ref[here, :], mine_ref[...]) + dot_nn(
                other_ref[here, :], theirs_ref[...]
            )
            store(rows.astype(BF16))


def late_call(own, other, mine, theirs, early, place, base, chips, column, after):
    features, tokens = own.shape
    first = early.shape[0]
    half, quarter = chips // 2, chips // 4
    whole = pl.BlockSpec((features, tokens), lambda i, p: (0, 0))
    source = pl.BlockSpec((tokens, column), lambda i, p: (0, jnp.maximum(p[base + i] - first, 0)))
    shape = (1, features // 2, column)
    outs = [
        pl.BlockSpec(shape, lambda i, p: (jnp.minimum(i, half - 1), 0, 0)),
        pl.BlockSpec(shape, lambda i, p: (jnp.maximum(i - half, 0), 0, 0)),
        pl.BlockSpec(shape, lambda i, p: (jnp.clip(i - quarter, 0, half - 1), 0, 0)),
        pl.BlockSpec(
            shape,
            lambda i, p: (jnp.where(i < 3 * quarter, jnp.minimum(i, quarter - 1), i - half), 0, 0),
        ),
    ]
    early_spec = pl.BlockSpec(
        (1, features, column), lambda i, p: (jnp.minimum(p[base + i], first - 1), 0, 0)
    )
    return pl.pallas_call(
        functools.partial(late_kernel, chips=chips, base=base, first=first),
        grid_spec=pltpu.PrefetchScalarGridSpec(
            num_scalar_prefetch=1,
            grid=(chips,),
            in_specs=[whole, whole, source, source, early_spec]
            + [pl.BlockSpec(memory_space=pl.ANY)] * len(after),
            out_specs=outs,
        ),
        out_shape=[jax.ShapeDtypeStruct((half, features // 2, column), BF16)] * 4,
        compiler_params=pltpu.CompilerParams(vmem_limit_bytes=VMEM_LIMIT),
        name="weight_terms_late",
    )(place, own, other, mine, theirs, early, *after)


def total_kernel(top_a, top_b, bottom_a, bottom_b, out):
    half = top_a.shape[0]
    out[pl.ds(0, half), :] = top_a[...].astype(F32) + top_b[...].astype(F32)
    out[pl.ds(half, half), :] = bottom_a[...].astype(F32) + bottom_b[...].astype(F32)


def total_call(top, bottom):
    rows, column = top[0].shape
    return pl.pallas_call(
        total_kernel,
        out_shape=jax.ShapeDtypeStruct((2 * rows, column), F32),
        compiler_params=pltpu.CompilerParams(vmem_limit_bytes=VMEM_LIMIT),
        name="weight_total",
    )(*top, *bottom)


def term_order(chips):
    top = chips // 2
    groups = {(1, 0): [], (1, 1): [], (0, 1): [], (0, 0): []}
    for i in range(chips):
        groups[i & 1, int(i & top != 0)].append(i)
    return [i for key in ((1, 0), (1, 1), (0, 1), (0, 0)) for i in groups[key]]


def fold_kernel(*refs, plans):
    at = 0
    out_at = 2 * len(plans)
    for plan in plans:
        kept, arrived = refs[at : at + 2]
        for out, pairs in zip(refs[out_at : out_at + 2], plan):
            for n, (k, m) in enumerate(pairs):
                out[n] = (kept[k].astype(F32) + arrived[m].astype(F32)).astype(BF16)
        at += 2
        out_at += 2


def fold_call(sides):
    plans, operands, names, shapes = [], [], [], []
    for sent, arrived, keep, kept, bit, following in sides:
        source = [i ^ bit for i in sent]
        parts = [[i for i in keep if (i & following != 0) == flag] for flag in (True, False)]
        plans.append([[(keep.index(i), source.index(i)) for i in part] for part in parts])
        operands += [kept, arrived]
        names.append(parts)
        shapes += [jax.ShapeDtypeStruct((len(p), *kept.shape[1:]), BF16) for p in parts]
    outs = pl.pallas_call(
        functools.partial(fold_kernel, plans=plans),
        out_shape=shapes,
        compiler_params=pltpu.CompilerParams(vmem_limit_bytes=VMEM_LIMIT),
        name="fold_terms",
    )(*operands)
    return [(names[n], outs[2 * n : 2 * n + 2]) for n in range(len(sides))]


def swap(value, axis, mask):
    return lax.ppermute(value, axis, [(i, i ^ mask) for i in range(lax.axis_size(axis))])


def line_pairs(count, rightward, leftward):
    pairs = [(i, i + 1) for i in rightward] + [(i, i - 1) for i in leftward]
    even = [p for p in pairs if min(p) % 2 == 0]
    return even, [p for p in pairs if min(p) % 2 == 1]


def along(value, pairs):
    return lax.ppermute(value, "head", pairs) if pairs else None


def per_device(query, key, value, out_weight, cotangent):
    tokens, width = query.shape
    model = out_weight.shape[1]
    count = lax.axis_size("head")
    ctx_count = lax.axis_size("ctx")
    column = model // ctx_count
    me = lax.axis_index("ctx")
    z = lax.axis_index("head")

    chips = ctx_count // 2
    per_chunk = chips // count
    early = [s for s in range(count) if s != 1]
    late = [1]
    grad_early = [s for s in early if s != count - 1]
    grad_late = sorted({1, count - 1})
    bits = [1 << n for n in range(chips.bit_length() - 1)]
    order = term_order(chips)
    slots = {s: n for n, s in enumerate(early + late)}
    flags = count + chips
    table = np.zeros((count, ctx_count, flags + 2), np.int32)
    for i in range(count):
        sign = 1 if i % 2 else -1
        for j in range(ctx_count):
            table[i, j, flags:] = (int(i in (0, count - 1)), j % 2)
            table[i, j, :count] = [(i + sign * d) % count for d in range(count)]
            for n, distance in enumerate(order):
                chip = (j // 2) ^ distance
                s = sign * (chip // per_chunk - i) % count
                table[i, j, count + n] = slots[s] * per_chunk + chip % per_chunk
    place = lax.dynamic_slice(jnp.asarray(table), (z, me, 0), (1, 1, flags + 2)).reshape(-1)

    even, odd = [cotangent], [cotangent]

    def pass_on(step):
        pairs = line_pairs(count, range(step - 1, count - 1), range(1, count - step + 1))
        even_next = along(odd[-1], pairs[0])
        odd.append(along(even[-1], pairs[1]))
        even.append(even_next)

    def send_on(step, values):
        pairs = line_pairs(count, range(0, step), range(count - step, count))
        return tuple(along(v, p) for v, p in zip(values, pairs))

    def chunk(s):
        if s == 0:
            return None, cotangent
        if s == 1:
            return PICK, odd[1], joint
        if s == count - 1:
            return None, even[1]
        return SUM, odd[s], even[count - s]

    pass_on(1)
    near, three, four = pool_call(key, value)
    three = swap(three, "ctx", 2)
    four_a = swap(four, "ctx", 4)
    four_b = swap(four, "ctx", 6)
    near = lower_call(near, three, four_a, four_b)
    near, even[1], odd[1] = lax.optimization_barrier((near, even[1], odd[1]))
    near = swap(near, "ctx", 1)
    received = (near, three, four_a, four_b)

    pass_on(2)
    attn, turned, lse, tops = forward_call(query, key, value, received, after=(place,))
    turned_other = swap(turned, "ctx", 1)
    products = product_call(attn, out_weight, place, count)
    for step in range(3, count - 1):
        pass_on(step)
    is_end = jnp.logical_or(z == 0, z == count - 1)
    ends = [(0, 1), (1, 0), (count - 2, count - 1), (count - 1, count - 2)]
    ends_in = jnp.where(is_end, products[1], odd[-1])
    joint = along(ends_in, ends)
    arrived = (joint, None)

    mine, send = split_call([chunk(s) for s in early], place, flags, column, after=(ends_in,))
    theirs = swap(send, "ctx", 1)
    grad_attn = grad_call(
        [chunk(s) for s in grad_early], out_weight, place, flags, grad_early, None, F32
    )
    level_max = jnp.transpose(tops[:, :LEVELS, 0])
    level_max = jnp.maximum(level_max, swap(level_max, "ctx", 1))
    terms = term_call(turned, turned_other, mine, theirs, column, (level_max, grad_attn))
    level_max, terms = lax.optimization_barrier((level_max, terms))
    level_max = jnp.maximum(level_max, swap(level_max, "ctx", 2))
    before_split = level_max
    mask = 4
    while mask < ctx_count:
        level_max = jnp.maximum(level_max, swap(level_max, "ctx", mask))
        mask *= 2

    def add_products(step, arrived):
        return add_call((products[step], arrived[1]), (products[count - step], arrived[0]))

    for step in range(2, count - 1):
        sums = add_products(step, arrived)
        arrived = send_on(step, sums)
    mine, send = split_call(
        [chunk(s) for s in late], place, flags, column, after=(terms, grad_attn, before_split, *[x for x in sums if x is not None])
    )
    theirs = swap(send, "ctx", 1)
    terms = late_call(turned, turned_other, mine, theirs, terms, place, count, chips, column, (level_max,))
    grad_attn = grad_call(
        [chunk(s) for s in grad_late], out_weight, place, flags, grad_late, grad_attn, BF16,
        after=tuple(terms),
    )
    half, quarter = chips // 2, chips // 4
    first = [swap(terms[0], "ctx", 2 * bits[0]), swap(terms[2], "ctx", 2 * bits[-1])]
    outs = backward_call(
        query, key, value, attn, grad_attn, lse, received, after=tuple(terms)
    )

    sums = add_products(count - 1, arrived)
    sums, first = lax.optimization_barrier((tuple(sums), first))
    arrived = send_on(count - 1, sums)
    ways = [bits, bits[::-1]]
    sent = [order[:half], order[quarter : 3 * quarter]]
    held = [order[half:], order[:quarter] + order[3 * quarter :]]
    kept = [terms[1], terms[3]]
    for n in range(len(bits) - 1):
        folded = fold_call(
            [
                (sent[k], first[k], held[k], kept[k], ways[k][n], ways[k][n + 1])
                for k in (0, 1)
            ]
        )
        sent, held = [[f[0][k] for f in folded] for k in (0, 1)]
        kept = [f[1][1] for f in folded]
        first = [swap(f[1][0], "ctx", 2 * ways[k][n + 1]) for k, f in enumerate(folded)]
    top, bottom = [(kept[k][0], first[k][0]) for k in (0, 1)]
    weight_grad = total_call(top, bottom)
    mixed = last_call(products[0], *arrived)

    grad_q, grad_k, grad_v, far, keep, four = outs
    far = swap(far, "ctx", 1)
    third = BLK + BLK // 2
    back = swap((keep.astype(F32) + far[2 * BLK : 2 * BLK + third]).astype(BF16), "ctx", 2)
    four = four.astype(F32) + far[2 * BLK + third :] + back[BLK:]
    four = swap(four.astype(BF16), "ctx", 4)
    grad_k, grad_v = finish_call(grad_k, grad_v, far, back, four)
    return mixed, grad_q, grad_k, grad_v, weight_grad, level_max


def solution(mesh):
    tokens = P("ctx", "head")
    return jax.shard_map(
        per_device,
        mesh=mesh,
        in_specs=(tokens, tokens, tokens, P("head", None), tokens),
        out_specs=(tokens, tokens, tokens, tokens, P("head", "ctx"), P(None, "head")),
        check_vma=False,
    )
```

```python
import functools
import math

import jax
import jax.numpy as jnp
import numpy as np
from jax import lax
from jax.experimental import pallas as pl
from jax.experimental.pallas import tpu as pltpu
from jax.sharding import PartitionSpec as P

DH = 128
BLK = 128
LEVELS = 5
SCALE = DH ** (-0.5)
LOG_TWO = math.log(2.0)
F32 = jnp.float32
BF16 = jnp.bfloat16
VMEM_LIMIT = 20 * 1024 * 1024


def dot_nn(a, b):
    return lax.dot_general(a, b, (((1,), (0,)), ((), ())), preferred_element_type=F32)


def dot_nt(a, b):
    return lax.dot_general(a, b, (((1,), (1,)), ((), ())), preferred_element_type=F32)


def dot_tn(a, b):
    return lax.dot_general(a, b, (((0,), (0,)), ((), ())), preferred_element_type=F32)


def pool_matrix(level, rows, tokens):
    row = lax.broadcasted_iota(jnp.int32, (rows, tokens), 0)
    token = lax.broadcasted_iota(jnp.int32, (rows, tokens), 1)
    return jnp.where(lax.shift_right_logical(token, level) == row, 0.5**level, 0.0).astype(BF16)


def fill_pool(pool, tokens):
    base = 0
    for level in range(1, LEVELS):
        rows = tokens >> level
        pool[pl.ds(base, rows), :] = pool_matrix(level, rows, tokens)
        base += rows


def pool_kernel(k_ref, v_ref, near_ref, three_ref, four_ref):
    tokens = k_ref.shape[0]
    matrix = jnp.concatenate([pool_matrix(l, tokens >> l, tokens) for l in (2, 3, 4)], 0)
    for part, ref in enumerate((k_ref, v_ref)):
        rows = dot_nn(matrix, ref[...]).astype(BF16)
        base = 0
        for level, out in ((2, near_ref), (3, three_ref), (4, four_ref)):
            size = tokens >> level
            out[pl.ds(part * size, size), :] = rows[base : base + size]
            base += size


def pool_call(key, value):
    tokens, width = key.shape
    step = min(512, width)
    spec = pl.BlockSpec((tokens, step), lambda i: (0, i))
    rows = [2 * (tokens >> level) for level in (2, 3, 4)]
    return pl.pallas_call(
        pool_kernel,
        grid=(width // step,),
        in_specs=[spec, spec],
        out_specs=[pl.BlockSpec((r, step), lambda i: (0, i)) for r in rows],
        out_shape=[jax.ShapeDtypeStruct((r, width), BF16) for r in (tokens, *rows[1:])],
        compiler_params=pltpu.CompilerParams(vmem_limit_bytes=VMEM_LIMIT),
        name="pool_keys",
    )(key, value)


def lower_kernel(near_in, three_ref, four_a, four_b, near_out):
    base = 0
    for ref in (three_ref, four_a, four_b):
        near_out[pl.ds(base, ref.shape[0]), :] = ref[...]
        base += ref.shape[0]


def lower_call(near, three, four_a, four_b):
    tokens, width = near.shape
    spec = lambda r: pl.BlockSpec((r.shape[0], width), lambda i: (0, 0))
    return pl.pallas_call(
        lower_kernel,
        grid=(1,),
        in_specs=[pl.BlockSpec(memory_space=pl.ANY), spec(three), spec(four_a), spec(four_b)],
        out_specs=pl.BlockSpec((tokens // 2, width), lambda i: (1, 0)),
        out_shape=jax.ShapeDtypeStruct((tokens, width), BF16),
        input_output_aliases={0: 0},
        compiler_params=pltpu.CompilerParams(vmem_limit_bytes=VMEM_LIMIT),
        name="lower_rows",
    )(near, three, four_a, four_b)


def expand_two(scratch, base, value):
    rows = value.shape[0]
    scratch[pl.ds(base, rows, stride=2), :] = value
    scratch[pl.ds(base + 1, rows, stride=2), :] = value
    return scratch[pl.ds(base, 2 * rows), :]


def partner_rows(near, three, four_a, four_b, columns):
    def cut(ref, base, half):
        return ref[pl.ds(base, half), columns], ref[pl.ds(base + half, half), columns]

    two = BLK
    join = lambda *pairs: tuple(jnp.concatenate(p, 0) for p in zip(*pairs))
    return {
        2: cut(near, 0, two),
        3: join(cut(three, 0, two // 2), cut(near, 2 * two, two // 2)),
        4: join(
            cut(four_a, 0, two // 4),
            cut(four_b, 0, two // 4),
            cut(near, 3 * two, two // 4),
            cut(near, 3 * two + two // 2, two // 4),
        ),
    }


def coarse_slices(tokens):
    base = 0
    found = {}
    for level in range(1, LEVELS):
        rows = tokens >> level
        found[level] = slice(base, base + rows)
        base += rows
    return found


def forward_kernel(
    q_ref, k_ref, v_ref, near, three, four_a, four_b, *rest, extra
):
    attn_ref, turned_ref, lse_ref, top_ref, pool, peak_s, total_s, summed_s = rest[extra:]
    tokens, width = q_ref.shape

    @pl.when(pl.program_id(0) == 0)
    def _():
        fill_pool(pool, tokens)

    q_all = dot_nn(pool[...], q_ref[...]).astype(BF16)
    half = pl.ds(0, tokens // 2)
    k_one = dot_nn(pool[half, :], k_ref[...]).astype(BF16)
    v_one = dot_nn(pool[half, :], v_ref[...]).astype(BF16)
    where = coarse_slices(tokens)
    heads = range(width // DH)
    columns = [pl.ds(h * DH, DH) for h in heads]
    lanes = [slice(h * DH, (h + 1) * DH) for h in heads]
    work = []
    for h in heads:
        partner = partner_rows(near, three, four_a, four_b, columns[h])
        for level in range(LEVELS - 1, -1, -1):
            if level >= 2:
                work.append((h, level, q_all[where[level], lanes[h]], *partner[level]))
            elif level == 1:
                qc, kc, vc = q_all[where[1], lanes[h]], k_one[:, lanes[h]], v_one[:, lanes[h]]
                for b in range(2):
                    mine = slice(b * BLK, (b + 1) * BLK)
                    other = slice((1 - b) * BLK, (2 - b) * BLK)
                    work.append((h, 1, qc[mine], kc[other], vc[other]))
            else:
                for b in range(tokens // (2 * BLK)):
                    both = pl.ds(b * 2 * BLK, 2 * BLK)
                    work.append(
                        (h, 0, q_ref[both, columns[h]], k_ref[both, columns[h]], v_ref[both, columns[h]])
                    )
    scores = [dot_nt(q, k) * SCALE for _, _, q, k, _ in work]
    peaks = [jnp.max(s, axis=-1, keepdims=True) for s in scores]
    weights = [jnp.exp(s - p).astype(BF16) for s, p in zip(scores, peaks)]
    sums = [
        dot_nn(w, jnp.concatenate([item[4], jnp.ones_like(item[4])], 1))
        for w, item in zip(weights, work)
    ]

    def joined(h, level, values):
        return jnp.concatenate([x for x, item in zip(values, work) if item[:2] == (h, level)], 0)

    row = lax.broadcasted_iota(jnp.int32, (8, 128), 0)
    tiles = [jnp.zeros((8, 128), F32) for _ in heads]
    state = {}
    base = 0
    for level in range(LEVELS - 1, -1, -1):
        rows = tokens >> level
        for h in heads:
            peak = joined(h, level, peaks)
            total = joined(h, level, sums)
            tiles[h] = jnp.where(row == level, jnp.max(peak), tiles[h])
            peak = jnp.broadcast_to(peak + level * LOG_TWO, (rows, DH))
            total, summed = total[:, DH:], total[:, :DH]
            if level < LEVELS - 1:
                place = h * 2 * tokens + base
                peak_up, total_up, summed_up = [
                    expand_two(scratch, place, value)
                    for scratch, value in zip((peak_s, total_s, summed_s), state[h])
                ]
                top = jnp.maximum(peak, peak_up)
                mine = jnp.exp(peak - top)
                other = jnp.exp(peak_up - top)
                total = mine * total + other * total_up
                summed = mine * summed + other * summed_up
                peak = top
            state[h] = (peak, total, summed)
        if level < LEVELS - 1:
            base += rows
    for h in heads:
        peak, total, summed = state[h]
        attn = (summed / total).astype(BF16)
        attn_ref[:, columns[h]] = attn
        turned_ref[columns[h], :] = attn.T
        lse_ref[:, columns[h]] = peak + jnp.log(total)
        top_ref[h] = tiles[h]


def forward_call(query, key, value, received, after=(), step=4):
    tokens, width = query.shape
    heads = width // DH
    spec = pl.BlockSpec((tokens, step * DH), lambda h: (0, h))
    others = [pl.BlockSpec((r.shape[0], step * DH), lambda h: (0, h)) for r in received]
    others += [pl.BlockSpec(memory_space=pl.ANY)] * len(after)
    return pl.pallas_call(
        functools.partial(forward_kernel, extra=len(after)),
        grid=(heads // step,),
        in_specs=[spec, spec, spec] + others,
        out_specs=[
            spec,
            pl.BlockSpec((step * DH, tokens), lambda h: (h, 0)),
            spec,
            pl.BlockSpec((step, 8, 128), lambda h: (h, 0, 0)),
        ],
        out_shape=[
            jax.ShapeDtypeStruct((tokens, width), BF16),
            jax.ShapeDtypeStruct((width, tokens), BF16),
            jax.ShapeDtypeStruct((tokens, width), F32),
            jax.ShapeDtypeStruct((heads, 8, 128), F32),
        ],
        scratch_shapes=[
            pltpu.VMEM((tokens - tokens // 16, tokens), BF16),
            pltpu.VMEM((step * 2 * tokens, 128), F32),
            pltpu.VMEM((step * 2 * tokens, 128), F32),
            pltpu.VMEM((step * 2 * tokens, 128), F32),
        ],
        compiler_params=pltpu.CompilerParams(vmem_limit_bytes=VMEM_LIMIT),
        name="attention_forward",
    )(query, key, value, *received, *after)


def backward_kernel(
    q_ref, k_ref, v_ref, attn_ref, grad_ref, lse_ref, near, three, four_a, four_b, *rest, extra
):
    gq_ref, gk_ref, gv_ref, far, keep, four, pool, lse_s, grad_s, scal_s, gq_s, gk_s, gv_s = rest[extra:]
    tokens, width = q_ref.shape

    @pl.when(pl.program_id(0) == 0)
    def _():
        fill_pool(pool, tokens)

    q_all = dot_nn(pool[...], q_ref[...]).astype(BF16)
    half_rows = pl.ds(0, tokens // 2)
    k_one = dot_nn(pool[half_rows, :], k_ref[...]).astype(BF16)
    v_one = dot_nn(pool[half_rows, :], v_ref[...]).astype(BF16)
    where = coarse_slices(tokens)
    heads = range(width // DH)
    columns = [pl.ds(h * DH, DH) for h in heads]
    lanes = [slice(h * DH, (h + 1) * DH) for h in heads]
    scalars = []
    for h in heads:
        grad_f = grad_ref[:, columns[h]].astype(F32)
        scalar = jnp.sum(grad_f * attn_ref[:, columns[h]].astype(F32), axis=-1, keepdims=True)
        scalars.append(scalar)
        first = pl.ds(h * 2 * tokens, tokens)
        lse_s[first, :] = lse_ref[:, columns[h]]
        scal_s[first, :] = jnp.broadcast_to(scalar, (tokens, 128))
        grad_s[first, :] = grad_f
    places = {}
    base = 0
    rows = tokens
    for level in range(1, LEVELS):
        half = rows // 2
        for h in heads:
            start = h * 2 * tokens + base
            even = pl.ds(start, half, stride=2)
            odd = pl.ds(start + 1, half, stride=2)
            lse_even, lse_odd = lse_s[even, :], lse_s[odd, :]
            least = jnp.minimum(lse_even, lse_odd)
            factor_even = jnp.exp(least - lse_even)
            factor_odd = jnp.exp(least - lse_odd)
            summed = factor_even * grad_s[even, :] + factor_odd * grad_s[odd, :]
            summed_scalar = factor_even * scal_s[even, :] + factor_odd * scal_s[odd, :]
            if level < LEVELS - 1:
                nxt = pl.ds(start + rows, half)
                lse_s[nxt, :] = least
                grad_s[nxt, :] = summed
                scal_s[nxt, :] = summed_scalar
            places[h, level] = (least, summed.astype(BF16), summed_scalar)
        base += rows
        rows = half
    work = []
    for h in heads:
        partner = partner_rows(near, three, four_a, four_b, columns[h])
        for level in range(LEVELS - 1, -1, -1):
            if level >= 2:
                work.append(
                    (h, level, q_all[where[level], lanes[h]], *partner[level], *places[h, level])
                )
            elif level == 1:
                low, gr, sc = places[h, 1]
                qc, kc, vc = q_all[where[1], lanes[h]], k_one[:, lanes[h]], v_one[:, lanes[h]]
                for b in range(2):
                    mine = slice(b * BLK, (b + 1) * BLK)
                    other = slice((1 - b) * BLK, (2 - b) * BLK)
                    work.append((h, 1, qc[mine], kc[other], vc[other], low[mine], gr[mine], sc[mine]))
            else:
                for b in range(tokens // (2 * BLK)):
                    both = pl.ds(b * 2 * BLK, 2 * BLK)
                    part = slice(b * 2 * BLK, (b + 1) * 2 * BLK)
                    low = lse_ref[both, columns[h]]
                    work.append((
                        h, 0, q_ref[both, columns[h]], k_ref[both, columns[h]], v_ref[both, columns[h]],
                        jnp.concatenate([low, low], 1), grad_ref[both, columns[h]], scalars[h][part],
                    ))
    scores = [dot_nt(item[2], item[3]) for item in work]
    grads = [dot_nt(item[6], item[4]) for item in work]
    weights = [
        jnp.exp(s * SCALE + (item[1] * LOG_TWO - item[5])) for s, item in zip(scores, work)
    ]
    grad_scores = [
        (w * (g - item[7])).astype(BF16) for w, g, item in zip(weights, grads, work)
    ]
    weights = [w.astype(BF16) for w in weights]
    parts_q = [dot_nn(s, item[3]) * SCALE for s, item in zip(grad_scores, work)]
    parts_k = [dot_tn(s, item[2]) * SCALE for s, item in zip(grad_scores, work)]
    parts_v = [dot_tn(w, item[6]) for w, item in zip(weights, work)]
    found = {}
    for item, *parts in zip(work, parts_q, parts_k, parts_v):
        found.setdefault(item[:2], []).append(parts)
    state = {}
    up = 0
    for level in range(LEVELS - 1, -1, -1):
        rows = tokens >> level
        for h in heads:
            parts = found[h, level]
            if level >= 2:
                part_q, part_k, part_v = parts[0]
                part_k = part_k.astype(BF16)
                part_v = part_v.astype(BF16)
                outs = {
                    2: ((far, 0),),
                    3: ((keep, 0), (far, 2 * BLK)),
                    4: ((four, 0), (keep, BLK), (far, 3 * BLK + BLK // 2), (far, 3 * BLK)),
                }[level]
                piece = BLK // len(outs)
                for i, (out, at) in enumerate(outs):
                    out[pl.ds(at, piece), columns[h]] = part_k[i * piece : (i + 1) * piece]
                    out[pl.ds(at + piece, piece), columns[h]] = part_v[i * piece : (i + 1) * piece]
            elif level == 1:
                part_q = jnp.concatenate([parts[0][0], parts[1][0]], 0)
                part_k = jnp.concatenate([parts[1][1], parts[0][1]], 0)
                part_v = jnp.concatenate([parts[1][2], parts[0][2]], 0)
                coarse_k = expand_two(gk_s, h * tokens, part_k * 0.5)
                coarse_v = expand_two(gv_s, h * tokens, part_v * 0.5)
                state[h, "k"], state[h, "v"] = coarse_k, coarse_v
            if level == 0:
                for b, (part_q, part_k, part_v) in enumerate(parts):
                    both = slice(b * 2 * BLK, (b + 1) * 2 * BLK)
                    here = pl.ds(b * 2 * BLK, 2 * BLK)
                    gq_ref[here, columns[h]] = part_q + state[h, "q"][both]
                    gk_ref[here, columns[h]] = (part_k + state[h, "k"][both]).astype(BF16)
                    gv_ref[here, columns[h]] = (part_v + state[h, "v"][both]).astype(BF16)
            else:
                grad_q = part_q if level == LEVELS - 1 else part_q + state[h, "q"]
                state[h, "q"] = expand_two(gq_s, h * 2 * tokens + up, grad_q * 0.5)
        up += 2 * rows


def backward_call(query, key, value, attn, grad, lse, received, after=(), step=2):
    tokens, width = query.shape
    steps = width // DH // step
    spec = pl.BlockSpec((tokens, step * DH), lambda h: (0, h))
    others = [pl.BlockSpec((r.shape[0], step * DH), lambda h: (0, h)) for r in received]
    others += [pl.BlockSpec(memory_space=pl.ANY)] * len(after)
    full = jax.ShapeDtypeStruct((tokens, width), F32)
    back_rows = (tokens, BLK + BLK // 2, BLK // 2)
    outs = [pl.BlockSpec((r, step * DH), lambda h: (0, h)) for r in back_rows]
    return pl.pallas_call(
        functools.partial(backward_kernel, extra=len(after)),
        grid=(steps,),
        in_specs=[spec] * 6 + others,
        out_specs=[spec] * 3 + outs,
        out_shape=[full] + [jax.ShapeDtypeStruct((tokens, width), BF16)] * 2
        + [jax.ShapeDtypeStruct((r, width), BF16) for r in back_rows],
        scratch_shapes=[pltpu.VMEM((tokens - tokens // 16, tokens), BF16)]
        + [pltpu.VMEM((step * 2 * tokens, 128), F32)] * 6,
        compiler_params=pltpu.CompilerParams(vmem_limit_bytes=VMEM_LIMIT),
        name="attention_backward",
    )(query, key, value, attn, grad, lse, *received, *after)


def finish_kernel(gk_ref, gv_ref, near, three, four, ok_ref, ov_ref, k_s, v_s):
    heads = range(gk_ref.shape[1] // DH)
    tokens = gk_ref.shape[0]
    state = {}
    base = 0
    for ref, rows in ((four, BLK // 4), (three, BLK // 2), (near, BLK), (None, 2 * BLK)):
        for h in heads:
            for part, scr in ((0, k_s), (1, v_s)):
                total = state.get((h, part))
                if ref is not None:
                    own = ref[pl.ds(part * rows, rows), pl.ds(h * DH, DH)].astype(F32)
                    total = own if total is None else total + own
                state[h, part] = expand_two(scr, h * 2 * tokens + base, total * 0.5)
        base += 2 * rows
    for h in heads:
        here = pl.ds(h * DH, DH)
        ok_ref[:, here] = gk_ref[:, here].astype(F32) + state[h, 0]
        ov_ref[:, here] = gv_ref[:, here].astype(F32) + state[h, 1]


def finish_call(grad_k, grad_v, near, three, four):
    tokens, width = grad_k.shape
    step = 2 * DH
    spec = pl.BlockSpec((tokens, step), lambda h: (0, h))
    rows = (2 * BLK, BLK, BLK // 2)
    extra = [pl.BlockSpec((r, step), lambda h: (0, h)) for r in rows]
    full = jax.ShapeDtypeStruct((tokens, width), F32)
    scratch = pltpu.VMEM((2 * 2 * tokens, DH), F32)
    return pl.pallas_call(
        finish_kernel,
        grid=(width // step,),
        in_specs=[spec, spec] + extra,
        out_specs=[spec, spec],
        out_shape=[full, full],
        scratch_shapes=[scratch, scratch],
        compiler_params=pltpu.CompilerParams(vmem_limit_bytes=VMEM_LIMIT),
        name="add_returned",
    )(grad_k, grad_v, near, three, four)


SUM, PICK = "sum", "pick"


def chunk_of(refs, mode, at_end):
    if mode is None:
        return refs[0][...]
    if mode == SUM:
        return refs[0][...] + refs[1][...]
    return jnp.where(at_end, refs[1][...], refs[0][...])


def used(mode):
    return 1 if mode is None else 2


def split_kernel(place_ref, *refs, modes, column, flags, extra):
    total = sum(used(m) for m in modes)
    sources = refs[:total]
    mine_ref, send_ref = refs[total + extra :]
    at_end = place_ref[flags] == 1
    first = place_ref[flags + 1] == 0
    at = 0
    for index, mode in enumerate(modes):
        chunk = chunk_of(sources[at:], mode, at_end)
        at += used(mode)
        width = chunk.shape[1]
        for group in range(width // (2 * column)):
            low = chunk[:, 2 * group * column : (2 * group + 1) * column]
            high = chunk[:, (2 * group + 1) * column : (2 * group + 2) * column]
            here = pl.ds(index * width // 2 + group * column, column)
            mine_ref[:, here] = jnp.where(first, low, high)
            send_ref[:, here] = jnp.where(first, high, low)


def split_call(chunks, place, flags, column, after=()):
    flat = [array for _, *arrays in chunks for array in arrays]
    tokens, width = flat[0].shape
    count = len(chunks)
    rows = 256
    spec = pl.BlockSpec((rows, width), lambda i: (i, 0))
    half = pl.BlockSpec((rows, count * width // 2), lambda i: (i, 0))
    return pl.pallas_call(
        functools.partial(
            split_kernel,
            modes=tuple(c[0] for c in chunks), column=column, flags=flags, extra=len(after),
        ),
        grid=(tokens // rows,),
        in_specs=[pl.BlockSpec(memory_space=pltpu.SMEM)]
        + [spec] * len(flat)
        + [pl.BlockSpec(memory_space=pl.ANY)] * len(after),
        out_specs=[half, half],
        out_shape=[jax.ShapeDtypeStruct((tokens, count * width // 2), BF16)] * 2,
        compiler_params=pltpu.CompilerParams(vmem_limit_bytes=VMEM_LIMIT),
        name="split_columns",
    )(place, *flat, *after)


def grad_kernel(place_ref, *refs, modes, flags, has_sum):
    total = sum(used(m) for m in modes)
    count = len(modes)
    sources = refs[:total]
    weights = refs[total : total + count]
    out = refs[-1]
    at_end = place_ref[flags] == 1
    result = refs[total + count][...] if has_sum else None
    at = 0
    for index, mode in enumerate(modes):
        part = dot_nt(chunk_of(sources[at:], mode, at_end), weights[index][...])
        result = part if result is None else result + part
        at += used(mode)
    out[...] = result.astype(out.dtype)


def grad_call(chunks, out_weight, place, flags, distances, partial_sum, dtype, after=()):
    flat = [array for _, *arrays in chunks for array in arrays]
    tokens, width = flat[0].shape
    features = out_weight.shape[0]
    step = min(512, features)
    chunk_spec = pl.BlockSpec((tokens, width), lambda i, p: (0, 0))
    out_spec = pl.BlockSpec((tokens, step), lambda i, p: (0, i))
    weight_specs = [
        pl.BlockSpec((step, width), lambda i, p, d=d: (i, p[d])) for d in distances
    ]
    sums = () if partial_sum is None else (partial_sum,)
    return pl.pallas_call(
        functools.partial(
            grad_kernel,
            modes=tuple(c[0] for c in chunks), flags=flags, has_sum=partial_sum is not None,
        ),
        grid_spec=pltpu.PrefetchScalarGridSpec(
            num_scalar_prefetch=1,
            grid=(features // step,),
            in_specs=[chunk_spec] * len(flat)
            + weight_specs
            + [out_spec] * len(sums)
            + [pl.BlockSpec(memory_space=pl.ANY)] * len(after),
            out_specs=out_spec,
        ),
        out_shape=jax.ShapeDtypeStruct((tokens, features), dtype),
        compiler_params=pltpu.CompilerParams(vmem_limit_bytes=VMEM_LIMIT),
        name="grad_products",
    )(place, *flat, *[out_weight] * len(chunks), *sums, *after)


def product_kernel(place_ref, attn_ref, *refs, count):
    for weight, out in zip(refs[:count], refs[-count:]):
        out[...] = dot_nn(attn_ref[...], weight[...]).astype(out.dtype)


def product_call(attn, out_weight, place, count, after=()):
    tokens, width = attn.shape
    features = out_weight.shape[0]
    step = min(256, width)
    per = width // step
    spec = pl.BlockSpec((tokens, step), lambda i, p: (0, i))
    return pl.pallas_call(
        functools.partial(product_kernel, count=count),
        grid_spec=pltpu.PrefetchScalarGridSpec(
            num_scalar_prefetch=1,
            grid=(per,),
            in_specs=[pl.BlockSpec((tokens, width), lambda i, p: (0, 0))]
            + [
                pl.BlockSpec((features, step), lambda i, p, d=d: (0, p[d] * per + i))
                for d in range(count)
            ]
            + [pl.BlockSpec(memory_space=pl.ANY)] * len(after),
            out_specs=[spec] * count,
        ),
        out_shape=[jax.ShapeDtypeStruct((tokens, width), BF16)] * count,
        compiler_params=pltpu.CompilerParams(vmem_limit_bytes=50 * 1024 * 1024),
        name="mixed_products",
    )(place, attn, *[out_weight] * count, *after)


def add_kernel(*refs):
    half = len(refs) // 3
    for n in range(half):
        a, b = refs[2 * n : 2 * n + 2]
        refs[2 * half + n][...] = (a[...].astype(F32) + b[...].astype(F32)).astype(BF16)


def add_call(*pairs):
    full = [p for p in pairs if p[1] is not None]
    tokens, width = pairs[0][0].shape
    spec = pl.BlockSpec((tokens // 2, width), lambda i: (i, 0))
    sums = pl.pallas_call(
        add_kernel,
        grid=(2,),
        in_specs=[spec] * (2 * len(full)),
        out_specs=[spec] * len(full),
        out_shape=[jax.ShapeDtypeStruct((tokens, width), BF16)] * len(full),
        compiler_params=pltpu.CompilerParams(vmem_limit_bytes=VMEM_LIMIT),
        name="mixed_add",
    )(*[x for p in full for x in p])
    sums = iter(sums)
    return [p[0] if p[1] is None else next(sums) for p in pairs]


def last_kernel(own, left, right, out):
    out[...] = own[...].astype(F32) + left[...].astype(F32) + right[...].astype(F32)


def last_call(own, left, right):
    tokens, width = own.shape
    spec = pl.BlockSpec((tokens // 4, width), lambda i: (i, 0))
    return pl.pallas_call(
        last_kernel,
        grid=(4,),
        in_specs=[spec] * 3,
        out_specs=spec,
        out_shape=jax.ShapeDtypeStruct((tokens, width), F32),
        compiler_params=pltpu.CompilerParams(vmem_limit_bytes=VMEM_LIMIT),
        name="mixed_last",
    )(own, left, right)


def term_kernel(own_ref, other_ref, mine_ref, theirs_ref, *refs):
    refs[-1][0] = (
        dot_nn(own_ref[...], mine_ref[...]) + dot_nn(other_ref[...], theirs_ref[...])
    ).astype(BF16)


def term_call(own, other, mine, theirs, column, after):
    features, tokens = own.shape
    count = mine.shape[1] // column
    whole = pl.BlockSpec((features, tokens), lambda i: (0, 0))
    source = pl.BlockSpec((tokens, column), lambda i: (0, i))
    return pl.pallas_call(
        term_kernel,
        grid=(count,),
        in_specs=[whole, whole, source, source] + [pl.BlockSpec(memory_space=pl.ANY)] * len(after),
        out_specs=pl.BlockSpec((1, features, column), lambda i: (i, 0, 0)),
        out_shape=jax.ShapeDtypeStruct((count, features, column), BF16),
        compiler_params=pltpu.CompilerParams(vmem_limit_bytes=VMEM_LIMIT),
        name="weight_terms",
    )(own, other, mine, theirs, *after)


def late_kernel(place_ref, own_ref, other_ref, mine_ref, theirs_ref, early_ref, *refs, chips, base, first):
    a_send, a_keep, b_send, b_keep = refs[-4:]
    step = pl.program_id(0)
    half = own_ref.shape[0] // 2
    in_a = step < chips // 2
    in_b = jnp.logical_and(step >= chips // 4, step < 3 * chips // 4)
    is_early = place_ref[base + step] < first
    for start, flag, send, keep in ((0, in_a, a_send, a_keep), (half, in_b, b_send, b_keep)):
        here = pl.ds(start, half)

        def store(rows):
            @pl.when(flag)
            def _():
                send[0] = rows

            @pl.when(jnp.logical_not(flag))
            def _():
                keep[0] = rows

        @pl.when(is_early)
        def _():
            store(early_ref[0, here, :])

        @pl.when(jnp.logical_not(is_early))
        def _():
            rows = dot_nn(own_ref[here, :], mine_ref[...]) + dot_nn(
                other_ref[here, :], theirs_ref[...]
            )
            store(rows.astype(BF16))


def late_call(own, other, mine, theirs, early, place, base, chips, column, after):
    features, tokens = own.shape
    first = early.shape[0]
    half, quarter = chips // 2, chips // 4
    whole = pl.BlockSpec((features, tokens), lambda i, p: (0, 0))
    source = pl.BlockSpec((tokens, column), lambda i, p: (0, jnp.maximum(p[base + i] - first, 0)))
    shape = (1, features // 2, column)
    outs = [
        pl.BlockSpec(shape, lambda i, p: (jnp.minimum(i, half - 1), 0, 0)),
        pl.BlockSpec(shape, lambda i, p: (jnp.maximum(i - half, 0), 0, 0)),
        pl.BlockSpec(shape, lambda i, p: (jnp.clip(i - quarter, 0, half - 1), 0, 0)),
        pl.BlockSpec(
            shape,
            lambda i, p: (jnp.where(i < 3 * quarter, jnp.minimum(i, quarter - 1), i - half), 0, 0),
        ),
    ]
    early_spec = pl.BlockSpec(
        (1, features, column), lambda i, p: (jnp.minimum(p[base + i], first - 1), 0, 0)
    )
    return pl.pallas_call(
        functools.partial(late_kernel, chips=chips, base=base, first=first),
        grid_spec=pltpu.PrefetchScalarGridSpec(
            num_scalar_prefetch=1,
            grid=(chips,),
            in_specs=[whole, whole, source, source, early_spec]
            + [pl.BlockSpec(memory_space=pl.ANY)] * len(after),
            out_specs=outs,
        ),
        out_shape=[jax.ShapeDtypeStruct((half, features // 2, column), BF16)] * 4,
        compiler_params=pltpu.CompilerParams(vmem_limit_bytes=VMEM_LIMIT),
        name="weight_terms_late",
    )(place, own, other, mine, theirs, early, *after)


def total_kernel(top_a, top_b, bottom_a, bottom_b, *refs):
    out = refs[-1]
    half = top_a.shape[0]
    out[pl.ds(0, half), :] = top_a[...].astype(F32) + top_b[...].astype(F32)
    out[pl.ds(half, half), :] = bottom_a[...].astype(F32) + bottom_b[...].astype(F32)


def total_call(top, bottom, after):
    rows, column = top[0].shape
    spec = pl.BlockSpec((rows, column), lambda: (0, 0))
    return pl.pallas_call(
        total_kernel,
        in_specs=[spec] * 4 + [pl.BlockSpec(memory_space=pl.ANY)] * len(after),
        out_specs=pl.BlockSpec((2 * rows, column), lambda: (0, 0)),
        out_shape=jax.ShapeDtypeStruct((2 * rows, column), F32),
        compiler_params=pltpu.CompilerParams(vmem_limit_bytes=VMEM_LIMIT),
        name="weight_total",
    )(*top, *bottom, *after)


def term_order(chips):
    top = chips // 2
    groups = {(1, 0): [], (1, 1): [], (0, 1): [], (0, 0): []}
    for i in range(chips):
        groups[i & 1, int(i & top != 0)].append(i)
    return [i for key in ((1, 0), (1, 1), (0, 1), (0, 0)) for i in groups[key]]


def fold_kernel(*refs, plans):
    at = 0
    out_at = 2 * len(plans)
    for plan in plans:
        kept, arrived = refs[at : at + 2]
        for out, pairs in zip(refs[out_at : out_at + 2], plan):
            for n, (k, m) in enumerate(pairs):
                out[n] = (kept[k].astype(F32) + arrived[m].astype(F32)).astype(BF16)
        at += 2
        out_at += 2


def fold_call(sides):
    plans, operands, names, shapes = [], [], [], []
    for sent, arrived, keep, kept, bit, following in sides:
        source = [i ^ bit for i in sent]
        parts = [[i for i in keep if (i & following != 0) == flag] for flag in (True, False)]
        plans.append([[(keep.index(i), source.index(i)) for i in part] for part in parts])
        operands += [kept, arrived]
        names.append(parts)
        shapes += [jax.ShapeDtypeStruct((len(p), *kept.shape[1:]), BF16) for p in parts]
    outs = pl.pallas_call(
        functools.partial(fold_kernel, plans=plans),
        out_shape=shapes,
        compiler_params=pltpu.CompilerParams(vmem_limit_bytes=VMEM_LIMIT),
        name="fold_terms",
    )(*operands)
    return [(names[n], outs[2 * n : 2 * n + 2]) for n in range(len(sides))]


def swap(value, axis, mask):
    return lax.ppermute(value, axis, [(i, i ^ mask) for i in range(lax.axis_size(axis))])


def line_pairs(count, rightward, leftward):
    pairs = [(i, i + 1) for i in rightward] + [(i, i - 1) for i in leftward]
    even = [p for p in pairs if min(p) % 2 == 0]
    return even, [p for p in pairs if min(p) % 2 == 1]


def along(value, pairs):
    return lax.ppermute(value, "head", pairs) if pairs else None


def per_device(query, key, value, out_weight, cotangent):
    tokens, width = query.shape
    model = out_weight.shape[1]
    count = lax.axis_size("head")
    ctx_count = lax.axis_size("ctx")
    column = model // ctx_count
    me = lax.axis_index("ctx")
    z = lax.axis_index("head")

    chips = ctx_count // 2
    per_chunk = chips // count
    early = [s for s in range(count) if s != 1]
    late = [1]
    grad_early = [s for s in early if s != count - 1]
    grad_late = sorted({1, count - 1})
    bits = [1 << n for n in range(chips.bit_length() - 1)]
    order = term_order(chips)
    slots = {s: n for n, s in enumerate(early + late)}
    flags = count + chips
    table = np.zeros((count, ctx_count, flags + 2), np.int32)
    for i in range(count):
        sign = 1 if i % 2 else -1
        for j in range(ctx_count):
            table[i, j, flags:] = (int(i in (0, count - 1)), j % 2)
            table[i, j, :count] = [(i + sign * d) % count for d in range(count)]
            for n, distance in enumerate(order):
                chip = (j // 2) ^ distance
                s = sign * (chip // per_chunk - i) % count
                table[i, j, count + n] = slots[s] * per_chunk + chip % per_chunk
    place = lax.dynamic_slice(jnp.asarray(table), (z, me, 0), (1, 1, flags + 2)).reshape(-1)

    even, odd = [cotangent], [cotangent]

    def pass_on(step):
        pairs = line_pairs(count, range(step - 1, count - 1), range(1, count - step + 1))
        even_next = along(odd[-1], pairs[0])
        odd.append(along(even[-1], pairs[1]))
        even.append(even_next)

    def send_on(step, values):
        pairs = line_pairs(count, range(0, step), range(count - step, count))
        return tuple(along(v, p) for v, p in zip(values, pairs))

    def chunk(s):
        if s == 0:
            return None, cotangent
        if s == 1:
            return PICK, odd[1], joint
        if s == count - 1:
            return None, even[1]
        return SUM, odd[s], even[count - s]

    pass_on(1)
    near, three, four = pool_call(key, value)
    three = swap(three, "ctx", 2)
    four_a = swap(four, "ctx", 4)
    four_b = swap(four, "ctx", 6)
    near = lower_call(near, three, four_a, four_b)
    near, even[1], odd[1] = lax.optimization_barrier((near, even[1], odd[1]))
    near = swap(near, "ctx", 1)
    received = (near, three, four_a, four_b)

    pass_on(2)
    attn, turned, lse, tops = forward_call(query, key, value, received, after=(place,))
    turned_other = swap(turned, "ctx", 1)
    products = product_call(attn, out_weight, place, count)
    for step in range(3, count - 1):
        pass_on(step)
    is_end = jnp.logical_or(z == 0, z == count - 1)
    ends = [(0, 1), (1, 0), (count - 2, count - 1), (count - 1, count - 2)]
    ends_in = jnp.where(is_end, products[1], odd[-1])
    joint = along(ends_in, ends)
    arrived = (joint, None)

    level_max = jnp.transpose(tops[:, :LEVELS, 0])
    level_max = jnp.maximum(level_max, swap(level_max, "ctx", 1))

    mine, send = split_call([chunk(s) for s in early], place, flags, column, after=(ends_in, level_max))
    theirs = swap(send, "ctx", 1)
    grad_attn = grad_call(
        [chunk(s) for s in grad_early], out_weight, place, flags, grad_early, None, F32
    )
    level_max, theirs = lax.optimization_barrier((level_max, theirs))
    level_max = jnp.maximum(level_max, swap(level_max, "ctx", 2))
    terms = term_call(turned, turned_other, mine, theirs, column, (grad_attn, level_max))
    level_max, terms = lax.optimization_barrier((level_max, terms))
    level_max = jnp.maximum(level_max, swap(level_max, "ctx", 4))
    before_split = level_max
    mask = 8
    while mask < ctx_count:
        level_max = jnp.maximum(level_max, swap(level_max, "ctx", mask))
        mask *= 2

    def add_products(step, arrived):
        return add_call((products[step], arrived[1]), (products[count - step], arrived[0]))

    for step in range(2, count - 1):
        sums = add_products(step, arrived)
        arrived = send_on(step, sums)
    mine, send = split_call(
        [chunk(s) for s in late], place, flags, column, after=(terms, grad_attn, before_split, *[x for x in sums if x is not None])
    )
    theirs = swap(send, "ctx", 1)
    terms = late_call(turned, turned_other, mine, theirs, terms, place, count, chips, column, (level_max,))
    grad_attn = grad_call(
        [chunk(s) for s in grad_late], out_weight, place, flags, grad_late, grad_attn, BF16,
        after=tuple(terms),
    )
    half, quarter = chips // 2, chips // 4
    first = [swap(terms[0], "ctx", 2 * bits[0]), swap(terms[2], "ctx", 2 * bits[-1])]
    outs = backward_call(
        query, key, value, attn, grad_attn, lse, received, after=tuple(terms)
    )

    sums = add_products(count - 1, arrived)
    sums, first = lax.optimization_barrier((tuple(sums), first))
    arrived = send_on(count - 1, sums)
    ways = [bits, bits[::-1]]
    sent = [order[:half], order[quarter : 3 * quarter]]
    held = [order[half:], order[:quarter] + order[3 * quarter :]]
    kept = [terms[1], terms[3]]
    for n in range(len(bits) - 1):
        folded = fold_call(
            [
                (sent[k], first[k], held[k], kept[k], ways[k][n], ways[k][n + 1])
                for k in (0, 1)
            ]
        )
        sent, held = [[f[0][k] for f in folded] for k in (0, 1)]
        kept = [f[1][1] for f in folded]
        first = [swap(f[1][0], "ctx", 2 * ways[k][n + 1]) for k, f in enumerate(folded)]
    top, bottom = [(kept[k][0], first[k][0]) for k in (0, 1)]
    mixed = last_call(products[0], *arrived)

    grad_q, grad_k, grad_v, far, keep, four = outs
    far = swap(far, "ctx", 1)
    third = BLK + BLK // 2
    back = swap((keep.astype(F32) + far[2 * BLK : 2 * BLK + third]).astype(BF16), "ctx", 2)
    four = four.astype(F32) + far[2 * BLK + third :] + back[BLK:]
    four = swap(four.astype(BF16), "ctx", 4)
    grad_k, grad_v = finish_call(grad_k, grad_v, far, back, four)
    weight_grad = total_call(top, bottom, (grad_k,))
    return mixed, grad_q, grad_k, grad_v, weight_grad, level_max


def solution(mesh):
    tokens = P("ctx", "head")
    return jax.shard_map(
        per_device,
        mesh=mesh,
        in_specs=(tokens, tokens, tokens, P("head", None), tokens),
        out_specs=(tokens, tokens, tokens, tokens, P("head", "ctx"), P(None, "head")),
        check_vma=False,
    )
```

```python
import functools
import math

import jax
import jax.numpy as jnp
import numpy as np
from jax import lax
from jax.experimental import pallas as pl
from jax.experimental.pallas import tpu as pltpu
from jax.sharding import PartitionSpec as P

DH = 128
BLK = 128
LEVELS = 5
SCALE = DH ** (-0.5)
LOG_TWO = math.log(2.0)
F32 = jnp.float32
BF16 = jnp.bfloat16
VMEM_LIMIT = 20 * 1024 * 1024


def dot_nn(a, b):
    return lax.dot_general(a, b, (((1,), (0,)), ((), ())), preferred_element_type=F32)


def dot_nt(a, b):
    return lax.dot_general(a, b, (((1,), (1,)), ((), ())), preferred_element_type=F32)


def dot_tn(a, b):
    return lax.dot_general(a, b, (((0,), (0,)), ((), ())), preferred_element_type=F32)


def pool_matrix(level, rows, tokens):
    row = lax.broadcasted_iota(jnp.int32, (rows, tokens), 0)
    token = lax.broadcasted_iota(jnp.int32, (rows, tokens), 1)
    return jnp.where(lax.shift_right_logical(token, level) == row, 0.5**level, 0.0).astype(BF16)


def fill_pool(pool, tokens):
    base = 0
    for level in range(1, LEVELS):
        rows = tokens >> level
        pool[pl.ds(base, rows), :] = pool_matrix(level, rows, tokens)
        base += rows


def pool_kernel(k_ref, v_ref, near_ref, three_ref, four_ref):
    tokens = k_ref.shape[0]
    matrix = jnp.concatenate([pool_matrix(l, tokens >> l, tokens) for l in (2, 3, 4)], 0)
    for part, ref in enumerate((k_ref, v_ref)):
        rows = dot_nn(matrix, ref[...]).astype(BF16)
        base = 0
        for level, out in ((2, near_ref), (3, three_ref), (4, four_ref)):
            size = tokens >> level
            out[pl.ds(part * size, size), :] = rows[base : base + size]
            base += size


def pool_call(key, value):
    tokens, width = key.shape
    step = min(512, width)
    spec = pl.BlockSpec((tokens, step), lambda i: (0, i))
    rows = [2 * (tokens >> level) for level in (2, 3, 4)]
    return pl.pallas_call(
        pool_kernel,
        grid=(width // step,),
        in_specs=[spec, spec],
        out_specs=[pl.BlockSpec((r, step), lambda i: (0, i)) for r in rows],
        out_shape=[jax.ShapeDtypeStruct((r, width), BF16) for r in (tokens, *rows[1:])],
        compiler_params=pltpu.CompilerParams(vmem_limit_bytes=56 * 1024 * 1024),
        name="pool_keys",
    )(key, value)


def lower_kernel(near_in, three_ref, four_a, four_b, near_out):
    base = 0
    for ref in (three_ref, four_a, four_b):
        near_out[pl.ds(base, ref.shape[0]), :] = ref[...]
        base += ref.shape[0]


def lower_call(near, three, four_a, four_b):
    tokens, width = near.shape
    spec = lambda r: pl.BlockSpec((r.shape[0], width), lambda i: (0, 0))
    return pl.pallas_call(
        lower_kernel,
        grid=(1,),
        in_specs=[pl.BlockSpec(memory_space=pl.ANY), spec(three), spec(four_a), spec(four_b)],
        out_specs=pl.BlockSpec((tokens // 2, width), lambda i: (1, 0)),
        out_shape=jax.ShapeDtypeStruct((tokens, width), BF16),
        input_output_aliases={0: 0},
        compiler_params=pltpu.CompilerParams(vmem_limit_bytes=VMEM_LIMIT),
        name="lower_rows",
    )(near, three, four_a, four_b)


def expand_two(scratch, base, value):
    rows = value.shape[0]
    scratch[pl.ds(base, rows, stride=2), :] = value
    scratch[pl.ds(base + 1, rows, stride=2), :] = value
    return scratch[pl.ds(base, 2 * rows), :]


def partner_rows(near, three, four_a, four_b, columns):
    def cut(ref, base, half):
        return ref[pl.ds(base, half), columns], ref[pl.ds(base + half, half), columns]

    two = BLK
    join = lambda *pairs: tuple(jnp.concatenate(p, 0) for p in zip(*pairs))
    return {
        2: cut(near, 0, two),
        3: join(cut(three, 0, two // 2), cut(near, 2 * two, two // 2)),
        4: join(
            cut(four_a, 0, two // 4),
            cut(four_b, 0, two // 4),
            cut(near, 3 * two, two // 4),
            cut(near, 3 * two + two // 2, two // 4),
        ),
    }


def coarse_slices(tokens):
    base = 0
    found = {}
    for level in range(1, LEVELS):
        rows = tokens >> level
        found[level] = slice(base, base + rows)
        base += rows
    return found


def forward_kernel(
    q_ref, k_ref, v_ref, near, three, four_a, four_b, *rest, extra
):
    attn_ref, turned_ref, lse_ref, top_ref, pool, peak_s, total_s, summed_s = rest[extra:]
    tokens, width = q_ref.shape

    @pl.when(pl.program_id(0) == 0)
    def _():
        fill_pool(pool, tokens)

    q_all = dot_nn(pool[...], q_ref[...]).astype(BF16)
    half = pl.ds(0, tokens // 2)
    k_one = dot_nn(pool[half, :], k_ref[...]).astype(BF16)
    v_one = dot_nn(pool[half, :], v_ref[...]).astype(BF16)
    where = coarse_slices(tokens)
    heads = range(width // DH)
    columns = [pl.ds(h * DH, DH) for h in heads]
    lanes = [slice(h * DH, (h + 1) * DH) for h in heads]
    work = []
    for h in heads:
        partner = partner_rows(near, three, four_a, four_b, columns[h])
        for level in range(LEVELS - 1, -1, -1):
            if level >= 2:
                work.append((h, level, q_all[where[level], lanes[h]], *partner[level]))
            elif level == 1:
                qc, kc, vc = q_all[where[1], lanes[h]], k_one[:, lanes[h]], v_one[:, lanes[h]]
                for b in range(2):
                    mine = slice(b * BLK, (b + 1) * BLK)
                    other = slice((1 - b) * BLK, (2 - b) * BLK)
                    work.append((h, 1, qc[mine], kc[other], vc[other]))
            else:
                for b in range(tokens // (2 * BLK)):
                    both = pl.ds(b * 2 * BLK, 2 * BLK)
                    work.append(
                        (h, 0, q_ref[both, columns[h]], k_ref[both, columns[h]], v_ref[both, columns[h]])
                    )
    scores = [dot_nt(q, k) * SCALE for _, _, q, k, _ in work]
    peaks = [jnp.max(s, axis=-1, keepdims=True) for s in scores]
    weights = [jnp.exp(s - p).astype(BF16) for s, p in zip(scores, peaks)]
    sums = [
        dot_nn(w, jnp.concatenate([item[4], jnp.ones_like(item[4])], 1))
        for w, item in zip(weights, work)
    ]

    def joined(h, level, values):
        return jnp.concatenate([x for x, item in zip(values, work) if item[:2] == (h, level)], 0)

    row = lax.broadcasted_iota(jnp.int32, (8, 128), 0)
    tiles = [jnp.zeros((8, 128), F32) for _ in heads]
    state = {}
    base = 0
    for level in range(LEVELS - 1, -1, -1):
        rows = tokens >> level
        for h in heads:
            peak = joined(h, level, peaks)
            total = joined(h, level, sums)
            tiles[h] = jnp.where(row == level, jnp.max(peak), tiles[h])
            peak = jnp.broadcast_to(peak + level * LOG_TWO, (rows, DH))
            total, summed = total[:, DH:], total[:, :DH]
            if level < LEVELS - 1:
                place = h * 2 * tokens + base
                peak_up, total_up, summed_up = [
                    expand_two(scratch, place, value)
                    for scratch, value in zip((peak_s, total_s, summed_s), state[h])
                ]
                top = jnp.maximum(peak, peak_up)
                mine = jnp.exp(peak - top)
                other = jnp.exp(peak_up - top)
                total = mine * total + other * total_up
                summed = mine * summed + other * summed_up
                peak = top
            state[h] = (peak, total, summed)
        if level < LEVELS - 1:
            base += rows
    for h in heads:
        peak, total, summed = state[h]
        attn = (summed / total).astype(BF16)
        attn_ref[:, columns[h]] = attn
        turned_ref[columns[h], :] = attn.T
        lse_ref[:, columns[h]] = peak + jnp.log(total)
        top_ref[h] = tiles[h]


def forward_call(query, key, value, received, after=(), step=4):
    tokens, width = query.shape
    heads = width // DH
    spec = pl.BlockSpec((tokens, step * DH), lambda h: (0, h))
    others = [pl.BlockSpec((r.shape[0], step * DH), lambda h: (0, h)) for r in received]
    others += [pl.BlockSpec(memory_space=pl.ANY)] * len(after)
    return pl.pallas_call(
        functools.partial(forward_kernel, extra=len(after)),
        grid=(heads // step,),
        in_specs=[spec, spec, spec] + others,
        out_specs=[
            spec,
            pl.BlockSpec((step * DH, tokens), lambda h: (h, 0)),
            spec,
            pl.BlockSpec((step, 8, 128), lambda h: (h, 0, 0)),
        ],
        out_shape=[
            jax.ShapeDtypeStruct((tokens, width), BF16),
            jax.ShapeDtypeStruct((width, tokens), BF16),
            jax.ShapeDtypeStruct((tokens, width), F32),
            jax.ShapeDtypeStruct((heads, 8, 128), F32),
        ],
        scratch_shapes=[
            pltpu.VMEM((tokens - tokens // 16, tokens), BF16),
            pltpu.VMEM((step * 2 * tokens, 128), F32),
            pltpu.VMEM((step * 2 * tokens, 128), F32),
            pltpu.VMEM((step * 2 * tokens, 128), F32),
        ],
        compiler_params=pltpu.CompilerParams(vmem_limit_bytes=50 * 1024 * 1024),
        name="attention_forward",
    )(query, key, value, *received, *after)


def backward_kernel(
    q_ref, k_ref, v_ref, attn_ref, grad_ref, lse_ref, near, three, four_a, four_b, *rest, extra
):
    gq_ref, gk_ref, gv_ref, far, keep, four, pool, lse_s, grad_s, scal_s, gq_s, gk_s, gv_s = rest[extra:]
    tokens, width = q_ref.shape

    @pl.when(pl.program_id(0) == 0)
    def _():
        fill_pool(pool, tokens)

    q_all = dot_nn(pool[...], q_ref[...]).astype(BF16)
    half_rows = pl.ds(0, tokens // 2)
    k_one = dot_nn(pool[half_rows, :], k_ref[...]).astype(BF16)
    v_one = dot_nn(pool[half_rows, :], v_ref[...]).astype(BF16)
    where = coarse_slices(tokens)
    heads = range(width // DH)
    columns = [pl.ds(h * DH, DH) for h in heads]
    lanes = [slice(h * DH, (h + 1) * DH) for h in heads]
    scalars = []
    for h in heads:
        grad_f = grad_ref[:, columns[h]].astype(F32)
        scalar = jnp.sum(grad_f * attn_ref[:, columns[h]].astype(F32), axis=-1, keepdims=True)
        scalars.append(scalar)
        first = pl.ds(h * 2 * tokens, tokens)
        lse_s[first, :] = lse_ref[:, columns[h]]
        scal_s[first, :] = jnp.broadcast_to(scalar, (tokens, 128))
        grad_s[first, :] = grad_f
    places = {}
    base = 0
    rows = tokens
    for level in range(1, LEVELS):
        half = rows // 2
        for h in heads:
            start = h * 2 * tokens + base
            even = pl.ds(start, half, stride=2)
            odd = pl.ds(start + 1, half, stride=2)
            lse_even, lse_odd = lse_s[even, :], lse_s[odd, :]
            least = jnp.minimum(lse_even, lse_odd)
            factor_even = jnp.exp(least - lse_even)
            factor_odd = jnp.exp(least - lse_odd)
            summed = factor_even * grad_s[even, :] + factor_odd * grad_s[odd, :]
            summed_scalar = factor_even * scal_s[even, :] + factor_odd * scal_s[odd, :]
            if level < LEVELS - 1:
                nxt = pl.ds(start + rows, half)
                lse_s[nxt, :] = least
                grad_s[nxt, :] = summed
                scal_s[nxt, :] = summed_scalar
            places[h, level] = (least, summed.astype(BF16), summed_scalar)
        base += rows
        rows = half
    work = []
    for h in heads:
        partner = partner_rows(near, three, four_a, four_b, columns[h])
        for level in range(LEVELS - 1, -1, -1):
            if level >= 2:
                work.append(
                    (h, level, q_all[where[level], lanes[h]], *partner[level], *places[h, level])
                )
            elif level == 1:
                low, gr, sc = places[h, 1]
                qc, kc, vc = q_all[where[1], lanes[h]], k_one[:, lanes[h]], v_one[:, lanes[h]]
                for b in range(2):
                    mine = slice(b * BLK, (b + 1) * BLK)
                    other = slice((1 - b) * BLK, (2 - b) * BLK)
                    work.append((h, 1, qc[mine], kc[other], vc[other], low[mine], gr[mine], sc[mine]))
            else:
                for b in range(tokens // (2 * BLK)):
                    both = pl.ds(b * 2 * BLK, 2 * BLK)
                    part = slice(b * 2 * BLK, (b + 1) * 2 * BLK)
                    low = lse_ref[both, columns[h]]
                    work.append((
                        h, 0, q_ref[both, columns[h]], k_ref[both, columns[h]], v_ref[both, columns[h]],
                        jnp.concatenate([low, low], 1), grad_ref[both, columns[h]], scalars[h][part],
                    ))
    scores = [dot_nt(item[2], item[3]) for item in work]
    grads = [dot_nt(item[6], item[4]) for item in work]
    weights = [
        jnp.exp(s * SCALE + (item[1] * LOG_TWO - item[5])) for s, item in zip(scores, work)
    ]
    grad_scores = [
        (w * (g - item[7])).astype(BF16) for w, g, item in zip(weights, grads, work)
    ]
    weights = [w.astype(BF16) for w in weights]
    parts_q = [dot_nn(s, item[3]) * SCALE for s, item in zip(grad_scores, work)]
    parts_k = [dot_tn(s, item[2]) * SCALE for s, item in zip(grad_scores, work)]
    parts_v = [dot_tn(w, item[6]) for w, item in zip(weights, work)]
    found = {}
    for item, *parts in zip(work, parts_q, parts_k, parts_v):
        found.setdefault(item[:2], []).append(parts)
    state = {}
    up = 0
    for level in range(LEVELS - 1, -1, -1):
        rows = tokens >> level
        for h in heads:
            parts = found[h, level]
            if level >= 2:
                part_q, part_k, part_v = parts[0]
                part_k = part_k.astype(BF16)
                part_v = part_v.astype(BF16)
                outs = {
                    2: ((far, 0),),
                    3: ((keep, 0), (far, 2 * BLK)),
                    4: ((four, 0), (keep, BLK), (far, 3 * BLK + BLK // 2), (far, 3 * BLK)),
                }[level]
                piece = BLK // len(outs)
                for i, (out, at) in enumerate(outs):
                    out[pl.ds(at, piece), columns[h]] = part_k[i * piece : (i + 1) * piece]
                    out[pl.ds(at + piece, piece), columns[h]] = part_v[i * piece : (i + 1) * piece]
            elif level == 1:
                part_q = jnp.concatenate([parts[0][0], parts[1][0]], 0)
                part_k = jnp.concatenate([parts[1][1], parts[0][1]], 0)
                part_v = jnp.concatenate([parts[1][2], parts[0][2]], 0)
                coarse_k = expand_two(gk_s, h * tokens, part_k * 0.5)
                coarse_v = expand_two(gv_s, h * tokens, part_v * 0.5)
                state[h, "k"], state[h, "v"] = coarse_k, coarse_v
            if level == 0:
                for b, (part_q, part_k, part_v) in enumerate(parts):
                    both = slice(b * 2 * BLK, (b + 1) * 2 * BLK)
                    here = pl.ds(b * 2 * BLK, 2 * BLK)
                    gq_ref[here, columns[h]] = part_q + state[h, "q"][both]
                    gk_ref[here, columns[h]] = (part_k + state[h, "k"][both]).astype(BF16)
                    gv_ref[here, columns[h]] = (part_v + state[h, "v"][both]).astype(BF16)
            else:
                grad_q = part_q if level == LEVELS - 1 else part_q + state[h, "q"]
                state[h, "q"] = expand_two(gq_s, h * 2 * tokens + up, grad_q * 0.5)
        up += 2 * rows


def backward_call(query, key, value, attn, grad, lse, received, after=(), step=2):
    tokens, width = query.shape
    steps = width // DH // step
    spec = pl.BlockSpec((tokens, step * DH), lambda h: (0, h))
    others = [pl.BlockSpec((r.shape[0], step * DH), lambda h: (0, h)) for r in received]
    others += [pl.BlockSpec(memory_space=pl.ANY)] * len(after)
    full = jax.ShapeDtypeStruct((tokens, width), F32)
    back_rows = (tokens, BLK + BLK // 2, BLK // 2)
    outs = [pl.BlockSpec((r, step * DH), lambda h: (0, h)) for r in back_rows]
    return pl.pallas_call(
        functools.partial(backward_kernel, extra=len(after)),
        grid=(steps,),
        in_specs=[spec] * 6 + others,
        out_specs=[spec] * 3 + outs,
        out_shape=[full] + [jax.ShapeDtypeStruct((tokens, width), BF16)] * 2
        + [jax.ShapeDtypeStruct((r, width), BF16) for r in back_rows],
        scratch_shapes=[pltpu.VMEM((tokens - tokens // 16, tokens), BF16)]
        + [pltpu.VMEM((step * 2 * tokens, 128), F32)] * 6,
        compiler_params=pltpu.CompilerParams(vmem_limit_bytes=VMEM_LIMIT),
        name="attention_backward",
    )(query, key, value, attn, grad, lse, *received, *after)


def finish_kernel(gk_ref, gv_ref, near, three, four, ok_ref, ov_ref, k_s, v_s):
    heads = range(gk_ref.shape[1] // DH)
    tokens = gk_ref.shape[0]
    state = {}
    base = 0
    for ref, rows in ((four, BLK // 4), (three, BLK // 2), (near, BLK), (None, 2 * BLK)):
        for h in heads:
            for part, scr in ((0, k_s), (1, v_s)):
                total = state.get((h, part))
                if ref is not None:
                    own = ref[pl.ds(part * rows, rows), pl.ds(h * DH, DH)].astype(F32)
                    total = own if total is None else total + own
                state[h, part] = expand_two(scr, h * 2 * tokens + base, total * 0.5)
        base += 2 * rows
    for h in heads:
        here = pl.ds(h * DH, DH)
        ok_ref[:, here] = gk_ref[:, here].astype(F32) + state[h, 0]
        ov_ref[:, here] = gv_ref[:, here].astype(F32) + state[h, 1]


def finish_call(grad_k, grad_v, near, three, four):
    tokens, width = grad_k.shape
    step = 2 * DH
    spec = pl.BlockSpec((tokens, step), lambda h: (0, h))
    rows = (2 * BLK, BLK, BLK // 2)
    extra = [pl.BlockSpec((r, step), lambda h: (0, h)) for r in rows]
    full = jax.ShapeDtypeStruct((tokens, width), F32)
    scratch = pltpu.VMEM((2 * 2 * tokens, DH), F32)
    return pl.pallas_call(
        finish_kernel,
        grid=(width // step,),
        in_specs=[spec, spec] + extra,
        out_specs=[spec, spec],
        out_shape=[full, full],
        scratch_shapes=[scratch, scratch],
        compiler_params=pltpu.CompilerParams(vmem_limit_bytes=50 * 1024 * 1024),
        name="add_returned",
    )(grad_k, grad_v, near, three, four)


SUM, PICK = "sum", "pick"


def chunk_of(refs, mode, at_end):
    if mode is None:
        return refs[0][...]
    if mode == SUM:
        return refs[0][...] + refs[1][...]
    return jnp.where(at_end, refs[1][...], refs[0][...])


def used(mode):
    return 1 if mode is None else 2


def split_kernel(place_ref, *refs, modes, column, flags, extra):
    total = sum(used(m) for m in modes)
    sources = refs[:total]
    mine_ref, send_ref = refs[total + extra :]
    at_end = place_ref[flags] == 1
    first = place_ref[flags + 1] == 0
    at = 0
    for index, mode in enumerate(modes):
        chunk = chunk_of(sources[at:], mode, at_end)
        at += used(mode)
        width = chunk.shape[1]
        for group in range(width // (2 * column)):
            low = chunk[:, 2 * group * column : (2 * group + 1) * column]
            high = chunk[:, (2 * group + 1) * column : (2 * group + 2) * column]
            here = pl.ds(index * width // 2 + group * column, column)
            mine_ref[:, here] = jnp.where(first, low, high)
            send_ref[:, here] = jnp.where(first, high, low)


def split_call(chunks, place, flags, column, after=()):
    flat = [array for _, *arrays in chunks for array in arrays]
    tokens, width = flat[0].shape
    count = len(chunks)
    rows = 256
    spec = pl.BlockSpec((rows, width), lambda i: (i, 0))
    half = pl.BlockSpec((rows, count * width // 2), lambda i: (i, 0))
    return pl.pallas_call(
        functools.partial(
            split_kernel,
            modes=tuple(c[0] for c in chunks), column=column, flags=flags, extra=len(after),
        ),
        grid=(tokens // rows,),
        in_specs=[pl.BlockSpec(memory_space=pltpu.SMEM)]
        + [spec] * len(flat)
        + [pl.BlockSpec(memory_space=pl.ANY)] * len(after),
        out_specs=[half, half],
        out_shape=[jax.ShapeDtypeStruct((tokens, count * width // 2), BF16)] * 2,
        compiler_params=pltpu.CompilerParams(vmem_limit_bytes=VMEM_LIMIT),
        name="split_columns",
    )(place, *flat, *after)


def grad_kernel(place_ref, *refs, modes, flags, has_sum):
    total = sum(used(m) for m in modes)
    count = len(modes)
    sources = refs[:total]
    weights = refs[total : total + count]
    out = refs[-1]
    at_end = place_ref[flags] == 1
    result = refs[total + count][...] if has_sum else None
    at = 0
    for index, mode in enumerate(modes):
        part = dot_nt(chunk_of(sources[at:], mode, at_end), weights[index][...])
        result = part if result is None else result + part
        at += used(mode)
    out[...] = result.astype(out.dtype)


def grad_call(chunks, out_weight, place, flags, distances, partial_sum, dtype, after=()):
    flat = [array for _, *arrays in chunks for array in arrays]
    tokens, width = flat[0].shape
    features = out_weight.shape[0]
    step = min(512, features)
    chunk_spec = pl.BlockSpec((tokens, width), lambda i, p: (0, 0))
    out_spec = pl.BlockSpec((tokens, step), lambda i, p: (0, i))
    weight_specs = [
        pl.BlockSpec((step, width), lambda i, p, d=d: (i, p[d])) for d in distances
    ]
    sums = () if partial_sum is None else (partial_sum,)
    return pl.pallas_call(
        functools.partial(
            grad_kernel,
            modes=tuple(c[0] for c in chunks), flags=flags, has_sum=partial_sum is not None,
        ),
        grid_spec=pltpu.PrefetchScalarGridSpec(
            num_scalar_prefetch=1,
            grid=(features // step,),
            in_specs=[chunk_spec] * len(flat)
            + weight_specs
            + [out_spec] * len(sums)
            + [pl.BlockSpec(memory_space=pl.ANY)] * len(after),
            out_specs=out_spec,
        ),
        out_shape=jax.ShapeDtypeStruct((tokens, features), dtype),
        compiler_params=pltpu.CompilerParams(vmem_limit_bytes=VMEM_LIMIT),
        name="grad_products",
    )(place, *flat, *[out_weight] * len(chunks), *sums, *after)


def product_kernel(place_ref, attn_ref, *refs, count):
    for weight, out in zip(refs[:count], refs[-count:]):
        out[...] = dot_nn(attn_ref[...], weight[...]).astype(out.dtype)


def product_call(attn, out_weight, place, count, after=()):
    tokens, width = attn.shape
    features = out_weight.shape[0]
    step = min(256, width)
    per = width // step
    spec = pl.BlockSpec((tokens, step), lambda i, p: (0, i))
    return pl.pallas_call(
        functools.partial(product_kernel, count=count),
        grid_spec=pltpu.PrefetchScalarGridSpec(
            num_scalar_prefetch=1,
            grid=(per,),
            in_specs=[pl.BlockSpec((tokens, width), lambda i, p: (0, 0))]
            + [
                pl.BlockSpec((features, step), lambda i, p, d=d: (0, p[d] * per + i))
                for d in range(count)
            ]
            + [pl.BlockSpec(memory_space=pl.ANY)] * len(after),
            out_specs=[spec] * count,
        ),
        out_shape=[jax.ShapeDtypeStruct((tokens, width), BF16)] * count,
        compiler_params=pltpu.CompilerParams(vmem_limit_bytes=50 * 1024 * 1024),
        name="mixed_products",
    )(place, attn, *[out_weight] * count, *after)


def add_kernel(*refs):
    half = len(refs) // 3
    for n in range(half):
        a, b = refs[2 * n : 2 * n + 2]
        refs[2 * half + n][...] = (a[...].astype(F32) + b[...].astype(F32)).astype(BF16)


def add_call(*pairs):
    full = [p for p in pairs if p[1] is not None]
    tokens, width = pairs[0][0].shape
    spec = pl.BlockSpec((tokens // 2, width), lambda i: (i, 0))
    sums = pl.pallas_call(
        add_kernel,
        grid=(2,),
        in_specs=[spec] * (2 * len(full)),
        out_specs=[spec] * len(full),
        out_shape=[jax.ShapeDtypeStruct((tokens, width), BF16)] * len(full),
        compiler_params=pltpu.CompilerParams(vmem_limit_bytes=VMEM_LIMIT),
        name="mixed_add",
    )(*[x for p in full for x in p])
    sums = iter(sums)
    return [p[0] if p[1] is None else next(sums) for p in pairs]


def last_kernel(own, left, right, out):
    out[...] = own[...].astype(F32) + left[...].astype(F32) + right[...].astype(F32)


def last_call(own, left, right):
    tokens, width = own.shape
    spec = pl.BlockSpec((tokens // 4, width), lambda i: (i, 0))
    return pl.pallas_call(
        last_kernel,
        grid=(4,),
        in_specs=[spec] * 3,
        out_specs=spec,
        out_shape=jax.ShapeDtypeStruct((tokens, width), F32),
        compiler_params=pltpu.CompilerParams(vmem_limit_bytes=VMEM_LIMIT),
        name="mixed_last",
    )(own, left, right)


def term_kernel(own_ref, other_ref, mine_ref, theirs_ref, *refs):
    refs[-1][0] = (
        dot_nn(own_ref[...], mine_ref[...]) + dot_nn(other_ref[...], theirs_ref[...])
    ).astype(BF16)


def term_call(own, other, mine, theirs, column, after):
    features, tokens = own.shape
    count = mine.shape[1] // column
    whole = pl.BlockSpec((features, tokens), lambda i: (0, 0))
    source = pl.BlockSpec((tokens, column), lambda i: (0, i))
    return pl.pallas_call(
        term_kernel,
        grid=(count,),
        in_specs=[whole, whole, source, source] + [pl.BlockSpec(memory_space=pl.ANY)] * len(after),
        out_specs=pl.BlockSpec((1, features, column), lambda i: (i, 0, 0)),
        out_shape=jax.ShapeDtypeStruct((count, features, column), BF16),
        compiler_params=pltpu.CompilerParams(vmem_limit_bytes=VMEM_LIMIT),
        name="weight_terms",
    )(own, other, mine, theirs, *after)


def late_kernel(place_ref, own_ref, other_ref, mine_ref, theirs_ref, early_ref, *refs, chips, base, first):
    a_send, a_keep, b_send, b_keep = refs[-4:]
    step = pl.program_id(0)
    half = own_ref.shape[0] // 2
    in_a = step < chips // 2
    in_b = jnp.logical_and(step >= chips // 4, step < 3 * chips // 4)
    is_early = place_ref[base + step] < first
    for start, flag, send, keep in ((0, in_a, a_send, a_keep), (half, in_b, b_send, b_keep)):
        here = pl.ds(start, half)

        def store(rows):
            @pl.when(flag)
            def _():
                send[0] = rows

            @pl.when(jnp.logical_not(flag))
            def _():
                keep[0] = rows

        @pl.when(is_early)
        def _():
            store(early_ref[0, here, :])

        @pl.when(jnp.logical_not(is_early))
        def _():
            rows = dot_nn(own_ref[here, :], mine_ref[...]) + dot_nn(
                other_ref[here, :], theirs_ref[...]
            )
            store(rows.astype(BF16))


def late_call(own, other, mine, theirs, early, place, base, chips, column, after):
    features, tokens = own.shape
    first = early.shape[0]
    half, quarter = chips // 2, chips // 4
    whole = pl.BlockSpec((features, tokens), lambda i, p: (0, 0))
    source = pl.BlockSpec((tokens, column), lambda i, p: (0, jnp.maximum(p[base + i] - first, 0)))
    shape = (1, features // 2, column)
    outs = [
        pl.BlockSpec(shape, lambda i, p: (jnp.minimum(i, half - 1), 0, 0)),
        pl.BlockSpec(shape, lambda i, p: (jnp.maximum(i - half, 0), 0, 0)),
        pl.BlockSpec(shape, lambda i, p: (jnp.clip(i - quarter, 0, half - 1), 0, 0)),
        pl.BlockSpec(
            shape,
            lambda i, p: (jnp.where(i < 3 * quarter, jnp.minimum(i, quarter - 1), i - half), 0, 0),
        ),
    ]
    early_spec = pl.BlockSpec(
        (1, features, column), lambda i, p: (jnp.minimum(p[base + i], first - 1), 0, 0)
    )
    return pl.pallas_call(
        functools.partial(late_kernel, chips=chips, base=base, first=first),
        grid_spec=pltpu.PrefetchScalarGridSpec(
            num_scalar_prefetch=1,
            grid=(chips,),
            in_specs=[whole, whole, source, source, early_spec]
            + [pl.BlockSpec(memory_space=pl.ANY)] * len(after),
            out_specs=outs,
        ),
        out_shape=[jax.ShapeDtypeStruct((half, features // 2, column), BF16)] * 4,
        compiler_params=pltpu.CompilerParams(vmem_limit_bytes=VMEM_LIMIT),
        name="weight_terms_late",
    )(place, own, other, mine, theirs, early, *after)


def total_kernel(top_a, top_b, bottom_a, bottom_b, *refs):
    out = refs[-1]
    half = top_a.shape[0]
    out[pl.ds(0, half), :] = top_a[...].astype(F32) + top_b[...].astype(F32)
    out[pl.ds(half, half), :] = bottom_a[...].astype(F32) + bottom_b[...].astype(F32)


def total_call(top, bottom, after):
    rows, column = top[0].shape
    spec = pl.BlockSpec((rows, column), lambda: (0, 0))
    return pl.pallas_call(
        total_kernel,
        in_specs=[spec] * 4 + [pl.BlockSpec(memory_space=pl.ANY)] * len(after),
        out_specs=pl.BlockSpec((2 * rows, column), lambda: (0, 0)),
        out_shape=jax.ShapeDtypeStruct((2 * rows, column), F32),
        compiler_params=pltpu.CompilerParams(vmem_limit_bytes=50 * 1024 * 1024),
        name="weight_total",
    )(*top, *bottom, *after)


def term_order(chips):
    top = chips // 2
    groups = {(1, 0): [], (1, 1): [], (0, 1): [], (0, 0): []}
    for i in range(chips):
        groups[i & 1, int(i & top != 0)].append(i)
    return [i for key in ((1, 0), (1, 1), (0, 1), (0, 0)) for i in groups[key]]


def fold_kernel(*refs, plans):
    at = 0
    out_at = 2 * len(plans)
    for plan in plans:
        kept, arrived = refs[at : at + 2]
        for out, pairs in zip(refs[out_at : out_at + 2], plan):
            for n, (k, m) in enumerate(pairs):
                out[n] = (kept[k].astype(F32) + arrived[m].astype(F32)).astype(BF16)
        at += 2
        out_at += 2


def fold_call(sides):
    plans, operands, names, shapes = [], [], [], []
    for sent, arrived, keep, kept, bit, following in sides:
        source = [i ^ bit for i in sent]
        parts = [[i for i in keep if (i & following != 0) == flag] for flag in (True, False)]
        plans.append([[(keep.index(i), source.index(i)) for i in part] for part in parts])
        operands += [kept, arrived]
        names.append(parts)
        shapes += [jax.ShapeDtypeStruct((len(p), *kept.shape[1:]), BF16) for p in parts]
    outs = pl.pallas_call(
        functools.partial(fold_kernel, plans=plans),
        out_shape=shapes,
        compiler_params=pltpu.CompilerParams(vmem_limit_bytes=VMEM_LIMIT),
        name="fold_terms",
    )(*operands)
    return [(names[n], outs[2 * n : 2 * n + 2]) for n in range(len(sides))]


def swap(value, axis, mask):
    return lax.ppermute(value, axis, [(i, i ^ mask) for i in range(lax.axis_size(axis))])


def line_pairs(count, rightward, leftward):
    pairs = [(i, i + 1) for i in rightward] + [(i, i - 1) for i in leftward]
    even = [p for p in pairs if min(p) % 2 == 0]
    return even, [p for p in pairs if min(p) % 2 == 1]


def along(value, pairs):
    return lax.ppermute(value, "head", pairs) if pairs else None


def per_device(query, key, value, out_weight, cotangent):
    tokens, width = query.shape
    model = out_weight.shape[1]
    count = lax.axis_size("head")
    ctx_count = lax.axis_size("ctx")
    column = model // ctx_count
    me = lax.axis_index("ctx")
    z = lax.axis_index("head")

    chips = ctx_count // 2
    per_chunk = chips // count
    early = [s for s in range(count) if s != 1]
    late = [1]
    grad_early = [s for s in early if s != count - 1]
    grad_late = sorted({1, count - 1})
    bits = [1 << n for n in range(chips.bit_length() - 1)]
    order = term_order(chips)
    slots = {s: n for n, s in enumerate(early + late)}
    flags = count + chips
    table = np.zeros((count, ctx_count, flags + 2), np.int32)
    for i in range(count):
        sign = 1 if i % 2 else -1
        for j in range(ctx_count):
            table[i, j, flags:] = (int(i in (0, count - 1)), j % 2)
            table[i, j, :count] = [(i + sign * d) % count for d in range(count)]
            for n, distance in enumerate(order):
                chip = (j // 2) ^ distance
                s = sign * (chip // per_chunk - i) % count
                table[i, j, count + n] = slots[s] * per_chunk + chip % per_chunk
    place = lax.dynamic_slice(jnp.asarray(table), (z, me, 0), (1, 1, flags + 2)).reshape(-1)

    even, odd = [cotangent], [cotangent]

    def pass_on(step):
        pairs = line_pairs(count, range(step - 1, count - 1), range(1, count - step + 1))
        even_next = along(odd[-1], pairs[0])
        odd.append(along(even[-1], pairs[1]))
        even.append(even_next)

    def send_on(step, values):
        pairs = line_pairs(count, range(0, step), range(count - step, count))
        return tuple(along(v, p) for v, p in zip(values, pairs))

    def chunk(s):
        if s == 0:
            return None, cotangent
        if s == 1:
            return PICK, odd[1], joint
        if s == count - 1:
            return None, even[1]
        return SUM, odd[s], even[count - s]

    pass_on(1)
    near, three, four = pool_call(key, value)
    three = swap(three, "ctx", 2)
    four_a = swap(four, "ctx", 4)
    four_b = swap(four, "ctx", 6)
    near = lower_call(near, three, four_a, four_b)
    near, even[1], odd[1] = lax.optimization_barrier((near, even[1], odd[1]))
    near = swap(near, "ctx", 1)
    received = (near, three, four_a, four_b)

    pass_on(2)
    attn, turned, lse, tops = forward_call(query, key, value, received, after=(place,))
    turned_other = swap(turned, "ctx", 1)
    products = product_call(attn, out_weight, place, count)
    for step in range(3, count - 1):
        pass_on(step)
    is_end = jnp.logical_or(z == 0, z == count - 1)
    ends = [(0, 1), (1, 0), (count - 2, count - 1), (count - 1, count - 2)]
    ends_in = jnp.where(is_end, products[1], odd[-1])
    joint = along(ends_in, ends)
    arrived = (joint, None)

    level_max = jnp.transpose(tops[:, :LEVELS, 0])
    level_max = jnp.maximum(level_max, swap(level_max, "ctx", 1))

    mine, send = split_call([chunk(s) for s in early], place, flags, column, after=(ends_in, level_max))
    theirs = swap(send, "ctx", 1)
    grad_attn = grad_call(
        [chunk(s) for s in grad_early], out_weight, place, flags, grad_early, None, F32
    )
    level_max, theirs = lax.optimization_barrier((level_max, theirs))
    level_max = jnp.maximum(level_max, swap(level_max, "ctx", 2))
    terms = term_call(turned, turned_other, mine, theirs, column, (grad_attn, level_max))
    level_max, terms = lax.optimization_barrier((level_max, terms))
    level_max = jnp.maximum(level_max, swap(level_max, "ctx", 4))
    before_split = level_max
    mask = 8
    while mask < ctx_count:
        level_max = jnp.maximum(level_max, swap(level_max, "ctx", mask))
        mask *= 2

    def add_products(step, arrived):
        return add_call((products[step], arrived[1]), (products[count - step], arrived[0]))

    for step in range(2, count - 1):
        sums = add_products(step, arrived)
        arrived = send_on(step, sums)
    mine, send = split_call(
        [chunk(s) for s in late], place, flags, column, after=(terms, grad_attn, before_split, *[x for x in sums if x is not None])
    )
    theirs = swap(send, "ctx", 1)
    terms = late_call(turned, turned_other, mine, theirs, terms, place, count, chips, column, (level_max,))
    grad_attn = grad_call(
        [chunk(s) for s in grad_late], out_weight, place, flags, grad_late, grad_attn, BF16,
        after=tuple(terms),
    )
    half, quarter = chips // 2, chips // 4
    first = [swap(terms[0], "ctx", 2 * bits[0]), swap(terms[2], "ctx", 2 * bits[-1])]
    outs = backward_call(
        query, key, value, attn, grad_attn, lse, received, after=tuple(terms)
    )

    sums = add_products(count - 1, arrived)
    sums, first = lax.optimization_barrier((tuple(sums), first))
    arrived = send_on(count - 1, sums)
    ways = [bits, bits[::-1]]
    sent = [order[:half], order[quarter : 3 * quarter]]
    held = [order[half:], order[:quarter] + order[3 * quarter :]]
    kept = [terms[1], terms[3]]
    for n in range(len(bits) - 1):
        folded = fold_call(
            [
                (sent[k], first[k], held[k], kept[k], ways[k][n], ways[k][n + 1])
                for k in (0, 1)
            ]
        )
        sent, held = [[f[0][k] for f in folded] for k in (0, 1)]
        kept = [f[1][1] for f in folded]
        first = [swap(f[1][0], "ctx", 2 * ways[k][n + 1]) for k, f in enumerate(folded)]
    top, bottom = [(kept[k][0], first[k][0]) for k in (0, 1)]
    mixed = last_call(products[0], *arrived)

    grad_q, grad_k, grad_v, far, keep, four = outs
    far = swap(far, "ctx", 1)
    third = BLK + BLK // 2
    back = swap((keep.astype(F32) + far[2 * BLK : 2 * BLK + third]).astype(BF16), "ctx", 2)
    four = four.astype(F32) + far[2 * BLK + third :] + back[BLK:]
    four = swap(four.astype(BF16), "ctx", 4)
    grad_k, grad_v = finish_call(grad_k, grad_v, far, back, four)
    weight_grad = total_call(top, bottom, (grad_k,))
    return mixed, grad_q, grad_k, grad_v, weight_grad, level_max


def solution(mesh):
    tokens = P("ctx", "head")
    return jax.shard_map(
        per_device,
        mesh=mesh,
        in_specs=(tokens, tokens, tokens, P("head", None), tokens),
        out_specs=(tokens, tokens, tokens, tokens, P("head", "ctx"), P(None, "head")),
        check_vma=False,
    )
```
